32 devices in a mesh: section: 2 (over y), expert: 16 (over z, x, core).
Axes of the slice: x: 2, y: 2, z: 4, core: 2. Of those that a mesh axis runs over, the one named last changes fastest.
Arguments:
- front_input: bfloat16 [2, 2048, 3584], P('section', 'expert'), may hold values from -6 to 6
- queries: bfloat16 [2, 2048, 3584], P('section', 'expert'), may hold values from -400 to 400
- keys_values: bfloat16 [2, 2048, 448], P('section', 'expert'), may hold values from -6 to 6
- selected_blocks: int32 [2, 32, 2, 4], P('section', 'expert'), may hold values from 0 to 31, as said below
- front_route: int32 [2, 2048, 1], P('section', 'expert'), may hold values from 0 to 3; in each aligned block of 128 rows (0 to 127, 128 to 255, ..., all dimensions but the last counted through in order) at most 36 rows name the same one
- front_gate: float32 [2, 2048, 1], P('section', 'expert'), may hold values from 0.3 to 1
- back_middle: bfloat16 [2, 2048, 3584], P('section', 'expert'), may hold values from -6 to 6
- back_grad: bfloat16 [2, 2048, 3584], P('section', 'expert'), may hold values from -6 to 6
- back_route: int32 [2, 2048, 1], P('section', 'expert'), may hold values from 0 to 3; in each aligned block of 128 rows (0 to 127, 128 to 255, ..., all dimensions but the last counted through in order) at most 36 rows name the same one
- back_gate: float32 [2, 2048, 1], P('section', 'expert'), may hold values from 0.3 to 1
- norm_gain: float32 [2, 3584], P('section'), may hold values from 0.1 to 1.9
- gate_slice: bfloat16 [2, 16, 3584, 256], P('section', 'expert'), may hold values from -0.09375 to 0.09375
- up_slice: bfloat16 [2, 16, 3584, 256], P('section', 'expert'), may hold values from -0.09375 to 0.09375
- down_slice: bfloat16 [2, 16, 256, 3584], P('section', 'expert'), may hold values from -0.1875 to 0.1875
Outputs:
- front_output: bfloat16 [2, 2048, 3584], P('section', 'expert')
- back_output: bfloat16 [2, 2048, 3584], P('section', 'expert')
The draws below stay inside these ranges and needn't reach their ends.
Inputs may be any that keep to these rules, and one draw needn't show every extreme that they name: `selected_blocks`: each list holds 4 different block numbers, among them the query block's own; the others are at most the larger of the query block's number and 3. `front_route`: in the tokens of one device at one section, no expert is named more than 36 times. `back_route`: in the tokens of one device at one section, no expert is named more than 36 times.
All inputs are finite; a program needn't handle non-finite values.
Results may differ from the reference program's by a relative error of at most 0.0057.
Values may be sent and summed in bfloat16 or wider, within the bound.
No kernel may reach another device: no remote copies, remote signals or barrier semaphores. Data moves between devices by JAX's collectives and lax.ppermute only.
A program may use at most 192 MiB of HBM per device.

```python
import math
import jax
import jax.numpy as jnp
import numpy as np
from jax import lax

D = 3584
FF = 1024
GROUP = 4
HEADS = 32
HEAD_DIM = 112
KV_HEADS = 2
BLK = 64
SEL = 4
TOP = 1
TOK_DEV = 128
SECTIONS = 2
SLICES = 16
FF_DEV = 256
EXPERTS = 4
TOKENS = 2048
QBLOCKS = 32
CAP = 36
N_SECTION = 2
N_EXPERT = 16


def common_attention_draw(key):
    query_key = jax.random.fold_in(key, 101)
    kv_key = jax.random.fold_in(key, 202)
    kv_width = KV_HEADS * HEAD_DIM
    kv_rows = jax.random.truncated_normal(kv_key, -6.0, 6.0, (N_SECTION, TOKENS, 2 * kv_width), jnp.float32)
    query_rows = jax.random.truncated_normal(query_key, -6.0, 6.0, (N_SECTION, TOKENS, HEADS * HEAD_DIM), jnp.float32)
    return (query_rows, kv_rows)


def draw_queries(key, part):
    return common_attention_draw(key)[0].astype(jnp.bfloat16)


def draw_keys_values(key, part):
    return common_attention_draw(key)[1].astype(jnp.bfloat16)


def draw_selected_blocks(key, part):
    block_count = QBLOCKS
    raw_scores = jax.random.randint(key, (N_SECTION, block_count, KV_HEADS, block_count), 0, 2 ** 16)
    block_ids = jnp.arange(block_count, dtype=jnp.int32)[None, None, None, :]
    query_ids = jnp.arange(block_count, dtype=jnp.int32)[None, :, None, None]
    limit = jnp.maximum(query_ids, SEL - 1)
    scores = raw_scores * block_count + block_ids
    scores = jnp.where(block_ids <= limit, scores, -1 - block_ids)
    scores = jnp.where(block_ids == query_ids, 2 ** 30, scores)
    chosen = lax.top_k(scores, SEL)[1]
    return chosen.astype(jnp.int32)


def level_of(own_key, dims, split, low, top_value):
    loudness, own = 1.0, jax.random.fold_in(own_key, 6)
    for dim, shards_of in split:
        heights = jnp.exp(jax.random.uniform(jax.random.fold_in(own, dim), (shards_of,), jnp.float32, low / len(split), top_value / len(split)))
        loudness = loudness * jnp.repeat(heights, dims[dim] // shards_of).reshape([-1 if axis == dim else 1 for axis in range(len(dims))])
    return loudness


def assign_block(own_key, own, number, rows, number_of, top, most, lean):
    ranking = jax.random.permutation(own_key, number_of)
    packed, ordinary = portions_of(number_of, rows * top, most, lean, True), portions_of(number_of, rows * top, most, lean, False)
    places = jnp.arange(number_of)

    def named(sizes, rotation):
        used = int((sizes > 0).sum())
        fixed = max(1, used // 4)
        passed = fixed + (places - fixed + rotation * (used - fixed)) % max(1, number_of - fixed)
        return jnp.zeros((number_of,), jnp.int32).at[ranking[jnp.where(places < fixed, places, passed)]].set(jnp.asarray(sizes, jnp.int32))

    sizes = jnp.where(number % 4 == 0, named(packed, number // 4), named(ordinary, number - number // 4 - 1))
    mixed = jax.random.permutation(jax.random.fold_in(own, 3), number_of)
    giver, receiver = mixed[0:number_of // 2 * 2:2], mixed[1:number_of // 2 * 2:2]
    slack = jnp.minimum(sizes[giver] - 1, most - sizes[receiver]) // 2
    slack = jnp.where((giver == ranking[0]) | (receiver == ranking[0]) | (sizes[receiver] == 0), 0, jnp.maximum(slack, 0))
    passed = jax.random.randint(jax.random.fold_in(own, 4), (number_of // 2,), 0, 1 << 20) % (slack + 1)
    sizes = sizes.at[giver].add(-passed).at[receiver].add(passed)
    labels = jnp.searchsorted(jnp.cumsum(sizes), jnp.arange(rows * top), side="right").astype(jnp.int32)
    grid = labels.reshape(top, rows).T
    grid = grid[jax.random.permutation(jax.random.fold_in(own, 1), rows)]
    rotation = jax.random.randint(jax.random.fold_in(own, 2), (rows, 1), 0, top)
    return jnp.take_along_axis(grid, (jnp.arange(top)[None, :] + rotation) % top, axis=1)


def portions_of(number_of, total, bound, lean, full):
    weights = [(1 << 20) // math.isqrt(grade ** lean) + 1 for grade in range(1, number_of + 1)]
    largest = bound if full else min(bound, max(-(-total // number_of), total * weights[0] // sum(weights)))
    least = 1 if total - largest >= number_of - 1 else 0
    given, surplus = [largest] + [least] * (number_of - 1), total - largest - least * (number_of - 1)
    while surplus > 0:
        candidates = [i for i in range(1, number_of) if given[i] < largest] or [i for i in range(1, number_of) if given[i] < bound]
        mass, budget = sum([weights[i] for i in candidates]), surplus
        for i in candidates:
            addition = min(bound - given[i], max(1, budget * weights[i] // mass), surplus)
            given[i] = given[i] + addition
            surplus = surplus - addition
    return np.array(given)


def noise(stream_key, shape, width, most, split=(), kind=jnp.bfloat16):
    drawn = jax.random.normal(stream_key, shape, jnp.float32) * width
    if len(split) > 0:
        drawn = level_of(stream_key, shape, split, -0.22, 0.18) * drawn
    return jnp.clip(drawn, min=-most, max=most).astype(kind)


def setup_inputs(seed: int = 0) -> dict:
    streams_of = jax.random.split(jax.random.key(seed), 15)
    front_input = noise(streams_of[0], (SECTIONS, TOKENS, D), 1.0, 6.0, ((0, 2), (1, 16)))
    queries = draw_queries(jax.random.fold_in(streams_of[14], 71), 0)
    keys_values = draw_keys_values(jax.random.fold_in(streams_of[14], 71), 0)
    selected_blocks = draw_selected_blocks(jax.random.fold_in(streams_of[14], 71), 0)
    front_route_keys = jax.random.split(jax.random.fold_in(streams_of[4], 1), SECTIONS * TOKENS // TOK_DEV)
    front_route_turns = jax.random.permutation(jax.random.fold_in(streams_of[4], 3), SECTIONS * TOKENS // TOK_DEV)
    front_route = jax.vmap(lambda own, number: assign_block(jax.random.fold_in(streams_of[4], 2), own, number, TOK_DEV, EXPERTS, TOP, CAP, 2))(front_route_keys, front_route_turns).reshape((SECTIONS, TOKENS, TOP))
    front_gate = jnp.clip(0.3 + 0.7 * jax.random.uniform(streams_of[5], (SECTIONS, TOKENS, TOP), jnp.float32) ** level_of(streams_of[5], (SECTIONS, TOKENS, TOP), ((0, 2), (1, 16)), -0.2, 0.2), 0.3, 1.0)
    back_middle = noise(streams_of[6], (SECTIONS, TOKENS, D), 1.0, 6.0, ((0, 2), (1, 16)))
    back_grad = noise(streams_of[7], (SECTIONS, TOKENS, D), 1.0, 6.0, ((0, 2), (1, 16)))
    back_route_keys = jax.random.split(jax.random.fold_in(streams_of[8], 1), SECTIONS * TOKENS // TOK_DEV)
    back_route_turns = jax.random.permutation(jax.random.fold_in(streams_of[8], 3), SECTIONS * TOKENS // TOK_DEV)
    back_route = jax.vmap(lambda own, number: assign_block(jax.random.fold_in(streams_of[8], 2), own, number, TOK_DEV, EXPERTS, TOP, CAP, 2))(back_route_keys, back_route_turns).reshape((SECTIONS, TOKENS, TOP))
    back_gate = jnp.clip(0.3 + 0.7 * jax.random.uniform(streams_of[9], (SECTIONS, TOKENS, TOP), jnp.float32) ** level_of(streams_of[9], (SECTIONS, TOKENS, TOP), ((0, 2), (1, 16)), -0.2, 0.2), 0.3, 1.0)
    norm_gain = jnp.clip(1.0 + 0.18 * jax.random.normal(streams_of[10], (SECTIONS, D), jnp.float32), 0.1, 1.9)
    gate_slice = noise(streams_of[11], (SECTIONS, SLICES, D, FF_DEV), D ** -0.5, 0.09375, ((0, 2), (1, 16)))
    up_slice = noise(streams_of[12], (SECTIONS, SLICES, D, FF_DEV), D ** -0.5, 0.09375, ((0, 2), (1, 16)))
    down_slice = noise(streams_of[13], (SECTIONS, SLICES, FF_DEV, D), FF ** -0.5, 0.1875, ((0, 2), (1, 16)))
    return dict(front_input=front_input, queries=queries, keys_values=keys_values, selected_blocks=selected_blocks, front_route=front_route, front_gate=front_gate, back_middle=back_middle, back_grad=back_grad, back_route=back_route, back_gate=back_gate, norm_gain=norm_gain, gate_slice=gate_slice, up_slice=up_slice, down_slice=down_slice)


epsilon = 1e-06
negative_large = -1e+30

def rms_scale(rows):
    return lax.rsqrt(lax.optimization_barrier(jnp.mean(rows * rows, axis=-1, keepdims=True)) + epsilon)

def attention(query_rows, kv_rows, chosen_blocks):
    kv_width = KV_HEADS * HEAD_DIM
    block_count = query_rows.shape[0] // BLK
    key_heads = kv_rows[:, :kv_width].reshape(block_count, BLK, KV_HEADS, HEAD_DIM).transpose(2, 0, 1, 3)
    value_heads = kv_rows[:, kv_width:].reshape(block_count, BLK, KV_HEADS, HEAD_DIM).transpose(2, 0, 1, 3)
    groups = HEADS // KV_HEADS
    query_blocks = query_rows.reshape(block_count, BLK, KV_HEADS, groups, HEAD_DIM)
    head_index = jnp.arange(KV_HEADS, dtype=jnp.int32)[:, None]
    offsets = jnp.arange(BLK, dtype=jnp.int32)

    def one_block(bundle):
        query_block, chosen, block_index = bundle
        key_sel = key_heads[head_index, chosen].reshape(KV_HEADS, SEL * BLK, HEAD_DIM).astype(jnp.float32)
        value_sel = value_heads[head_index, chosen].reshape(KV_HEADS, SEL * BLK, HEAD_DIM).astype(jnp.float32)
        scores = jnp.einsum('qhgd,hkd->hgqk', query_block.astype(jnp.float32), key_sel) * HEAD_DIM ** (-0.5)
        key_pos = (chosen[:, :, None] * BLK + offsets[None, None, :]).reshape(KV_HEADS, SEL * BLK)
        query_pos = block_index * BLK + offsets
        allowed = key_pos[:, None, None, :] <= query_pos[None, None, :, None]
        scores = jnp.where(allowed, scores, negative_large)
        row_max = lax.optimization_barrier(jnp.max(scores, axis=-1, keepdims=True))
        exp_scores = jnp.exp(scores - row_max)
        row_total = lax.optimization_barrier(jnp.sum(exp_scores, axis=-1, keepdims=True))
        attention_weights = (exp_scores / row_total).astype(jnp.bfloat16)
        mixed_out = jnp.einsum('hgqk,hkd->qhgd', attention_weights.astype(jnp.float32), value_sel)
        return mixed_out.reshape(BLK, HEADS * HEAD_DIM)
    attended = lax.map(one_block, (query_blocks, chosen_blocks, jnp.arange(block_count, dtype=jnp.int32)))
    return attended.reshape(block_count * BLK, HEADS * HEAD_DIM)

def slot_table(route):
    per_device = route.reshape(N_EXPERT, TOK_DEV * TOP)
    onehot = (per_device[:, :, None] == jnp.arange(EXPERTS, dtype=jnp.int32)[None, None, :]).astype(jnp.int32)
    before = jnp.cumsum(onehot, axis=1) - onehot
    slot_of = lax.optimization_barrier(jnp.sum(before * onehot, axis=2)).astype(jnp.int32)
    source_of = jnp.broadcast_to(jnp.arange(N_EXPERT, dtype=jnp.int32)[:, None], per_device.shape)
    return (per_device, source_of, slot_of)

def dispatch(rows, expert_of, source_of, slot_of):
    buffer = jnp.zeros((EXPERTS, N_EXPERT, CAP, D), rows.dtype)
    return buffer.at[expert_of, source_of, slot_of].set(rows)

def expert_forward(bundle):
    rows, w_gate, w_up, w_down = bundle
    rows = rows.reshape(N_EXPERT * CAP, D)
    total_val = jnp.zeros((N_EXPERT * CAP, D), jnp.float32)
    for slice_index in range(GROUP):
        gate_val = jnp.dot(rows, w_gate[slice_index], preferred_element_type=jnp.float32)
        up_val = jnp.dot(rows, w_up[slice_index], preferred_element_type=jnp.float32)
        hidden = (jax.nn.silu(gate_val) * up_val).astype(jnp.bfloat16)
        partial_value = jnp.dot(hidden, w_down[slice_index], preferred_element_type=jnp.float32).astype(jnp.bfloat16)
        total_val = total_val + partial_value.astype(jnp.float32)
    return total_val.reshape(N_EXPERT, CAP, D)

def expert_backward(bundle):
    rows, grads, w_gate, w_up, w_down = bundle
    rows = rows.reshape(N_EXPERT * CAP, D)
    grads = grads.reshape(N_EXPERT * CAP, D)
    total_val = jnp.zeros((N_EXPERT * CAP, D), jnp.float32)
    for slice_index in range(GROUP):
        gate_val = jnp.dot(rows, w_gate[slice_index], preferred_element_type=jnp.float32)
        up_val = jnp.dot(rows, w_up[slice_index], preferred_element_type=jnp.float32)
        sigmoid_val = jax.nn.sigmoid(gate_val)
        act_val = gate_val * sigmoid_val
        slope_val = sigmoid_val * (1.0 + gate_val * (1.0 - sigmoid_val))
        down_back = jnp.dot(grads, w_down[slice_index].T, preferred_element_type=jnp.float32)
        gate_grad = (down_back * up_val * slope_val).astype(jnp.bfloat16)
        up_grad = (down_back * act_val).astype(jnp.bfloat16)
        slice_grad = jnp.dot(gate_grad, w_gate[slice_index].T, preferred_element_type=jnp.float32)
        slice_grad = slice_grad + jnp.dot(up_grad, w_up[slice_index].T, preferred_element_type=jnp.float32)
        total_val = total_val + slice_grad.astype(jnp.bfloat16).astype(jnp.float32)
    return total_val.reshape(N_EXPERT, CAP, D)

def reference(front_input, queries, keys_values, selected_blocks, front_route, front_gate, back_middle, back_grad, back_route, back_gate, norm_gain, gate_slice, up_slice, down_slice):
    front_list = []
    back_list = []
    for section_index in range(N_SECTION):
        gain_row = norm_gain[section_index]
        w_gate = gate_slice[section_index].reshape(EXPERTS, GROUP, D, FF_DEV)
        w_up = up_slice[section_index].reshape(EXPERTS, GROUP, D, FF_DEV)
        w_down = down_slice[section_index].reshape(EXPERTS, GROUP, FF_DEV, D)
        attention_out = attention(queries[section_index], keys_values[section_index], selected_blocks[section_index])
        middle = (front_input[section_index].astype(jnp.float32) + attention_out).astype(jnp.bfloat16)
        middle = lax.optimization_barrier(middle).astype(jnp.float32)
        normed = (middle * rms_scale(middle) * gain_row).astype(jnp.bfloat16)
        expert_of, source_of, slot_of = slot_table(front_route[section_index])
        rows = jnp.repeat(normed.reshape(N_EXPERT, TOK_DEV, D), TOP, axis=1)
        buffer = dispatch(rows, expert_of, source_of, slot_of)
        expert_out = lax.map(expert_forward, (buffer, w_gate, w_up, w_down))
        picked = expert_out[expert_of, source_of, slot_of]
        weighted = picked * front_gate[section_index].reshape(N_EXPERT, TOK_DEV * TOP)[:, :, None]
        contrib = lax.optimization_barrier(jnp.sum(weighted.reshape(TOKENS, TOP, D), axis=1))
        front_list.append((middle + contrib).astype(jnp.bfloat16))
        back_mid = back_middle[section_index].astype(jnp.float32)
        back_scale = rms_scale(back_mid)
        back_normed = (back_mid * back_scale * gain_row).astype(jnp.bfloat16)
        expert_of, source_of, slot_of = slot_table(back_route[section_index])
        grad_rows = jnp.repeat(back_grad[section_index].astype(jnp.float32), TOP, axis=0)
        scaled = (back_gate[section_index].reshape(TOKENS * TOP, 1) * grad_rows).astype(jnp.bfloat16)
        rows = jnp.repeat(back_normed.reshape(N_EXPERT, TOK_DEV, D), TOP, axis=1)
        buffer_rows = dispatch(rows, expert_of, source_of, slot_of)
        buffer_grads = dispatch(scaled.reshape(N_EXPERT, TOK_DEV * TOP, D), expert_of, source_of, slot_of)
        expert_grad = lax.map(expert_backward, (buffer_rows, buffer_grads, w_gate, w_up, w_down))
        picked = expert_grad[expert_of, source_of, slot_of]
        normed_grad = lax.optimization_barrier(jnp.sum(picked.reshape(TOKENS, TOP, D), axis=1))
        amount = gain_row * normed_grad
        cube = back_scale * back_scale * back_scale
        back_result = back_grad[section_index].astype(jnp.float32) + back_scale * amount - back_mid * cube * lax.optimization_barrier(jnp.mean(back_mid * amount, axis=-1, keepdims=True))
        back_list.append(back_result.astype(jnp.bfloat16))
    front_output = jnp.roll(jnp.stack(front_list), 1, axis=0)
    back_output = jnp.roll(jnp.stack(back_list), -1, axis=0)
    return (front_output, back_output)
```

```python
import jax
import jax.numpy as jnp
from jax import lax
from jax.sharding import PartitionSpec as P

GROUP = 4
HEADS = 32
HEAD_DIM = 112
KV_HEADS = 2
BLK = 64


epsilon = 1e-06
negative_large = -1e30


def passed_along(array, axis, by):
    length = lax.axis_size(axis)
    return lax.ppermute(array, axis, [(i, (i + by) % length) for i in range(length)])


def rms_scale(rows):
    return lax.rsqrt(jnp.mean(rows * rows, axis=-1, keepdims=True) + epsilon)


def swapped(array, bit):
    return lax.ppermute(array, "expert", [(i, i ^ bit) for i in range(lax.axis_size("expert"))])


def across_experts(array):
    experts = lax.axis_size("expert") // GROUP
    groups = [[e * GROUP + j for e in range(experts)] for j in range(GROUP)]
    return lax.all_to_all(
        array, "expert", split_axis=0, concat_axis=0, axis_index_groups=groups, tiled=True
    )


def gather_blocks(kv_rows):
    length = lax.axis_size("expert")
    experts = length // GROUP
    column = [kv_rows]
    for back in range(1, experts):
        pairs = [(i, i + back * GROUP) for i in range(length - back * GROUP)]
        column.append(lax.ppermute(kv_rows, "expert", pairs))
    column = jnp.concatenate(column, axis=0)
    chip = jnp.concatenate([column, swapped(column, 2)], axis=0)
    return jnp.concatenate([chip, swapped(chip, 1)], axis=0)


def attend_local(query_rows, kv_rows, chosen_blocks):
    gathered = gather_blocks(kv_rows)
    experts = lax.axis_size("expert") // GROUP
    per_device = kv_rows.shape[0] // BLK
    me = lax.axis_index("expert")
    blocks_view = gathered.reshape(-1, BLK, kv_rows.shape[1])
    groups = HEADS // KV_HEADS
    query_blocks = query_rows.reshape(-1, BLK, KV_HEADS, groups, HEAD_DIM)
    local_blocks = query_blocks.shape[0]
    first_block = me * local_blocks
    offsets = jnp.arange(BLK, dtype=jnp.int32)
    owner = chosen_blocks // per_device
    place = (owner % GROUP) ^ (me % GROUP)
    place = (place % 2) * 2 + place // 2
    index = (place * experts + me // GROUP - owner // GROUP) * per_device
    index = jnp.clip(index + chosen_blocks % per_device, 0, blocks_view.shape[0] - 1)

    def one_block(query_block, chosen, place_of, block_index):
        picked = blocks_view[place_of].reshape(KV_HEADS, -1, 2, KV_HEADS, HEAD_DIM)
        key_sel = jnp.stack([picked[h, :, 0, h] for h in range(KV_HEADS)])
        value_sel = jnp.stack([picked[h, :, 1, h] for h in range(KV_HEADS)])
        scores = jnp.einsum(
            "qhgd,hkd->hgqk", query_block, key_sel, preferred_element_type=jnp.float32
        ) * HEAD_DIM ** (-0.5)
        key_pos = (chosen[:, :, None] * BLK + offsets[None, None, :]).reshape(KV_HEADS, -1)
        query_pos = block_index * BLK + offsets
        allowed = key_pos[:, None, None, :] <= query_pos[None, None, :, None]
        scores = jnp.where(allowed, scores, negative_large)
        row_max = jnp.max(scores, axis=-1, keepdims=True)
        exp_scores = jnp.exp(scores - row_max)
        row_total = jnp.sum(exp_scores, axis=-1, keepdims=True)
        attention_weights = (exp_scores / row_total).astype(jnp.bfloat16)
        mixed_out = jnp.einsum(
            "hgqk,hkd->qhgd", attention_weights, value_sel, preferred_element_type=jnp.float32
        )
        return mixed_out.reshape(BLK, HEADS * HEAD_DIM)

    attended = jax.vmap(one_block)(
        query_blocks,
        chosen_blocks,
        index,
        first_block + jnp.arange(local_blocks, dtype=jnp.int32),
    )
    return attended.reshape(query_rows.shape[0], HEADS * HEAD_DIM)


def place_rows(route, experts, capacity):
    flat_route = route.reshape(-1)
    onehot = (flat_route[:, None] == jnp.arange(experts, dtype=jnp.int32)[None, :]).astype(
        jnp.int32
    )
    before = jnp.cumsum(onehot, axis=0) - onehot
    first = flat_route * (2 * capacity) + jnp.sum(before * onehot, axis=1)
    return jnp.concatenate([first, first + capacity])


def selection(places, count):
    return (jnp.arange(count, dtype=jnp.int32)[:, None] == places[None, :]).astype(jnp.bfloat16)


def moved(matrix, rows):
    return jnp.dot(matrix, rows, preferred_element_type=jnp.float32)


def halves_down(rows):
    return jnp.concatenate(jnp.split(rows, 2, axis=1), axis=0)


def halves_across(rows):
    return jnp.concatenate(jnp.split(rows, 2, axis=0), axis=1)


def gather_group(rows):
    other_chip = swapped(rows, 2)
    return [rows, other_chip, swapped(rows, 1), swapped(other_chip, 1)]


def sum_group(pieces):
    own = pieces[0].astype(jnp.float32) + swapped(pieces[2], 1).astype(jnp.float32)
    other = pieces[1].astype(jnp.float32) + swapped(pieces[3], 1).astype(jnp.float32)
    return own + swapped(other.astype(jnp.bfloat16), 2).astype(jnp.float32)


def slice_forward(rows, w_gate, w_up, w_down):
    gate_val = jnp.dot(rows, w_gate, preferred_element_type=jnp.float32)
    up_val = jnp.dot(rows, w_up, preferred_element_type=jnp.float32)
    hidden = (jax.nn.silu(gate_val) * up_val).astype(jnp.bfloat16)
    return jnp.dot(hidden, w_down, preferred_element_type=jnp.float32).astype(jnp.bfloat16)


def slice_backward(rows, grads, w_gate, w_up, w_down):
    contract_last = (((1,), (1,)), ((), ()))
    gate_val = jnp.dot(rows, w_gate, preferred_element_type=jnp.float32)
    up_val = jnp.dot(rows, w_up, preferred_element_type=jnp.float32)
    sigmoid_val = jax.nn.sigmoid(gate_val)
    act_val = gate_val * sigmoid_val
    slope_val = sigmoid_val * (1.0 + gate_val * (1.0 - sigmoid_val))
    down_back = lax.dot_general(grads, w_down, contract_last, preferred_element_type=jnp.float32)
    gate_grad = (down_back * up_val * slope_val).astype(jnp.bfloat16)
    up_grad = (down_back * act_val).astype(jnp.bfloat16)
    total_val = lax.dot_general(
        gate_grad, w_gate, contract_last, preferred_element_type=jnp.float32
    ) + lax.dot_general(up_grad, w_up, contract_last, preferred_element_type=jnp.float32)
    return total_val.astype(jnp.bfloat16)


def shards(
    front_input,
    queries,
    keys_values,
    selected_blocks,
    front_route,
    front_gate,
    back_middle,
    back_grad,
    back_route,
    back_gate,
    norm_gain,
    gate_slice,
    up_slice,
    down_slice,
):
    tokens_here = front_input.shape[1]
    experts = lax.axis_size("expert") // GROUP
    average = tokens_here // experts
    capacity = average + max(1, average // 8)
    slots = experts * capacity
    w_gate = gate_slice[0, 0]
    w_up = up_slice[0, 0]
    w_down = down_slice[0, 0]
    gain_row = norm_gain[0]

    order = jnp.arange(2 * slots, dtype=jnp.int32).reshape(2, experts, capacity)
    order = order.transpose(1, 0, 2).reshape(-1)
    apart = selection(order, 2 * slots)
    together = apart.T

    back_mid = back_middle[0].astype(jnp.float32)
    back_scale = rms_scale(back_mid)
    back_normed = (back_mid * back_scale * gain_row).astype(jnp.bfloat16)
    scaled = (back_gate[0] * back_grad[0].astype(jnp.float32)).astype(jnp.bfloat16)
    back_pick = selection(place_rows(back_route[0], experts, capacity), 2 * slots)
    back_send = moved(back_pick, jnp.concatenate([back_normed, scaled], axis=0))
    received = across_experts(back_send.astype(jnp.bfloat16))
    received = moved(apart, received).astype(jnp.bfloat16)
    pieces = [
        slice_backward(piece[:slots], piece[slots:], w_gate, w_up, w_down)
        for piece in gather_group(received)
    ]
    back_total = sum_group(pieces).astype(jnp.bfloat16)
    back_return = across_experts(moved(together, halves_down(back_total)).astype(jnp.bfloat16))

    attention_out = attend_local(queries[0], keys_values[0], selected_blocks[0])
    middle = (front_input[0].astype(jnp.float32) + attention_out).astype(jnp.bfloat16)
    middle = lax.optimization_barrier(middle).astype(jnp.float32)
    normed = (middle * rms_scale(middle) * gain_row).astype(jnp.bfloat16)
    front_pick = selection(place_rows(front_route[0], experts, capacity), 2 * slots)
    front_send = moved(front_pick, halves_down(normed)).astype(jnp.bfloat16)
    received = across_experts(front_send)
    received = halves_across(moved(apart, received).astype(jnp.bfloat16))
    pieces = [slice_forward(piece, w_gate, w_up, w_down) for piece in gather_group(received)]
    front_total = sum_group(pieces).astype(jnp.bfloat16)
    front_return = across_experts(moved(together, halves_down(front_total)).astype(jnp.bfloat16))

    normed_grad = halves_across(moved(back_pick.T, back_return))
    amount = gain_row * normed_grad
    cube = back_scale * back_scale * back_scale
    back_result = (
        back_grad[0].astype(jnp.float32)
        + back_scale * amount
        - back_mid * cube * jnp.mean(back_mid * amount, axis=-1, keepdims=True)
    )
    back_result = back_result.astype(jnp.bfloat16)
    back_output = passed_along(back_result, "section", -1)

    contrib = front_gate[0] * halves_across(moved(front_pick.T, front_return))
    front_result = (middle + contrib).astype(jnp.bfloat16)
    front_output = passed_along(front_result, "section", 1)
    return (front_output[None], back_output[None])


def solution(mesh):
    placed = (
        P("section", "expert", None),
        P("section", "expert", None),
        P("section", "expert", None),
        P("section", "expert", None, None),
        P("section", "expert", None),
        P("section", "expert", None),
        P("section", "expert", None),
        P("section", "expert", None),
        P("section", "expert", None),
        P("section", "expert", None),
        P("section", None),
        P("section", "expert", None, None),
        P("section", "expert", None, None),
        P("section", "expert", None, None),
    )
    return jax.shard_map(
        shards,
        mesh=mesh,
        in_specs=placed,
        out_specs=(P("section", "expert", None), P("section", "expert", None)),
        check_vma=False,
    )
```

```python
import functools

import jax
import jax.numpy as jnp
from jax import lax
from jax.experimental import pallas as pl
from jax.experimental.pallas import tpu as pltpu
from jax.sharding import PartitionSpec as P

GROUP = 4
HEADS = 32
HEAD_DIM = 112
KV_HEADS = 2
BLK = 64
SEL = 4
PARTS = 4
LANES = 128
VMEM_BYTES = 56 * 1024 * 1024

epsilon = 1e-06
negative_large = -1e30
bf16 = jnp.bfloat16
f32 = jnp.float32


def passed_along(array, axis, by):
    length = lax.axis_size(axis)
    return lax.ppermute(array, axis, [(i, (i + by) % length) for i in range(length)])


def swapped(array, bit):
    return lax.ppermute(array, "expert", [(i, i ^ bit) for i in range(lax.axis_size("expert"))])


def turned(array, by):
    length = lax.axis_size("expert")
    return lax.ppermute(
        array, "expert", [(i, (i + by * GROUP) % length) for i in range(length)]
    )


def call(body, outs, args, scratch=(), flops=0, smem=0):
    specs = [
        pl.BlockSpec(memory_space=pltpu.SMEM if i < smem else pltpu.VMEM)
        for i in range(len(args))
    ]
    many = isinstance(outs, list)
    shapes = outs if many else [outs]
    moved_bytes = sum(a.size * a.dtype.itemsize for a in list(args) + shapes)
    result = pl.pallas_call(
        body,
        out_shape=shapes,
        in_specs=specs,
        out_specs=[pl.BlockSpec(memory_space=pltpu.VMEM) for _ in shapes],
        scratch_shapes=list(scratch),
        compiler_params=pltpu.CompilerParams(vmem_limit_bytes=VMEM_BYTES),
        cost_estimate=pl.CostEstimate(
            flops=int(flops), bytes_accessed=int(moved_bytes), transcendentals=0
        ),
    )(*args)
    return result if many else result[0]


def dot(a, b):
    return jnp.dot(a, b, preferred_element_type=f32)


def dot_last(a, b):
    return lax.dot_general(a, b, (((1,), (1,)), ((), ())), preferred_element_type=f32)


def rms_scale(rows):
    return lax.rsqrt(jnp.mean(rows * rows, axis=-1, keepdims=True) + epsilon)


def iota(shape, dim):
    return lax.broadcasted_iota(jnp.int32, shape, dim)


def stacked(rows):
    width = rows.shape[1] // PARTS
    return jnp.concatenate([rows[:, p * width : (p + 1) * width] for p in range(PARTS)], axis=0)


def place_across(route_row, experts, capacity):
    tokens = route_row.shape[1]
    names = iota((max(8, experts), tokens), 0)
    onehot = jnp.where(names == route_row, 1.0, 0.0)
    earlier = jnp.where(iota((tokens, tokens), 0) < iota((tokens, tokens), 1), 1.0, 0.0)
    before = dot(onehot.astype(bf16), earlier.astype(bf16))
    place = onehot * (before + (names * (PARTS * capacity)).astype(f32))
    return jnp.sum(place, axis=0, keepdims=True).astype(jnp.int32)


def place_down(route_column, experts, capacity):
    tokens = route_column.shape[0]
    names = iota((tokens, LANES), 1)
    onehot = jnp.where(names == route_column, 1.0, 0.0)
    earlier = jnp.where(iota((tokens, tokens), 1) < iota((tokens, tokens), 0), 1.0, 0.0)
    before = dot(earlier.astype(bf16), onehot.astype(bf16))
    place = onehot * (before + (names * (PARTS * capacity)).astype(f32))
    return jnp.sum(place, axis=1, keepdims=True).astype(jnp.int32)


def pack_into(rows, place, out_refs, capacity):
    tokens = rows.shape[0]
    height = PARTS * capacity
    total = height * len(out_refs)
    places = jnp.concatenate([place + p * capacity for p in range(PARTS)], axis=1)
    pick = jnp.where(iota((total, PARTS * tokens), 0) == places, 1.0, 0.0).astype(bf16)
    packed = dot(pick, stacked(rows)).astype(bf16)
    for e, ref in enumerate(out_refs):
        ref[...] = packed[e * height : (e + 1) * height]


def back_pack_body(experts, capacity, route_ref, gate_ref, gain_ref, middle_ref, grad_ref, *outs):
    place = place_across(route_ref[...], experts, capacity)
    middle = middle_ref[...].astype(f32)
    normed = (middle * rms_scale(middle) * gain_ref[...]).astype(bf16)
    pack_into(normed, place, outs[:experts], capacity)
    scaled = (gate_ref[...] * grad_ref[...].astype(f32)).astype(bf16)
    pack_into(scaled, place, outs[experts:], capacity)


def join_body(capacity, *refs):
    chunks, out = refs[:-1], refs[-1]
    sources = len(chunks)
    height = PARTS * capacity
    rows = jnp.concatenate([ref[...] for ref in chunks], axis=0)
    slots = sources * capacity
    width = rows.shape[1]
    index = iota((slots, 1), 0)
    source = index * 0
    for s in range(1, sources):
        source = source + jnp.where(index >= s * capacity, 1, 0)
    first = index + source * (height - capacity)
    columns = iota((slots, rows.shape[0]), 1)
    for p in range(PARTS):
        pick = jnp.where(columns == first + p * capacity, 1.0, 0.0).astype(bf16)
        out[:, p * width : (p + 1) * width] = dot(pick, rows).astype(bf16)


def split_body(capacity, own_ref, core_ref, chip_ref, *outs):
    total = own_ref[...].astype(f32) + core_ref[...].astype(f32) + chip_ref[...].astype(f32)
    rows = stacked(total.astype(bf16))
    height = PARTS * capacity
    slots = own_ref.shape[0]
    count = height * len(outs)
    index = iota((count, 1), 0)
    group = index * 0
    source = index * 0
    for g in range(1, count // capacity):
        group = group + jnp.where(index >= g * capacity, 1, 0)
    for s in range(1, len(outs)):
        source = source + jnp.where(index >= s * height, 1, 0)
    part = group - source * PARTS
    place = part * slots + source * capacity + index - group * capacity
    pick = jnp.where(iota((count, PARTS * slots), 1) == place, 1.0, 0.0).astype(bf16)
    packed = dot(pick, rows).astype(bf16)
    for s, ref in enumerate(outs):
        ref[...] = packed[s * height : (s + 1) * height]


def unpacked(route_column, chunk_refs, experts, capacity):
    tokens = route_column.shape[0]
    place = place_down(route_column, experts, capacity)
    rows = jnp.concatenate([ref[...] for ref in chunk_refs], axis=0)
    columns = iota((tokens, rows.shape[0]), 1)
    parts = []
    for p in range(PARTS):
        pick = jnp.where(columns == place + p * capacity, 1.0, 0.0).astype(bf16)
        parts.append(dot(pick, rows))
    return jnp.concatenate(parts, axis=1)


def front_finish_body(experts, capacity, route_ref, gate_ref, middle_ref, *refs):
    chunks, out = refs[:-1], refs[-1]
    contrib = gate_ref[...] * unpacked(route_ref[...], chunks, experts, capacity)
    out[...] = (middle_ref[...].astype(f32) + contrib).astype(bf16)


def back_finish_body(experts, capacity, route_ref, gain_ref, middle_ref, grad_ref, *refs):
    chunks, out = refs[:-1], refs[-1]
    amount = gain_ref[...] * unpacked(route_ref[...], chunks, experts, capacity)
    middle = middle_ref[...].astype(f32)
    scale = rms_scale(middle)
    cube = scale * scale * scale
    mean = jnp.mean(middle * amount, axis=-1, keepdims=True)
    out[...] = (grad_ref[...].astype(f32) + scale * amount - middle * cube * mean).astype(bf16)


def forward_body(first_ref, second_ref, gate_ref, up_ref, down_ref, first_out, second_out):
    half = first_ref.shape[0]
    rows = jnp.concatenate([first_ref[...], second_ref[...]], axis=0)
    gate_val = dot(rows, gate_ref[...])
    up_val = dot(rows, up_ref[...])
    hidden = (gate_val / (1.0 + jnp.exp(-gate_val)) * up_val).astype(bf16)
    width = down_ref.shape[1]
    step = 4 * LANES
    for n in range(0, width, step):
        value = dot(hidden, down_ref[:, n : n + step]).astype(bf16)
        first_out[:, n : n + step] = value[:half]
        second_out[:, n : n + step] = value[half:]


def backward_body(
    first_ref, second_ref, first_grad, second_grad, gate_ref, up_ref, down_ref, first_out, second_out
):
    half = first_ref.shape[0]
    rows = jnp.concatenate([first_ref[...], second_ref[...]], axis=0)
    gate_val = dot(rows, gate_ref[...])
    up_val = dot(rows, up_ref[...])
    grads = jnp.concatenate([first_grad[...], second_grad[...]], axis=0)
    down_back = dot_last(grads, down_ref[...])
    sigmoid_val = 1.0 / (1.0 + jnp.exp(-gate_val))
    slope_val = sigmoid_val * (1.0 + gate_val * (1.0 - sigmoid_val))
    gate_grad = (down_back * up_val * slope_val).astype(bf16)
    up_grad = (down_back * gate_val * sigmoid_val).astype(bf16)
    width = down_ref.shape[1]
    step = 4 * LANES
    for n in range(0, width, step):
        value = dot_last(gate_grad, gate_ref[n : n + step])
        value = (value + dot_last(up_grad, up_ref[n : n + step])).astype(bf16)
        first_out[:, n : n + step] = value[:half]
        second_out[:, n : n + step] = value[half:]


def attend_body(
    experts,
    capacity,
    chosen_ref,
    index_ref,
    base_ref,
    route_ref,
    gain_ref,
    input_ref,
    query_ref,
    kv0,
    kv1,
    kv2,
    kv3,
    middle_ref,
    *refs,
):
    outs, (kv_all, kv_now, stack, attended) = refs[:experts], refs[experts:]
    tokens, width = query_ref.shape
    rows_each = kv0.shape[0]
    for place, ref in enumerate((kv0, kv1, kv2, kv3)):
        kv_all[place * rows_each : (place + 1) * rows_each, : ref.shape[1]] = ref[...]
    attended[...] = jnp.zeros_like(attended)
    heads_each = HEADS // KV_HEADS
    period = 8
    window = 2 * LANES
    keys = SEL * BLK
    lane = iota((keys, LANES), 1)
    batch = 4
    scale = HEAD_DIM**-0.5

    def one_block(block, _):
        top = pl.multiple_of(block * BLK, BLK)
        position = (base_ref[0] + block) * BLK + (iota((batch * BLK, keys), 0) & (BLK - 1))
        for head in range(KV_HEADS):
            key_pos = iota((1, keys), 1)
            shift = key_pos * 0
            for s in range(SEL):
                at = (block * KV_HEADS + head) * SEL + s
                start = pl.multiple_of(index_ref[at] * BLK, BLK)
                kv_now[s * BLK : (s + 1) * BLK, :] = kv_all[pl.ds(start, BLK), :].astype(f32)
                inside = (key_pos >= s * BLK) & (key_pos < (s + 1) * BLK)
                shift = jnp.where(inside, (chosen_ref[at] - s) * BLK, shift)
            allowed = key_pos + shift <= position
            sides = []
            for side in range(2):
                lead = (side * KV_HEADS + head) * HEAD_DIM
                tile = min(lead // LANES, 2)
                piece = kv_now[:, tile * LANES : tile * LANES + window]
                offset = lead - tile * LANES
                if offset:
                    piece = pltpu.roll(piece, window - offset, 1)
                sides.append(jnp.where(lane < HEAD_DIM, piece[:, :LANES], 0.0).astype(bf16))
            key_rows, value_rows = sides
            spots = []
            for j in range(heads_each):
                c = j % period
                tile = min(c * HEAD_DIM // LANES, period - 3)
                offset = c * HEAD_DIM - tile * LANES
                tile = tile + (j // period) * (period - 1) + head * heads_each * HEAD_DIM // LANES
                spots.append((tile * LANES, offset))
            for j, (lead, offset) in enumerate(spots):
                piece = query_ref[pl.ds(top, BLK), lead : lead + window].astype(f32)
                if offset:
                    piece = pltpu.roll(piece, window - offset, 1)
                stack[j * BLK : (j + 1) * BLK, :] = piece[:, :LANES].astype(bf16)
            for b in range(0, heads_each, batch):
                scores = dot_last(stack[b * BLK : (b + batch) * BLK, :], key_rows) * scale
                scores = jnp.where(allowed, scores, negative_large)
                exp_scores = jnp.exp(scores - jnp.max(scores, axis=-1, keepdims=True))
                total = jnp.sum(exp_scores, axis=-1, keepdims=True)
                mixed = dot((exp_scores / total).astype(bf16), value_rows)
                for i in range(batch):
                    lead, offset = spots[b + i]
                    piece = mixed[i * BLK : (i + 1) * BLK]
                    piece = jnp.concatenate([piece, jnp.zeros_like(piece)], axis=1)
                    if offset:
                        piece = pltpu.roll(piece, offset, 1)
                    spot = (pl.ds(top, BLK), slice(lead, lead + window))
                    attended[spot] = attended[spot] + piece
        return 0

    lax.fori_loop(0, tokens // BLK, one_block, 0)
    middle = (input_ref[...].astype(f32) + attended[...]).astype(bf16)
    middle_ref[...] = middle
    middle = middle.astype(f32)
    normed = (middle * rms_scale(middle) * gain_ref[...]).astype(bf16)
    pack_into(normed, place_across(route_ref[...], experts, capacity), outs, capacity)


def after(arrays, others):
    count = len(arrays)
    return list(lax.optimization_barrier(tuple(arrays) + tuple(others))[:count])


def shape_of(rows, columns, kind=bf16):
    return jax.ShapeDtypeStruct((rows, columns), kind)


def shards(
    front_input,
    queries,
    keys_values,
    selected_blocks,
    front_route,
    front_gate,
    back_middle,
    back_grad,
    back_route,
    back_gate,
    norm_gain,
    gate_slice,
    up_slice,
    down_slice,
):
    tokens, width = front_input.shape[1:]
    length = lax.axis_size("expert")
    experts = length // GROUP
    average = tokens // experts
    capacity = average + max(1, average // 8)
    slots = experts * capacity
    hidden_width = gate_slice.shape[3]
    weights = (gate_slice[0, 0], up_slice[0, 0], down_slice[0, 0])
    me = lax.axis_index("expert")
    group = me // GROUP
    chunk = shape_of(PARTS * capacity, width // PARTS)
    piece = shape_of(slots, width)
    whole = shape_of(tokens, width)

    column = [keys_values[0]]
    for back in range(1, experts):
        pairs = [(i, i + back * GROUP) for i in range(length - back * GROUP)]
        column.append(lax.ppermute(keys_values[0], "expert", pairs))
    column = jnp.concatenate(column, axis=0)
    other_chip = swapped(column, 2)
    kv = [column, other_chip, swapped(column, 1), swapped(other_chip, 1)]

    front_from = lax.rem(front_route[0] - group + experts, experts)
    back_from = lax.rem(back_route[0] - group + experts, experts)
    front_row, back_row = front_from.reshape(1, tokens), back_from.reshape(1, tokens)

    pack_flops = 4 * slots * PARTS * tokens * width
    packed = call(
        functools.partial(back_pack_body, experts, capacity),
        [chunk] * (2 * experts),
        (back_row, back_gate[0], norm_gain, back_middle[0], back_grad[0]),
        flops=2 * pack_flops,
    )
    packed = after(packed, [column])

    def joined(chunks):
        chunks = [chunks[0]] + [turned(chunks[k], k) for k in range(1, experts)]
        return call(functools.partial(join_body, capacity), piece, chunks, flops=pack_flops)

    def pieces_of(rows):
        other = swapped(rows, 2)
        return [rows, swapped(rows, 1), other, swapped(other, 1)]

    def returned(near, far):
        chip = far[0].astype(f32) + swapped(far[1], 1).astype(f32)
        parts = (near[0], swapped(near[1], 1), swapped(chip.astype(bf16), 2))
        chunks = call(
            functools.partial(split_body, capacity), [chunk] * experts, parts, flops=pack_flops
        )
        return [chunks[0]] + [turned(chunks[k], -k) for k in range(1, experts)]

    back_rows = joined(packed[:experts])
    grad_chunks = after(packed[experts:], [back_rows])
    back_pieces = pieces_of(back_rows)
    back_grads = joined(grad_chunks)
    grad_pieces = pieces_of(back_grads)

    per_device = tokens // BLK
    chosen = selected_blocks[0].reshape(-1)
    owner = chosen // per_device
    place = (owner % GROUP) ^ (me % GROUP)
    place = (place % 2) * 2 + place // 2
    index = (place * experts + group - owner // GROUP) * per_device + chosen % per_device
    index = jnp.clip(index, 0, length * per_device - 1)
    base = (me * per_device).astype(jnp.int32).reshape(1)
    result = call(
        functools.partial(attend_body, experts, capacity),
        [whole] + [chunk] * experts,
        (chosen, index, base, front_row, norm_gain, front_input[0], queries[0], *kv),
        scratch=[
            pltpu.VMEM((length * tokens, 4 * LANES), bf16),
            pltpu.VMEM((SEL * BLK, 4 * LANES), f32),
            pltpu.VMEM((HEADS // KV_HEADS * BLK, LANES), bf16),
            pltpu.VMEM((tokens, width), f32),
        ],
        flops=pack_flops + 4 * tokens * HEADS * SEL * BLK * LANES,
        smem=3,
    )
    middle, front_chunks = result[0], result[1:]
    front_rows = joined(front_chunks)
    front_pieces = pieces_of(front_rows)

    work = 2 * 2 * slots * width * hidden_width

    def backward(first, second):
        return call(
            backward_body,
            [piece, piece],
            (*back_pieces[first:second], *grad_pieces[first:second], *weights),
            flops=5 * work,
        )

    def forward(first, second):
        return call(
            forward_body,
            [piece, piece],
            (*front_pieces[first:second], *weights),
            flops=3 * work,
        )

    back_far = backward(2, 4)
    back_near = backward(0, 2)
    back_return = returned(back_near, back_far)
    back_result = call(
        functools.partial(back_finish_body, experts, capacity),
        whole,
        (back_from, norm_gain, back_middle[0], back_grad[0], *back_return),
        flops=pack_flops,
    )
    back_output = passed_along(back_result, "section", -1)

    front_far = forward(2, 4)
    front_near = forward(0, 2)
    front_return = returned(front_near, front_far)
    front_result = call(
        functools.partial(front_finish_body, experts, capacity),
        whole,
        (front_from, front_gate[0], middle, *front_return),
        flops=pack_flops,
    )
    front_output = passed_along(front_result, "section", 1)
    return (front_output[None], back_output[None])


def solution(mesh):
    placed = (
        P("section", "expert", None),
        P("section", "expert", None),
        P("section", "expert", None),
        P("section", "expert", None, None),
        P("section", "expert", None),
        P("section", "expert", None),
        P("section", "expert", None),
        P("section", "expert", None),
        P("section", "expert", None),
        P("section", "expert", None),
        P("section", None),
        P("section", "expert", None, None),
        P("section", "expert", None, None),
        P("section", "expert", None, None),
    )
    return jax.shard_map(
        shards,
        mesh=mesh,
        in_specs=placed,
        out_specs=(P("section", "expert", None), P("section", "expert", None)),
        check_vma=False,
    )
```

```python
import functools

import jax
import jax.numpy as jnp
from jax import lax
from jax.experimental import pallas as pl
from jax.experimental.pallas import tpu as pltpu
from jax.sharding import PartitionSpec as P

GROUP = 4
HEADS = 32
HEAD_DIM = 112
KV_HEADS = 2
BLK = 64
SEL = 4
PARTS = 4
LANES = 128
VMEM_BYTES = 28 * 1024 * 1024

epsilon = 1e-06
negative_large = -1e30
bf16 = jnp.bfloat16
f32 = jnp.float32


def passed_along(array, axis, by):
    length = lax.axis_size(axis)
    return lax.ppermute(array, axis, [(i, (i + by) % length) for i in range(length)])


def swapped(array, bit):
    return lax.ppermute(array, "expert", [(i, i ^ bit) for i in range(lax.axis_size("expert"))])


def turned(array, by):
    length = lax.axis_size("expert")
    return lax.ppermute(
        array, "expert", [(i, (i + by * GROUP) % length) for i in range(length)]
    )


def call(body, outs, args, scratch=(), flops=0, smem=0, vmem=VMEM_BYTES):
    specs = [
        pl.BlockSpec(memory_space=pltpu.SMEM if i < smem else pltpu.VMEM)
        for i in range(len(args))
    ]
    many = isinstance(outs, list)
    shapes = outs if many else [outs]
    moved_bytes = sum(a.size * a.dtype.itemsize for a in list(args) + shapes)
    result = pl.pallas_call(
        body,
        out_shape=shapes,
        in_specs=specs,
        out_specs=[pl.BlockSpec(memory_space=pltpu.VMEM) for _ in shapes],
        scratch_shapes=list(scratch),
        compiler_params=pltpu.CompilerParams(vmem_limit_bytes=vmem),
        cost_estimate=pl.CostEstimate(
            flops=int(flops), bytes_accessed=int(moved_bytes), transcendentals=0
        ),
    )(*args)
    return result if many else result[0]


def dot(a, b):
    return jnp.dot(a, b, preferred_element_type=f32)


def dot_last(a, b):
    return lax.dot_general(a, b, (((1,), (1,)), ((), ())), preferred_element_type=f32)


def rms_scale(rows):
    return lax.rsqrt(jnp.mean(rows * rows, axis=-1, keepdims=True) + epsilon)


def iota(shape, dim):
    return lax.broadcasted_iota(jnp.int32, shape, dim)


def stacked(rows):
    width = rows.shape[1] // PARTS
    return jnp.concatenate([rows[:, p * width : (p + 1) * width] for p in range(PARTS)], axis=0)


def place_across(route_row, experts, capacity):
    tokens = route_row.shape[1]
    names = iota((max(8, experts), tokens), 0)
    onehot = jnp.where(names == route_row, 1.0, 0.0)
    earlier = jnp.where(iota((tokens, tokens), 0) < iota((tokens, tokens), 1), 1.0, 0.0)
    before = dot(onehot.astype(bf16), earlier.astype(bf16))
    place = onehot * (before + (names * (PARTS * capacity)).astype(f32))
    return jnp.sum(place, axis=0, keepdims=True).astype(jnp.int32)


def place_down(route_column, experts, capacity):
    tokens = route_column.shape[0]
    names = iota((tokens, LANES), 1)
    onehot = jnp.where(names == route_column, 1.0, 0.0)
    earlier = jnp.where(iota((tokens, tokens), 1) < iota((tokens, tokens), 0), 1.0, 0.0)
    before = dot(earlier.astype(bf16), onehot.astype(bf16))
    place = onehot * (before + (names * (PARTS * capacity)).astype(f32))
    return jnp.sum(place, axis=1, keepdims=True).astype(jnp.int32)


def pack_into(rows, place, out_refs, capacity):
    tokens = rows.shape[0]
    height = PARTS * capacity
    total = height * len(out_refs)
    places = jnp.concatenate([place + p * capacity for p in range(PARTS)], axis=1)
    pick = jnp.where(iota((total, PARTS * tokens), 0) == places, 1.0, 0.0).astype(bf16)
    packed = dot(pick, stacked(rows)).astype(bf16)
    for e, ref in enumerate(out_refs):
        ref[...] = packed[e * height : (e + 1) * height]


def back_pack_body(experts, capacity, route_ref, gate_ref, gain_ref, middle_ref, grad_ref, *outs):
    place = place_across(route_ref[...], experts, capacity)
    middle = middle_ref[...].astype(f32)
    normed = (middle * rms_scale(middle) * gain_ref[...]).astype(bf16)
    pack_into(normed, place, outs[:experts], capacity)
    scaled = (gate_ref[...] * grad_ref[...].astype(f32)).astype(bf16)
    pack_into(scaled, place, outs[experts:], capacity)


def join_body(capacity, *refs):
    chunks, out = refs[:-1], refs[-1]
    sources = len(chunks)
    height = PARTS * capacity
    rows = jnp.concatenate([ref[...] for ref in chunks], axis=0)
    slots = sources * capacity
    width = rows.shape[1]
    index = iota((slots, 1), 0)
    source = index * 0
    for s in range(1, sources):
        source = source + jnp.where(index >= s * capacity, 1, 0)
    first = index + source * (height - capacity)
    columns = iota((slots, rows.shape[0]), 1)
    for p in range(PARTS):
        pick = jnp.where(columns == first + p * capacity, 1.0, 0.0).astype(bf16)
        out[:, p * width : (p + 1) * width] = dot(pick, rows).astype(bf16)


def split_body(capacity, own_ref, core_ref, chip_ref, *outs):
    total = own_ref[...].astype(f32) + core_ref[...].astype(f32) + chip_ref[...].astype(f32)
    rows = stacked(total.astype(bf16))
    height = PARTS * capacity
    slots = own_ref.shape[0]
    count = height * len(outs)
    index = iota((count, 1), 0)
    group = index * 0
    source = index * 0
    for g in range(1, count // capacity):
        group = group + jnp.where(index >= g * capacity, 1, 0)
    for s in range(1, len(outs)):
        source = source + jnp.where(index >= s * height, 1, 0)
    part = group - source * PARTS
    place = part * slots + source * capacity + index - group * capacity
    pick = jnp.where(iota((count, PARTS * slots), 1) == place, 1.0, 0.0).astype(bf16)
    packed = dot(pick, rows).astype(bf16)
    for s, ref in enumerate(outs):
        ref[...] = packed[s * height : (s + 1) * height]


def unpacked(route_column, chunk_refs, experts, capacity):
    tokens = route_column.shape[0]
    place = place_down(route_column, experts, capacity)
    rows = jnp.concatenate([ref[...] for ref in chunk_refs], axis=0)
    columns = iota((tokens, rows.shape[0]), 1)
    parts = []
    for p in range(PARTS):
        pick = jnp.where(columns == place + p * capacity, 1.0, 0.0).astype(bf16)
        parts.append(dot(pick, rows))
    return jnp.concatenate(parts, axis=1)


def front_finish_body(experts, capacity, route_ref, gate_ref, middle_ref, *refs):
    chunks, out = refs[:-1], refs[-1]
    contrib = gate_ref[...] * unpacked(route_ref[...], chunks, experts, capacity)
    out[...] = (middle_ref[...].astype(f32) + contrib).astype(bf16)


def back_finish_body(experts, capacity, route_ref, gain_ref, middle_ref, grad_ref, *refs):
    chunks, out = refs[:-1], refs[-1]
    amount = gain_ref[...] * unpacked(route_ref[...], chunks, experts, capacity)
    middle = middle_ref[...].astype(f32)
    scale = rms_scale(middle)
    cube = scale * scale * scale
    mean = jnp.mean(middle * amount, axis=-1, keepdims=True)
    out[...] = (grad_ref[...].astype(f32) + scale * amount - middle * cube * mean).astype(bf16)


def forward_body(first_ref, second_ref, gate_ref, up_ref, down_ref, first_out, second_out):
    half = first_ref.shape[0]
    rows = jnp.concatenate([first_ref[...], second_ref[...]], axis=0)
    gate_val = dot(rows, gate_ref[...])
    up_val = dot(rows, up_ref[...])
    hidden = (gate_val / (1.0 + jnp.exp(-gate_val)) * up_val).astype(bf16)
    width = down_ref.shape[1]
    step = 4 * LANES
    for n in range(0, width, step):
        value = dot(hidden, down_ref[:, n : n + step]).astype(bf16)
        first_out[:, n : n + step] = value[:half]
        second_out[:, n : n + step] = value[half:]


def backward_body(
    first_ref, second_ref, first_grad, second_grad, gate_ref, up_ref, down_ref, first_out, second_out
):
    half = first_ref.shape[0]
    rows = jnp.concatenate([first_ref[...], second_ref[...]], axis=0)
    gate_val = dot(rows, gate_ref[...])
    up_val = dot(rows, up_ref[...])
    grads = jnp.concatenate([first_grad[...], second_grad[...]], axis=0)
    down_back = dot_last(grads, down_ref[...])
    sigmoid_val = 1.0 / (1.0 + jnp.exp(-gate_val))
    slope_val = sigmoid_val * (1.0 + gate_val * (1.0 - sigmoid_val))
    gate_grad = (down_back * up_val * slope_val).astype(bf16)
    up_grad = (down_back * gate_val * sigmoid_val).astype(bf16)
    width = down_ref.shape[1]
    step = 4 * LANES
    for n in range(0, width, step):
        value = dot_last(gate_grad, gate_ref[n : n + step])
        value = (value + dot_last(up_grad, up_ref[n : n + step])).astype(bf16)
        first_out[:, n : n + step] = value[:half]
        second_out[:, n : n + step] = value[half:]


def attend_body(
    experts,
    capacity,
    chosen_ref,
    index_ref,
    base_ref,
    route_ref,
    gain_ref,
    input_ref,
    query_ref,
    kv0,
    kv1,
    kv2,
    kv3,
    middle_ref,
    *refs,
):
    outs, (kv_all, kv_now, stack, attended) = refs[:experts], refs[experts:]
    tokens, width = query_ref.shape
    rows_each = kv0.shape[0]
    for place, ref in enumerate((kv0, kv1, kv2, kv3)):
        kv_all[place * rows_each : (place + 1) * rows_each, : ref.shape[1]] = ref[...]
    attended[...] = jnp.zeros_like(attended)
    heads_each = HEADS // KV_HEADS
    period = 8
    window = 2 * LANES
    keys = SEL * BLK
    lane = iota((keys, LANES), 1)
    batch = 4
    scale = HEAD_DIM**-0.5

    def one_block(block, _):
        top = pl.multiple_of(block * BLK, BLK)
        position = (base_ref[0] + block) * BLK + (iota((batch * BLK, keys), 0) & (BLK - 1))
        for head in range(KV_HEADS):
            key_pos = iota((1, keys), 1)
            shift = key_pos * 0
            for s in range(SEL):
                at = (block * KV_HEADS + head) * SEL + s
                start = pl.multiple_of(index_ref[at] * BLK, BLK)
                kv_now[s * BLK : (s + 1) * BLK, :] = kv_all[pl.ds(start, BLK), :].astype(f32)
                inside = (key_pos >= s * BLK) & (key_pos < (s + 1) * BLK)
                shift = jnp.where(inside, (chosen_ref[at] - s) * BLK, shift)
            allowed = key_pos + shift <= position
            sides = []
            for side in range(2):
                lead = (side * KV_HEADS + head) * HEAD_DIM
                tile = min(lead // LANES, 2)
                piece = kv_now[:, tile * LANES : tile * LANES + window]
                offset = lead - tile * LANES
                if offset:
                    piece = pltpu.roll(piece, window - offset, 1)
                sides.append(jnp.where(lane < HEAD_DIM, piece[:, :LANES], 0.0).astype(bf16))
            key_rows, value_rows = sides
            spots = []
            for j in range(heads_each):
                c = j % period
                tile = min(c * HEAD_DIM // LANES, period - 3)
                offset = c * HEAD_DIM - tile * LANES
                tile = tile + (j // period) * (period - 1) + head * heads_each * HEAD_DIM // LANES
                spots.append((tile * LANES, offset))
            for j, (lead, offset) in enumerate(spots):
                piece = query_ref[pl.ds(top, BLK), lead : lead + window].astype(f32)
                if offset:
                    piece = pltpu.roll(piece, window - offset, 1)
                stack[j * BLK : (j + 1) * BLK, :] = piece[:, :LANES].astype(bf16)
            for b in range(0, heads_each, batch):
                scores = dot_last(stack[b * BLK : (b + batch) * BLK, :], key_rows) * scale
                scores = jnp.where(allowed, scores, negative_large)
                exp_scores = jnp.exp(scores - jnp.max(scores, axis=-1, keepdims=True))
                total = jnp.sum(exp_scores, axis=-1, keepdims=True)
                mixed = dot((exp_scores / total).astype(bf16), value_rows)
                for i in range(batch):
                    lead, offset = spots[b + i]
                    piece = mixed[i * BLK : (i + 1) * BLK]
                    piece = jnp.concatenate([piece, jnp.zeros_like(piece)], axis=1)
                    if offset:
                        piece = pltpu.roll(piece, offset, 1)
                    spot = (pl.ds(top, BLK), slice(lead, lead + window))
                    attended[spot] = attended[spot] + piece
        return 0

    lax.fori_loop(0, tokens // BLK, one_block, 0)
    middle = (input_ref[...].astype(f32) + attended[...]).astype(bf16)
    middle_ref[...] = middle
    middle = middle.astype(f32)
    normed = (middle * rms_scale(middle) * gain_ref[...]).astype(bf16)
    pack_into(normed, place_across(route_ref[...], experts, capacity), outs, capacity)


def after(arrays, others):
    count = len(arrays)
    return list(lax.optimization_barrier(tuple(arrays) + tuple(others))[:count])


def shape_of(rows, columns, kind=bf16):
    return jax.ShapeDtypeStruct((rows, columns), kind)


def shards(
    front_input,
    queries,
    keys_values,
    selected_blocks,
    front_route,
    front_gate,
    back_middle,
    back_grad,
    back_route,
    back_gate,
    norm_gain,
    gate_slice,
    up_slice,
    down_slice,
):
    tokens, width = front_input.shape[1:]
    length = lax.axis_size("expert")
    experts = length // GROUP
    average = tokens // experts
    capacity = average + max(1, average // 8)
    slots = experts * capacity
    hidden_width = gate_slice.shape[3]
    weights = (gate_slice[0, 0], up_slice[0, 0], down_slice[0, 0])
    me = lax.axis_index("expert")
    group = me // GROUP
    chunk = shape_of(PARTS * capacity, width // PARTS)
    piece = shape_of(slots, width)
    whole = shape_of(tokens, width)

    column = [keys_values[0]]
    for back in range(1, experts):
        pairs = [(i, i + back * GROUP) for i in range(length - back * GROUP)]
        column.append(lax.ppermute(keys_values[0], "expert", pairs))
    front_from = lax.rem(front_route[0] - group + experts, experts)
    back_from = lax.rem(back_route[0] - group + experts, experts)
    front_row, back_row = front_from.reshape(1, tokens), back_from.reshape(1, tokens)

    pack_flops = 4 * slots * PARTS * tokens * width
    packed = call(
        functools.partial(back_pack_body, experts, capacity),
        [chunk] * (2 * experts),
        (back_row, back_gate[0], norm_gain, back_middle[0], back_grad[0]),
        flops=2 * pack_flops,
    )
    column = after(column, [packed[0]])
    column = jnp.concatenate(column, axis=0)
    other_chip = swapped(column, 2)
    kv = [column, other_chip, swapped(column, 1), swapped(other_chip, 1)]

    packed = after(packed, [column])

    def sent(chunks):
        return [chunks[0]] + [turned(chunks[k], k) for k in range(1, experts)]

    def joined(chunks):
        return call(functools.partial(join_body, capacity), piece, chunks, flops=pack_flops)

    def pieces_of(rows):
        other = swapped(rows, 2)
        return [rows, swapped(rows, 1), other, swapped(other, 1)]

    def shares(near, far):
        chip = far[0].astype(f32) + swapped(far[1], 1).astype(f32)
        parts = (near[0], swapped(near[1], 1), swapped(chip.astype(bf16), 2))
        return parts

    def split(parts):
        return call(
            functools.partial(split_body, capacity), [chunk] * experts, parts, flops=pack_flops
        )

    def sent_back(chunks):
        return [chunks[0]] + [turned(chunks[k], -k) for k in range(1, experts)]

    row_chunks = sent(packed[:experts])
    grad_chunks = sent(after(packed[experts:], row_chunks))

    per_device = tokens // BLK
    chosen = selected_blocks[0].reshape(-1)
    owner = chosen // per_device
    place = (owner % GROUP) ^ (me % GROUP)
    place = (place % 2) * 2 + place // 2
    index = (place * experts + group - owner // GROUP) * per_device + chosen % per_device
    index = jnp.clip(index, 0, length * per_device - 1)
    base = (me * per_device).astype(jnp.int32).reshape(1)
    result = call(
        functools.partial(attend_body, experts, capacity),
        [whole] + [chunk] * experts,
        (chosen, index, base, front_row, norm_gain, front_input[0], queries[0], *kv),
        scratch=[
            pltpu.VMEM((length * tokens, 4 * LANES), bf16),
            pltpu.VMEM((SEL * BLK, 4 * LANES), f32),
            pltpu.VMEM((HEADS // KV_HEADS * BLK, LANES), bf16),
            pltpu.VMEM((tokens, width), f32),
        ],
        flops=pack_flops + 4 * tokens * HEADS * SEL * BLK * LANES,
        smem=3,
        vmem=VMEM_BYTES + 2 * length * tokens * 4 * LANES * 2,
    )
    middle, front_chunks = result[0], result[1:]
    front_chunks = sent(front_chunks)
    back_pieces = pieces_of(joined(after(row_chunks, [middle])))
    grad_pieces = pieces_of(joined(after(grad_chunks, [back_pieces[0]])))
    front_rows = joined(front_chunks)
    front_other = swapped(front_rows, 2)

    work = 2 * 2 * slots * width * hidden_width

    def backward(first, second):
        return call(
            backward_body,
            [piece, piece],
            (*back_pieces[first:second], *grad_pieces[first:second], *weights),
            flops=5 * work,
        )

    def forward(first, second):
        return call(
            forward_body,
            [piece, piece],
            (*front_pieces[first:second], *weights),
            flops=3 * work,
        )

    back_far = backward(2, 4)
    back_near = backward(0, 2)
    back_shares = shares(back_near, back_far)

    (front_other,) = after([front_other], back_near + back_far)
    front_pieces = [front_rows, swapped(front_rows, 1), front_other, swapped(front_other, 1)]
    front_far = forward(2, 4)
    front_near = forward(0, 2)
    front_shares = shares(front_near, front_far)

    back_chunks = split(after(back_shares, front_near + front_far))
    back_return = sent_back(back_chunks)
    front_chunks = split(after(front_shares, back_chunks))
    front_return = sent_back(front_chunks)
    back_return = after(back_return, front_chunks)

    back_result = call(
        functools.partial(back_finish_body, experts, capacity),
        whole,
        (back_from, norm_gain, back_middle[0], back_grad[0], *back_return),
        flops=pack_flops,
    )
    back_output = passed_along(back_result, "section", -1)
    front_return = after(front_return, [back_result])
    front_result = call(
        functools.partial(front_finish_body, experts, capacity),
        whole,
        (front_from, front_gate[0], middle, *front_return),
        flops=pack_flops,
    )
    front_output = passed_along(front_result, "section", 1)
    return (front_output[None], back_output[None])


def solution(mesh):
    placed = (
        P("section", "expert", None),
        P("section", "expert", None),
        P("section", "expert", None),
        P("section", "expert", None, None),
        P("section", "expert", None),
        P("section", "expert", None),
        P("section", "expert", None),
        P("section", "expert", None),
        P("section", "expert", None),
        P("section", "expert", None),
        P("section", None),
        P("section", "expert", None, None),
        P("section", "expert", None, None),
        P("section", "expert", None, None),
    )
    return jax.shard_map(
        shards,
        mesh=mesh,
        in_specs=placed,
        out_specs=(P("section", "expert", None), P("section", "expert", None)),
        check_vma=False,
    )
```

```python
import functools

import jax
import jax.numpy as jnp
from jax import lax
from jax.experimental import pallas as pl
from jax.experimental.pallas import tpu as pltpu
from jax.sharding import PartitionSpec as P

GROUP = 4
HEADS = 32
HEAD_DIM = 112
KV_HEADS = 2
BLK = 64
SEL = 4
PARTS = 4
LANES = 128
VMEM_BYTES = 28 * 1024 * 1024

epsilon = 1e-06
negative_large = -1e30
bf16 = jnp.bfloat16
f32 = jnp.float32


def passed_along(array, by, back=0):
    sections, length = lax.axis_size("section"), lax.axis_size("expert")
    pairs = [
        (s * length + i, (s + by) % sections * length + (i - back * GROUP) % length)
        for s in range(sections)
        for i in range(length)
    ]
    return lax.ppermute(array, ("section", "expert"), pairs)


def swapped(array, bit):
    return lax.ppermute(array, "expert", [(i, i ^ bit) for i in range(lax.axis_size("expert"))])


def turned(array, by):
    length = lax.axis_size("expert")
    return lax.ppermute(
        array, "expert", [(i, (i + by * GROUP) % length) for i in range(length)]
    )


def call(body, outs, args, scratch=(), flops=0, smem=0, vmem=VMEM_BYTES):
    specs = [
        pl.BlockSpec(memory_space=pltpu.SMEM if i < smem else pltpu.VMEM)
        for i in range(len(args))
    ]
    many = isinstance(outs, list)
    shapes = outs if many else [outs]
    moved_bytes = sum(a.size * a.dtype.itemsize for a in list(args) + shapes)
    result = pl.pallas_call(
        body,
        out_shape=shapes,
        in_specs=specs,
        out_specs=[pl.BlockSpec(memory_space=pltpu.VMEM) for _ in shapes],
        scratch_shapes=list(scratch),
        compiler_params=pltpu.CompilerParams(vmem_limit_bytes=vmem),
        cost_estimate=pl.CostEstimate(
            flops=int(flops), bytes_accessed=int(moved_bytes), transcendentals=0
        ),
    )(*args)
    return result if many else result[0]


def dot(a, b):
    return jnp.dot(a, b, preferred_element_type=f32)


def dot_last(a, b):
    return lax.dot_general(a, b, (((1,), (1,)), ((), ())), preferred_element_type=f32)


def rms_scale(rows):
    return lax.rsqrt(jnp.mean(rows * rows, axis=-1, keepdims=True) + epsilon)


def iota(shape, dim):
    return lax.broadcasted_iota(jnp.int32, shape, dim)


def stacked(rows):
    width = rows.shape[1] // PARTS
    return jnp.concatenate([rows[:, p * width : (p + 1) * width] for p in range(PARTS)], axis=0)


def place_across(route_row, experts, capacity):
    tokens = route_row.shape[1]
    names = iota((max(8, experts), tokens), 0)
    onehot = jnp.where(names == route_row, 1.0, 0.0)
    earlier = jnp.where(iota((tokens, tokens), 0) < iota((tokens, tokens), 1), 1.0, 0.0)
    before = dot(onehot.astype(bf16), earlier.astype(bf16))
    place = onehot * (before + (names * (PARTS * capacity)).astype(f32))
    return jnp.sum(place, axis=0, keepdims=True).astype(jnp.int32)


def place_down(route_column, experts, capacity):
    tokens = route_column.shape[0]
    names = iota((tokens, LANES), 1)
    onehot = jnp.where(names == route_column, 1.0, 0.0)
    earlier = jnp.where(iota((tokens, tokens), 1) < iota((tokens, tokens), 0), 1.0, 0.0)
    before = dot(earlier.astype(bf16), onehot.astype(bf16))
    place = onehot * (before + (names * (PARTS * capacity)).astype(f32))
    return jnp.sum(place, axis=1, keepdims=True).astype(jnp.int32)


def pack_into(rows, place, out_refs, capacity):
    tokens = rows.shape[0]
    height = PARTS * capacity
    total = height * len(out_refs)
    places = jnp.concatenate([place + p * capacity for p in range(PARTS)], axis=1)
    pick = jnp.where(iota((total, PARTS * tokens), 0) == places, 1.0, 0.0).astype(bf16)
    packed = dot(pick, stacked(rows)).astype(bf16)
    for e, ref in enumerate(out_refs):
        ref[...] = packed[e * height : (e + 1) * height]


def back_pack_body(experts, capacity, route_ref, gate_ref, gain_ref, middle_ref, grad_ref, *outs):
    place = place_across(route_ref[...], experts, capacity)
    middle = middle_ref[...].astype(f32)
    normed = (middle * rms_scale(middle) * gain_ref[...]).astype(bf16)
    pack_into(normed, place, outs[:experts], capacity)
    scaled = (gate_ref[...] * grad_ref[...].astype(f32)).astype(bf16)
    pack_into(scaled, place, outs[experts:], capacity)


def join_body(capacity, *refs):
    chunks, out = refs[:-1], refs[-1]
    sources = len(chunks)
    height = PARTS * capacity
    rows = jnp.concatenate([ref[...] for ref in chunks], axis=0)
    slots = sources * capacity
    width = rows.shape[1]
    index = iota((slots, 1), 0)
    source = index * 0
    for s in range(1, sources):
        source = source + jnp.where(index >= s * capacity, 1, 0)
    first = index + source * (height - capacity)
    columns = iota((slots, rows.shape[0]), 1)
    for p in range(PARTS):
        pick = jnp.where(columns == first + p * capacity, 1.0, 0.0).astype(bf16)
        out[:, p * width : (p + 1) * width] = dot(pick, rows).astype(bf16)


def split_body(capacity, count_shares, *refs):
    shares, outs = refs[:count_shares], refs[count_shares:]
    total = shares[0][...].astype(f32)
    for ref in shares[1:]:
        total = total + ref[...].astype(f32)
    rows = stacked(total.astype(bf16))
    height = PARTS * capacity
    slots = shares[0].shape[0]
    count = height * len(outs)
    index = iota((count, 1), 0)
    group = index * 0
    source = index * 0
    for g in range(1, count // capacity):
        group = group + jnp.where(index >= g * capacity, 1, 0)
    for s in range(1, len(outs)):
        source = source + jnp.where(index >= s * height, 1, 0)
    part = group - source * PARTS
    place = part * slots + source * capacity + index - group * capacity
    pick = jnp.where(iota((count, PARTS * slots), 1) == place, 1.0, 0.0).astype(bf16)
    packed = dot(pick, rows).astype(bf16)
    for s, ref in enumerate(outs):
        ref[...] = packed[s * height : (s + 1) * height]


def unpacked(route_column, chunk_refs, experts, capacity):
    tokens = route_column.shape[0]
    place = place_down(route_column, experts, capacity)
    rows = jnp.concatenate([ref[...] for ref in chunk_refs], axis=0)
    columns = iota((tokens, rows.shape[0]), 1)
    parts = []
    for p in range(PARTS):
        pick = jnp.where(columns == place + p * capacity, 1.0, 0.0).astype(bf16)
        parts.append(dot(pick, rows))
    return jnp.concatenate(parts, axis=1)


def front_finish_body(experts, capacity, route_ref, gate_ref, middle_ref, *refs):
    chunks, out = refs[:-1], refs[-1]
    contrib = gate_ref[...] * unpacked(route_ref[...], chunks, experts, capacity)
    out[...] = (middle_ref[...].astype(f32) + contrib).astype(bf16)


def back_finish_body(experts, capacity, route_ref, gain_ref, middle_ref, grad_ref, *refs):
    chunks, out = refs[:-1], refs[-1]
    amount = gain_ref[...] * unpacked(route_ref[...], chunks, experts, capacity)
    middle = middle_ref[...].astype(f32)
    scale = rms_scale(middle)
    cube = scale * scale * scale
    mean = jnp.mean(middle * amount, axis=-1, keepdims=True)
    out[...] = (grad_ref[...].astype(f32) + scale * amount - middle * cube * mean).astype(bf16)


def hidden_body(first_ref, second_ref, gate_ref, up_ref, out_ref):
    rows = jnp.concatenate([first_ref[...], second_ref[...]], axis=0)
    gate_val = dot(rows, gate_ref[...])
    up_val = dot(rows, up_ref[...])
    out_ref[...] = (gate_val / (1.0 + jnp.exp(-gate_val)) * up_val).astype(bf16)


def output_body(own_ref, other_ref, down_ref, top_ref, low_ref, first_out, second_out):
    half = first_out.shape[0]
    hidden = jnp.concatenate([own_ref[...], other_ref[...]], axis=1)
    step = 4 * LANES
    for n in range(0, down_ref.shape[1], step):
        part = slice(n, n + step)
        weight = jnp.concatenate([down_ref[:, part], top_ref[:, part], low_ref[:, part]], axis=0)
        value = dot(hidden, weight).astype(bf16)
        first_out[:, part] = value[:half]
        second_out[:, part] = value[half:]


def down_back_body(first_ref, second_ref, down_ref, top_ref, low_ref, own_out, other_out):
    grads = jnp.concatenate([first_ref[...], second_ref[...]], axis=0)
    own_out[...] = dot_last(grads, down_ref[...]).astype(own_out.dtype)
    other = jnp.concatenate([top_ref[...], low_ref[...]], axis=0)
    other_out[...] = dot_last(grads, other).astype(other_out.dtype)


def backward_body(first_ref, second_ref, back_ref, gate_ref, up_ref, first_out, second_out):
    half = first_ref.shape[0]
    rows = jnp.concatenate([first_ref[...], second_ref[...]], axis=0)
    gate_val = dot(rows, gate_ref[...])
    up_val = dot(rows, up_ref[...])
    down_back = back_ref[...].astype(f32)
    sigmoid_val = 1.0 / (1.0 + jnp.exp(-gate_val))
    slope_val = sigmoid_val * (1.0 + gate_val * (1.0 - sigmoid_val))
    gate_grad = (down_back * up_val * slope_val).astype(bf16)
    up_grad = (down_back * gate_val * sigmoid_val).astype(bf16)
    step = 4 * LANES
    for n in range(0, gate_ref.shape[0], step):
        value = dot_last(gate_grad, gate_ref[n : n + step])
        value = (value + dot_last(up_grad, up_ref[n : n + step])).astype(bf16)
        first_out[:, n : n + step] = value[:half]
        second_out[:, n : n + step] = value[half:]


def attend_body(
    experts,
    capacity,
    chosen_ref,
    index_ref,
    base_ref,
    route_ref,
    gain_ref,
    input_ref,
    query_ref,
    kv0,
    kv1,
    kv2,
    kv3,
    middle_ref,
    *refs,
):
    outs, (kv_all, kv_now, stack, attended) = refs[:experts], refs[experts:]
    tokens, width = query_ref.shape
    rows_each = kv0.shape[0]
    for place, ref in enumerate((kv0, kv1, kv2, kv3)):
        kv_all[place * rows_each : (place + 1) * rows_each, : ref.shape[1]] = ref[...]
    attended[...] = jnp.zeros_like(attended)
    heads_each = HEADS // KV_HEADS
    period = 8
    window = 2 * LANES
    keys = SEL * BLK
    lane = iota((keys, LANES), 1)
    batch = 4
    scale = HEAD_DIM**-0.5

    def one_block(block, _):
        top = pl.multiple_of(block * BLK, BLK)
        position = (base_ref[0] + block) * BLK + (iota((batch * BLK, keys), 0) & (BLK - 1))
        for head in range(KV_HEADS):
            key_pos = iota((1, keys), 1)
            shift = key_pos * 0
            for s in range(SEL):
                at = (block * KV_HEADS + head) * SEL + s
                start = pl.multiple_of(index_ref[at] * BLK, BLK)
                kv_now[s * BLK : (s + 1) * BLK, :] = kv_all[pl.ds(start, BLK), :].astype(f32)
                inside = (key_pos >= s * BLK) & (key_pos < (s + 1) * BLK)
                shift = jnp.where(inside, (chosen_ref[at] - s) * BLK, shift)
            allowed = key_pos + shift <= position
            sides = []
            for side in range(2):
                lead = (side * KV_HEADS + head) * HEAD_DIM
                tile = min(lead // LANES, 2)
                piece = kv_now[:, tile * LANES : tile * LANES + window]
                offset = lead - tile * LANES
                if offset:
                    piece = pltpu.roll(piece, window - offset, 1)
                sides.append(jnp.where(lane < HEAD_DIM, piece[:, :LANES], 0.0).astype(bf16))
            key_rows, value_rows = sides
            spots = []
            for j in range(heads_each):
                c = j % period
                tile = min(c * HEAD_DIM // LANES, period - 3)
                offset = c * HEAD_DIM - tile * LANES
                tile = tile + (j // period) * (period - 1) + head * heads_each * HEAD_DIM // LANES
                spots.append((tile * LANES, offset))
            for j, (lead, offset) in enumerate(spots):
                piece = query_ref[pl.ds(top, BLK), lead : lead + window].astype(f32)
                if offset:
                    piece = pltpu.roll(piece, window - offset, 1)
                stack[j * BLK : (j + 1) * BLK, :] = piece[:, :LANES].astype(bf16)
            for b in range(0, heads_each, batch):
                scores = dot_last(stack[b * BLK : (b + batch) * BLK, :], key_rows) * scale
                scores = jnp.where(allowed, scores, negative_large)
                exp_scores = jnp.exp(scores - jnp.max(scores, axis=-1, keepdims=True))
                total = jnp.sum(exp_scores, axis=-1, keepdims=True)
                mixed = dot((exp_scores / total).astype(bf16), value_rows)
                for i in range(batch):
                    lead, offset = spots[b + i]
                    piece = mixed[i * BLK : (i + 1) * BLK]
                    piece = jnp.concatenate([piece, jnp.zeros_like(piece)], axis=1)
                    if offset:
                        piece = pltpu.roll(piece, offset, 1)
                    spot = (pl.ds(top, BLK), slice(lead, lead + window))
                    attended[spot] = attended[spot] + piece
        return 0

    lax.fori_loop(0, tokens // BLK, one_block, 0)
    middle = (input_ref[...].astype(f32) + attended[...]).astype(bf16)
    middle_ref[...] = middle
    middle = middle.astype(f32)
    normed = (middle * rms_scale(middle) * gain_ref[...]).astype(bf16)
    pack_into(normed, place_across(route_ref[...], experts, capacity), outs, capacity)


def after(arrays, others):
    count = len(arrays)
    return list(lax.optimization_barrier(tuple(arrays) + tuple(others))[:count])


def shape_of(rows, columns, kind=bf16):
    return jax.ShapeDtypeStruct((rows, columns), kind)


def shards(
    front_input,
    queries,
    keys_values,
    selected_blocks,
    front_route,
    front_gate,
    back_middle,
    back_grad,
    back_route,
    back_gate,
    norm_gain,
    gate_slice,
    up_slice,
    down_slice,
):
    tokens, width = front_input.shape[1:]
    length = lax.axis_size("expert")
    experts = length // GROUP
    average = tokens // experts
    capacity = average + max(1, average // 8)
    slots = experts * capacity
    hidden_width = gate_slice.shape[3]
    w_gate, w_up, w_down = gate_slice[0, 0], up_slice[0, 0], down_slice[0, 0]
    me = lax.axis_index("expert")
    group = me // GROUP
    chunk = shape_of(PARTS * capacity, width // PARTS)
    piece = shape_of(slots, width)
    whole = shape_of(tokens, width)

    column = [keys_values[0]]
    for back in range(1, experts):
        pairs = [(i, i + back * GROUP) for i in range(length - back * GROUP)]
        column.append(lax.ppermute(keys_values[0], "expert", pairs))
    early = hidden_width * 3 // 8
    down_top = swapped(w_down[:early], 2)

    front_from = lax.rem(front_route[0] - group + experts, experts)
    back_from = lax.rem(back_route[0] - group + experts, experts)
    front_row, back_row = front_from.reshape(1, tokens), back_from.reshape(1, tokens)

    pack_flops = 4 * slots * PARTS * tokens * width
    packed = call(
        functools.partial(back_pack_body, experts, capacity),
        [chunk] * (2 * experts),
        (back_row, back_gate[0], norm_gain, back_middle[0], back_grad[0]),
        flops=2 * pack_flops,
    )
    column = after(column, [packed[0]])
    column = jnp.concatenate(column, axis=0)
    other_chip = swapped(after([column], [down_top])[0], 2)
    kv = [column, other_chip, swapped(column, 1), None]
    packed = after(packed, [column])
    down_low = swapped(after([w_down[early:]], [other_chip])[0], 2)
    downs = (w_down, down_top, down_low)

    front_small = jnp.concatenate([front_from.astype(f32), front_gate[0]], axis=0).reshape(1, -1)
    back_small = jnp.concatenate([back_from.astype(f32).reshape(1, -1), norm_gain], axis=1)

    def sent(chunks):
        return [chunks[0]] + [turned(chunks[k], k) for k in range(1, experts)]

    def joined(chunks):
        return call(functools.partial(join_body, capacity), piece, chunks, flops=pack_flops)

    def pieces_of(rows):
        other = swapped(rows, 2)
        return [rows, swapped(rows, 1), other, swapped(other, 1)]

    def split(parts):
        return call(
            functools.partial(split_body, capacity, len(parts)),
            [chunk] * experts,
            parts,
            flops=pack_flops,
        )

    def sent_back(chunks, by):
        return [passed_along(chunks[k], by, k) for k in range(experts)]

    row_chunks = packed[:experts]
    for k in range(1, experts, 2):
        row_chunks[k] = turned(row_chunks[k], k)
    arrived = row_chunks[1::2]
    for k in range(2, experts, 2):
        row_chunks[k] = turned(after([row_chunks[k]], arrived)[0], k)
    kv[3] = swapped(after([other_chip], arrived)[0], 1)

    per_device = tokens // BLK
    chosen = selected_blocks[0].reshape(-1)
    owner = chosen // per_device
    place = (owner % GROUP) ^ (me % GROUP)
    place = (place % 2) * 2 + place // 2
    index = (place * experts + group - owner // GROUP) * per_device + chosen % per_device
    index = jnp.clip(index, 0, length * per_device - 1)
    base = (me * per_device).astype(jnp.int32).reshape(1)
    result = call(
        functools.partial(attend_body, experts, capacity),
        [whole] + [chunk] * experts,
        (chosen, index, base, front_row, norm_gain, front_input[0], queries[0], *kv),
        scratch=[
            pltpu.VMEM((length * tokens, 4 * LANES), bf16),
            pltpu.VMEM((SEL * BLK, 4 * LANES), f32),
            pltpu.VMEM((HEADS // KV_HEADS * BLK, LANES), bf16),
            pltpu.VMEM((tokens, width), f32),
        ],
        flops=pack_flops + 4 * tokens * HEADS * SEL * BLK * LANES,
        smem=3,
        vmem=VMEM_BYTES + 2 * length * tokens * 4 * LANES * 2,
    )
    middle, front_chunks = result[0], result[1:]
    front_chunks = sent(after(front_chunks, row_chunks))
    back_pieces = pieces_of(after([joined(after(row_chunks, [middle]))], [down_low])[0])
    front_small, back_small = after([front_small, back_small], [back_pieces[0]])
    there_small = passed_along(front_small, 1)
    there_back_small = passed_along(back_small, -1)
    there_front_from = there_small[0, :tokens].astype(jnp.int32).reshape(tokens, 1)
    there_front_gate = there_small[0, tokens:].reshape(tokens, 1)
    there_back_from = there_back_small[0, :tokens].astype(jnp.int32).reshape(tokens, 1)
    there_gain = there_back_small[:, tokens:]
    there_back_middle = passed_along(after([back_middle[0]], [back_pieces[0]])[0], -1)
    front_chunks = after(front_chunks, [back_pieces[0], there_small, there_back_small])
    grad_chunks = sent(after(packed[experts:], front_chunks))
    there_back_grad = passed_along(after([back_grad[0]], [there_back_middle])[0], -1)
    front_pieces = pieces_of(joined(after(front_chunks, [there_back_middle])))
    there_middle = passed_along(after([middle], [there_back_grad])[0], 1)
    grad_near = joined(after(grad_chunks, [front_pieces[0], there_back_grad]))
    grad_near = [grad_near, swapped(grad_near, 1)]

    work = 2 * 2 * slots * width * hidden_width
    pair = 2 * slots

    def hidden(rows):
        return call(
            hidden_body, shape_of(pair, hidden_width), (*rows, w_gate, w_up), flops=2 * work
        )

    def backward(rows, grads):
        return call(backward_body, [piece, piece], (*rows, grads, w_gate, w_up), flops=4 * work)

    hidden_near = hidden(front_pieces[:2])
    hidden_far = hidden(front_pieces[2:])
    down_back, other_back = call(
        down_back_body,
        [shape_of(pair, hidden_width, f32), shape_of(pair, hidden_width)],
        (*grad_near, *downs),
        flops=2 * work,
    )
    hidden_other = swapped(hidden_far, 2)
    far_back = swapped(other_back, 2)

    back_near = backward(back_pieces[:2], down_back)
    back_far = backward(back_pieces[2:], far_back)
    chip = back_far[0].astype(f32) + swapped(back_far[1], 1).astype(f32)
    back_shares = (back_near[0], swapped(back_near[1], 1), swapped(chip.astype(bf16), 2))

    front_own, front_core = call(
        output_body, [piece, piece], (hidden_near, hidden_other, *downs), flops=2 * work
    )
    front_chunks = split((front_own, swapped(front_core, 1)))
    front_return = sent_back(front_chunks, 1)

    back_chunks = split(after(back_shares, front_chunks))
    back_return = sent_back(back_chunks, -1)

    front_return = after(front_return, back_chunks)
    front_output = call(
        functools.partial(front_finish_body, experts, capacity),
        whole,
        (there_front_from, there_front_gate, there_middle, *front_return),
        flops=pack_flops,
    )
    back_return = after(back_return, [front_output])
    back_output = call(
        functools.partial(back_finish_body, experts, capacity),
        whole,
        (there_back_from, there_gain, there_back_middle, there_back_grad, *back_return),
        flops=pack_flops,
    )
    return (front_output[None], back_output[None])


def solution(mesh):
    placed = (
        P("section", "expert", None),
        P("section", "expert", None),
        P("section", "expert", None),
        P("section", "expert", None, None),
        P("section", "expert", None),
        P("section", "expert", None),
        P("section", "expert", None),
        P("section", "expert", None),
        P("section", "expert", None),
        P("section", "expert", None),
        P("section", None),
        P("section", "expert", None, None),
        P("section", "expert", None, None),
        P("section", "expert", None, None),
    )
    return jax.shard_map(
        shards,
        mesh=mesh,
        in_specs=placed,
        out_specs=(P("section", "expert", None), P("section", "expert", None)),
        check_vma=False,
    )
```

```python
import functools

import jax
import jax.numpy as jnp
from jax import lax
from jax.experimental import pallas as pl
from jax.experimental.pallas import tpu as pltpu
from jax.sharding import PartitionSpec as P

GROUP = 4
HEADS = 32
HEAD_DIM = 112
KV_HEADS = 2
BLK = 64
SEL = 4
PARTS = 4
LANES = 128
VMEM_BYTES = 28 * 1024 * 1024

epsilon = 1e-06
negative_large = -1e30
bf16 = jnp.bfloat16
f32 = jnp.float32


def passed_along(array, by, back=0):
    sections, length = lax.axis_size("section"), lax.axis_size("expert")
    pairs = [
        (s * length + i, (s + by) % sections * length + (i - back * GROUP) % length)
        for s in range(sections)
        for i in range(length)
    ]
    return lax.ppermute(array, ("section", "expert"), pairs)


def swapped(array, bit):
    return lax.ppermute(array, "expert", [(i, i ^ bit) for i in range(lax.axis_size("expert"))])


def turned(array, by):
    length = lax.axis_size("expert")
    return lax.ppermute(
        array, "expert", [(i, (i + by * GROUP) % length) for i in range(length)]
    )


def call(body, outs, args, scratch=(), flops=0, smem=0, vmem=VMEM_BYTES):
    specs = [
        pl.BlockSpec(memory_space=pltpu.SMEM if i < smem else pltpu.VMEM)
        for i in range(len(args))
    ]
    many = isinstance(outs, list)
    shapes = outs if many else [outs]
    moved_bytes = sum(a.size * a.dtype.itemsize for a in list(args) + shapes)
    result = pl.pallas_call(
        body,
        out_shape=shapes,
        in_specs=specs,
        out_specs=[pl.BlockSpec(memory_space=pltpu.VMEM) for _ in shapes],
        scratch_shapes=list(scratch),
        compiler_params=pltpu.CompilerParams(vmem_limit_bytes=vmem),
        cost_estimate=pl.CostEstimate(
            flops=int(flops), bytes_accessed=int(moved_bytes), transcendentals=0
        ),
    )(*args)
    return list(result) if many else result[0]


def dot(a, b):
    return jnp.dot(a, b, preferred_element_type=f32)


def dot_last(a, b):
    return lax.dot_general(a, b, (((1,), (1,)), ((), ())), preferred_element_type=f32)


def rms_scale(rows):
    return lax.rsqrt(jnp.mean(rows * rows, axis=-1, keepdims=True) + epsilon)


def iota(shape, dim):
    return lax.broadcasted_iota(jnp.int32, shape, dim)


def stacked(rows):
    width = rows.shape[1] // PARTS
    return jnp.concatenate([rows[:, p * width : (p + 1) * width] for p in range(PARTS)], axis=0)


def place_across(route_row, experts, capacity):
    tokens = route_row.shape[1]
    names = iota((max(8, experts), tokens), 0)
    onehot = jnp.where(names == route_row, 1.0, 0.0)
    earlier = jnp.where(iota((tokens, tokens), 0) < iota((tokens, tokens), 1), 1.0, 0.0)
    before = dot(onehot.astype(bf16), earlier.astype(bf16))
    place = onehot * (before + (names * (PARTS * capacity)).astype(f32))
    return jnp.sum(place, axis=0, keepdims=True).astype(jnp.int32)


def place_down(route_column, experts, capacity):
    tokens = route_column.shape[0]
    names = iota((tokens, LANES), 1)
    onehot = jnp.where(names == route_column, 1.0, 0.0)
    earlier = jnp.where(iota((tokens, tokens), 1) < iota((tokens, tokens), 0), 1.0, 0.0)
    before = dot(earlier.astype(bf16), onehot.astype(bf16))
    place = onehot * (before + (names * (PARTS * capacity)).astype(f32))
    return jnp.sum(place, axis=1, keepdims=True).astype(jnp.int32)


def pack_into(rows, place, out_refs, capacity):
    tokens = rows.shape[0]
    height = PARTS * capacity
    total = height * len(out_refs)
    places = jnp.concatenate([place + p * capacity for p in range(PARTS)], axis=1)
    pick = jnp.where(iota((total, PARTS * tokens), 0) == places, 1.0, 0.0).astype(bf16)
    packed = dot(pick, stacked(rows)).astype(bf16)
    for e, ref in enumerate(out_refs):
        ref[...] = packed[e * height : (e + 1) * height]


def back_pack_body(experts, capacity, route_ref, gate_ref, gain_ref, middle_ref, grad_ref, *outs):
    place = place_across(route_ref[...], experts, capacity)
    middle = middle_ref[...].astype(f32)
    normed = (middle * rms_scale(middle) * gain_ref[...]).astype(bf16)
    pack_into(normed, place, outs[:experts], capacity)
    scaled = (gate_ref[...] * grad_ref[...].astype(f32)).astype(bf16)
    pack_into(scaled, place, outs[experts:], capacity)


def join_body(capacity, *refs):
    chunks, out = refs[:-1], refs[-1]
    sources = len(chunks)
    height = PARTS * capacity
    rows = jnp.concatenate([ref[...] for ref in chunks], axis=0)
    slots = sources * capacity
    width = rows.shape[1]
    index = iota((slots, 1), 0)
    source = index * 0
    for s in range(1, sources):
        source = source + jnp.where(index >= s * capacity, 1, 0)
    first = index + source * (height - capacity)
    columns = iota((slots, rows.shape[0]), 1)
    for p in range(PARTS):
        pick = jnp.where(columns == first + p * capacity, 1.0, 0.0).astype(bf16)
        out[:, p * width : (p + 1) * width] = dot(pick, rows).astype(bf16)


def split_body(capacity, count_shares, *refs):
    shares, outs = refs[:count_shares], refs[count_shares:]
    total = shares[0][...].astype(f32)
    for ref in shares[1:]:
        total = total + ref[...].astype(f32)
    rows = stacked(total.astype(bf16))
    height = PARTS * capacity
    slots = shares[0].shape[0]
    count = height * len(outs)
    index = iota((count, 1), 0)
    group = index * 0
    source = index * 0
    for g in range(1, count // capacity):
        group = group + jnp.where(index >= g * capacity, 1, 0)
    for s in range(1, len(outs)):
        source = source + jnp.where(index >= s * height, 1, 0)
    part = group - source * PARTS
    place = part * slots + source * capacity + index - group * capacity
    pick = jnp.where(iota((count, PARTS * slots), 1) == place, 1.0, 0.0).astype(bf16)
    packed = dot(pick, rows).astype(bf16)
    for s, ref in enumerate(outs):
        ref[...] = packed[s * height : (s + 1) * height]


def unpacked(route_column, chunk_refs, experts, capacity):
    tokens = route_column.shape[0]
    place = place_down(route_column, experts, capacity)
    rows = jnp.concatenate([ref[...] for ref in chunk_refs], axis=0)
    columns = iota((tokens, rows.shape[0]), 1)
    parts = []
    for p in range(PARTS):
        pick = jnp.where(columns == place + p * capacity, 1.0, 0.0).astype(bf16)
        parts.append(dot(pick, rows))
    return jnp.concatenate(parts, axis=1)


def front_finish_body(experts, capacity, route_ref, gate_ref, middle_ref, *refs):
    chunks, out = refs[:-1], refs[-1]
    contrib = gate_ref[...] * unpacked(route_ref[...], chunks, experts, capacity)
    out[...] = (middle_ref[...].astype(f32) + contrib).astype(bf16)


def back_finish_body(experts, capacity, route_ref, gain_ref, middle_ref, grad_ref, *refs):
    chunks, out = refs[:-1], refs[-1]
    amount = gain_ref[...] * unpacked(route_ref[...], chunks, experts, capacity)
    middle = middle_ref[...].astype(f32)
    scale = rms_scale(middle)
    cube = scale * scale * scale
    mean = jnp.mean(middle * amount, axis=-1, keepdims=True)
    out[...] = (grad_ref[...].astype(f32) + scale * amount - middle * cube * mean).astype(bf16)


def hidden_body(first_ref, second_ref, gate_ref, up_ref, out_ref):
    rows = jnp.concatenate([first_ref[...], second_ref[...]], axis=0)
    gate_val = dot(rows, gate_ref[...])
    up_val = dot(rows, up_ref[...])
    out_ref[...] = (gate_val / (1.0 + jnp.exp(-gate_val)) * up_val).astype(bf16)


def output_body(own_ref, other_ref, down_ref, far_ref, first_out, second_out):
    half = first_out.shape[0]
    hidden = jnp.concatenate([own_ref[...], other_ref[...]], axis=1)
    step = 4 * LANES
    for n in range(0, down_ref.shape[1], step):
        part = slice(n, n + step)
        weight = jnp.concatenate([down_ref[:, part], far_ref[:, part]], axis=0)
        value = dot(hidden, weight).astype(bf16)
        first_out[:, part] = value[:half]
        second_out[:, part] = value[half:]


def down_back_body(first_ref, second_ref, down_ref, far_ref, own_out, other_out):
    grads = jnp.concatenate([first_ref[...], second_ref[...]], axis=0)
    own_out[...] = dot_last(grads, down_ref[...]).astype(own_out.dtype)
    other_out[...] = dot_last(grads, far_ref[...]).astype(other_out.dtype)


def backward_body(first_ref, second_ref, back_ref, gate_ref, up_ref, first_out, second_out):
    half = first_ref.shape[0]
    rows = jnp.concatenate([first_ref[...], second_ref[...]], axis=0)
    gate_val = dot(rows, gate_ref[...])
    up_val = dot(rows, up_ref[...])
    down_back = back_ref[...].astype(f32)
    sigmoid_val = 1.0 / (1.0 + jnp.exp(-gate_val))
    slope_val = sigmoid_val * (1.0 + gate_val * (1.0 - sigmoid_val))
    gate_grad = (down_back * up_val * slope_val).astype(bf16)
    up_grad = (down_back * gate_val * sigmoid_val).astype(bf16)
    step = 4 * LANES
    for n in range(0, gate_ref.shape[0], step):
        value = dot_last(gate_grad, gate_ref[n : n + step])
        value = (value + dot_last(up_grad, up_ref[n : n + step])).astype(bf16)
        first_out[:, n : n + step] = value[:half]
        second_out[:, n : n + step] = value[half:]


def attend_body(
    experts,
    capacity,
    chosen_ref,
    index_ref,
    base_ref,
    route_ref,
    gain_ref,
    input_ref,
    query_ref,
    kv0,
    kv1,
    kv2,
    middle_ref,
    *refs,
):
    outs, (kv_all, kv_now, stack, attended) = refs[:experts], refs[experts:]
    tokens, width = query_ref.shape
    lead = 0
    for ref in (kv0, kv1, kv2):
        kv_all[lead : lead + ref.shape[0], : ref.shape[1]] = ref[...]
        lead += ref.shape[0]
    attended[...] = jnp.zeros_like(attended)
    heads_each = HEADS // KV_HEADS
    period = 8
    window = 2 * LANES
    keys = SEL * BLK
    lane = iota((keys, LANES), 1)
    batch = 4
    scale = HEAD_DIM**-0.5

    def one_block(block, _):
        top = pl.multiple_of(block * BLK, BLK)
        position = (base_ref[0] + block) * BLK + (iota((batch * BLK, keys), 0) & (BLK - 1))
        for head in range(KV_HEADS):
            key_pos = iota((1, keys), 1)
            shift = key_pos * 0
            for s in range(SEL):
                at = (block * KV_HEADS + head) * SEL + s
                start = pl.multiple_of(index_ref[at] * BLK, BLK)
                kv_now[s * BLK : (s + 1) * BLK, :] = kv_all[pl.ds(start, BLK), :].astype(f32)
                inside = (key_pos >= s * BLK) & (key_pos < (s + 1) * BLK)
                shift = jnp.where(inside, (chosen_ref[at] - s) * BLK, shift)
            allowed = key_pos + shift <= position
            sides = []
            for side in range(2):
                lead = (side * KV_HEADS + head) * HEAD_DIM
                tile = min(lead // LANES, 2)
                piece = kv_now[:, tile * LANES : tile * LANES + window]
                offset = lead - tile * LANES
                if offset:
                    piece = pltpu.roll(piece, window - offset, 1)
                sides.append(jnp.where(lane < HEAD_DIM, piece[:, :LANES], 0.0).astype(bf16))
            key_rows, value_rows = sides
            spots = []
            for j in range(heads_each):
                c = j % period
                tile = min(c * HEAD_DIM // LANES, period - 3)
                offset = c * HEAD_DIM - tile * LANES
                tile = tile + (j // period) * (period - 1) + head * heads_each * HEAD_DIM // LANES
                spots.append((tile * LANES, offset))
            for j, (lead, offset) in enumerate(spots):
                piece = query_ref[pl.ds(top, BLK), lead : lead + window].astype(f32)
                if offset:
                    piece = pltpu.roll(piece, window - offset, 1)
                stack[j * BLK : (j + 1) * BLK, :] = piece[:, :LANES].astype(bf16)
            for b in range(0, heads_each, batch):
                scores = dot_last(stack[b * BLK : (b + batch) * BLK, :], key_rows) * scale
                scores = jnp.where(allowed, scores, negative_large)
                exp_scores = jnp.exp(scores - jnp.max(scores, axis=-1, keepdims=True))
                total = jnp.sum(exp_scores, axis=-1, keepdims=True)
                mixed = dot((exp_scores / total).astype(bf16), value_rows)
                for i in range(batch):
                    lead, offset = spots[b + i]
                    piece = mixed[i * BLK : (i + 1) * BLK]
                    piece = jnp.concatenate([piece, jnp.zeros_like(piece)], axis=1)
                    if offset:
                        piece = pltpu.roll(piece, offset, 1)
                    spot = (pl.ds(top, BLK), slice(lead, lead + window))
                    attended[spot] = attended[spot] + piece
        return 0

    lax.fori_loop(0, tokens // BLK, one_block, 0)
    middle = (input_ref[...].astype(f32) + attended[...]).astype(bf16)
    middle_ref[...] = middle
    middle = middle.astype(f32)
    normed = (middle * rms_scale(middle) * gain_ref[...]).astype(bf16)
    pack_into(normed, place_across(route_ref[...], experts, capacity), outs, capacity)


def after(arrays, others):
    count = len(arrays)
    return list(lax.optimization_barrier(tuple(arrays) + tuple(others))[:count])


def shape_of(rows, columns, kind=bf16):
    return jax.ShapeDtypeStruct((rows, columns), kind)


def shards(
    front_input,
    queries,
    keys_values,
    selected_blocks,
    front_route,
    front_gate,
    back_middle,
    back_grad,
    back_route,
    back_gate,
    norm_gain,
    gate_slice,
    up_slice,
    down_slice,
):
    tokens, width = front_input.shape[1:]
    length = lax.axis_size("expert")
    experts = length // GROUP
    average = tokens // experts
    capacity = average + max(1, average // 8)
    slots = experts * capacity
    hidden_width = gate_slice.shape[3]
    w_gate, w_up, w_down = gate_slice[0, 0], up_slice[0, 0], down_slice[0, 0]
    me = lax.axis_index("expert")
    group = me // GROUP
    chunk = shape_of(PARTS * capacity, width // PARTS)
    piece = shape_of(slots, width)
    whole = shape_of(tokens, width)

    column = [keys_values[0]]
    for back in range(1, experts):
        pairs = [(i, i + back * GROUP) for i in range(length - back * GROUP)]
        column.append(lax.ppermute(keys_values[0], "expert", pairs))
    front_from = lax.rem(front_route[0] - group + experts, experts)
    back_from = lax.rem(back_route[0] - group + experts, experts)
    front_row, back_row = front_from.reshape(1, tokens), back_from.reshape(1, tokens)

    pack_flops = 4 * slots * PARTS * tokens * width
    packed = call(
        functools.partial(back_pack_body, experts, capacity),
        [chunk] * (2 * experts),
        (back_row, back_gate[0], norm_gain, back_middle[0], back_grad[0]),
        flops=2 * pack_flops,
    )
    column = after(column, [packed[0]])
    column = jnp.concatenate(column, axis=0)
    other_chip = swapped(column, 2)
    packed = after(packed, [column])
    down_other = swapped(w_down, 2)
    downs = (w_down, down_other)

    front_small = jnp.concatenate([front_from.astype(f32), front_gate[0]], axis=0).reshape(1, -1)
    back_small = jnp.concatenate([back_from.astype(f32).reshape(1, -1), norm_gain], axis=1)

    def sent(chunks):
        return [chunks[0]] + [turned(chunks[k], k) for k in range(1, experts)]

    def joined(chunks):
        return call(functools.partial(join_body, capacity), piece, chunks, flops=pack_flops)

    def pieces_of(rows):
        other = swapped(rows, 2)
        return [rows, swapped(rows, 1), other, swapped(other, 1)]

    def split(parts):
        return call(
            functools.partial(split_body, capacity, len(parts)),
            [chunk] * experts,
            parts,
            flops=pack_flops,
        )

    def sent_back(chunks, by):
        return [passed_along(chunks[k], by, k) for k in range(experts)]

    row_chunks, grad_chunks = packed[:experts], packed[experts:]
    first = 1 + 2 * (experts - 1) // 3
    for k in range(1, first):
        row_chunks[k] = turned(row_chunks[k], k)
    arrived = row_chunks[1:first]
    there_back_middle = passed_along(after([back_middle[0]], [packed[0]])[0], -1)
    chip = jnp.concatenate([column, other_chip], axis=0)
    kv = [column, other_chip, swapped(after([chip], arrived + [there_back_middle])[0], 1)]
    for k in range(first, experts):
        row_chunks[k] = turned(after([row_chunks[k]], arrived)[0], k)
    beside = range(1, 2)
    for k in beside:
        grad_chunks[k] = turned(after([grad_chunks[k]], arrived)[0], k)
    there_back_grad = passed_along(after([back_grad[0]], [there_back_middle])[0], -1)

    per_device = tokens // BLK
    chosen = selected_blocks[0].reshape(-1)
    owner = chosen // per_device
    place = (owner % GROUP) ^ (me % GROUP)
    place = (place % 2) * 2 + place // 2
    index = (place * experts + group - owner // GROUP) * per_device + chosen % per_device
    index = jnp.clip(index, 0, length * per_device - 1)
    base = (me * per_device).astype(jnp.int32).reshape(1)
    result = call(
        functools.partial(attend_body, experts, capacity),
        [whole] + [chunk] * experts,
        (chosen, index, base, front_row, norm_gain, front_input[0], queries[0], *kv),
        scratch=[
            pltpu.VMEM((length * tokens, 4 * LANES), bf16),
            pltpu.VMEM((SEL * BLK, 4 * LANES), f32),
            pltpu.VMEM((HEADS // KV_HEADS * BLK, LANES), bf16),
            pltpu.VMEM((tokens, width), f32),
        ],
        flops=pack_flops + 4 * tokens * HEADS * SEL * BLK * LANES,
        smem=3,
        vmem=VMEM_BYTES + 2 * length * tokens * 4 * LANES * 2,
    )
    middle, front_chunks = result[0], result[1:]
    ready = row_chunks + [grad_chunks[k] for k in beside]
    front_chunks = sent(after(front_chunks, ready))
    back_rows = joined(after(ready, [middle, there_back_grad])[:experts])
    back_pieces = pieces_of(after([back_rows], [down_other])[0])
    there_middle = passed_along(after([middle], [back_rows])[0], 1)
    for k in range(1, experts):
        if k not in beside:
            grad_chunks[k] = turned(after([grad_chunks[k]], front_chunks)[0], k)
    front_near = joined(after(front_chunks, [there_middle, back_pieces[2]]))
    front_other = swapped(front_near, 2)

    front_small, back_small = after([front_small, back_small], [front_near])
    there_small = passed_along(front_small, 1)
    there_back_small = passed_along(back_small, -1)
    there_front_from = there_small[0, :tokens].astype(jnp.int32).reshape(tokens, 1)
    there_front_gate = there_small[0, tokens:].reshape(tokens, 1)
    there_back_from = there_back_small[0, :tokens].astype(jnp.int32).reshape(tokens, 1)
    there_gain = there_back_small[:, tokens:]
    grad_near = joined(after(grad_chunks, [there_small, there_back_small]))
    grad_near = [grad_near, swapped(grad_near, 1)]

    work = 2 * 2 * slots * width * hidden_width
    pair = 2 * slots

    def hidden(rows):
        return call(
            hidden_body, shape_of(pair, hidden_width), (*rows, w_gate, w_up), flops=2 * work
        )

    def backward(rows, grads):
        return call(backward_body, [piece, piece], (*rows, grads, w_gate, w_up), flops=4 * work)

    down_back, other_back = call(
        down_back_body,
        [shape_of(pair, hidden_width, f32), shape_of(pair, hidden_width)],
        (*grad_near, *downs),
        flops=2 * work,
    )
    (front_other,) = after([front_other], [other_back])
    front_pieces = [front_near, swapped(front_near, 1), front_other, swapped(front_other, 1)]
    hidden_near = hidden(front_pieces[:2])
    hidden_far = hidden(front_pieces[2:])
    hidden_other = swapped(hidden_far, 2)
    far_back = swapped(other_back, 2)

    back_near = backward(back_pieces[:2], down_back)
    back_far = backward(back_pieces[2:], far_back)
    chip = back_far[0].astype(f32) + swapped(back_far[1], 1).astype(f32)
    back_shares = (back_near[0], swapped(back_near[1], 1), swapped(chip.astype(bf16), 2))

    front_own, front_core = call(
        output_body, [piece, piece], (hidden_near, hidden_other, *downs), flops=2 * work
    )
    front_chunks = split((front_own, swapped(front_core, 1)))
    front_return = sent_back(front_chunks, 1)

    back_chunks = split(after(back_shares, front_chunks))
    back_return = sent_back(back_chunks, -1)

    front_return = after(front_return, back_chunks)
    front_output = call(
        functools.partial(front_finish_body, experts, capacity),
        whole,
        (there_front_from, there_front_gate, there_middle, *front_return),
        flops=pack_flops,
    )
    back_return = after(back_return, [front_output])
    back_output = call(
        functools.partial(back_finish_body, experts, capacity),
        whole,
        (there_back_from, there_gain, there_back_middle, there_back_grad, *back_return),
        flops=pack_flops,
    )
    return (front_output[None], back_output[None])


def solution(mesh):
    placed = (
        P("section", "expert", None),
        P("section", "expert", None),
        P("section", "expert", None),
        P("section", "expert", None, None),
        P("section", "expert", None),
        P("section", "expert", None),
        P("section", "expert", None),
        P("section", "expert", None),
        P("section", "expert", None),
        P("section", "expert", None),
        P("section", None),
        P("section", "expert", None, None),
        P("section", "expert", None, None),
        P("section", "expert", None, None),
    )
    return jax.shard_map(
        shards,
        mesh=mesh,
        in_specs=placed,
        out_specs=(P("section", "expert", None), P("section", "expert", None)),
        check_vma=False,
    )
```

```python
import functools

import jax
import jax.numpy as jnp
from jax import lax
from jax.experimental import pallas as pl
from jax.experimental.pallas import tpu as pltpu
from jax.sharding import PartitionSpec as P

GROUP = 4
HEADS = 32
HEAD_DIM = 112
KV_HEADS = 2
BLK = 64
SEL = 4
PARTS = 4
LANES = 128
VMEM_BYTES = 28 * 1024 * 1024

epsilon = 1e-06
negative_large = -1e30
bf16 = jnp.bfloat16
f32 = jnp.float32


def passed_along(array, by, back=0):
    sections, length = lax.axis_size("section"), lax.axis_size("expert")
    pairs = [
        (s * length + i, (s + by) % sections * length + (i - back * GROUP) % length)
        for s in range(sections)
        for i in range(length)
    ]
    return lax.ppermute(array, ("section", "expert"), pairs)


def swapped(array, bit):
    return lax.ppermute(array, "expert", [(i, i ^ bit) for i in range(lax.axis_size("expert"))])


def turned(array, by):
    length = lax.axis_size("expert")
    return lax.ppermute(
        array, "expert", [(i, (i + by * GROUP) % length) for i in range(length)]
    )


def call(body, outs, args, scratch=(), flops=0, smem=0, vmem=VMEM_BYTES):
    specs = [
        pl.BlockSpec(memory_space=pltpu.SMEM if i < smem else pltpu.VMEM)
        for i in range(len(args))
    ]
    many = isinstance(outs, list)
    shapes = outs if many else [outs]
    moved_bytes = sum(a.size * a.dtype.itemsize for a in list(args) + shapes)
    result = pl.pallas_call(
        body,
        out_shape=shapes,
        in_specs=specs,
        out_specs=[pl.BlockSpec(memory_space=pltpu.VMEM) for _ in shapes],
        scratch_shapes=list(scratch),
        compiler_params=pltpu.CompilerParams(vmem_limit_bytes=vmem),
        cost_estimate=pl.CostEstimate(
            flops=int(flops), bytes_accessed=int(moved_bytes), transcendentals=0
        ),
    )(*args)
    return list(result) if many else result[0]


def dot(a, b):
    return jnp.dot(a, b, preferred_element_type=f32)


def dot_last(a, b):
    return lax.dot_general(a, b, (((1,), (1,)), ((), ())), preferred_element_type=f32)


def rms_scale(rows):
    return lax.rsqrt(jnp.mean(rows * rows, axis=-1, keepdims=True) + epsilon)


def iota(shape, dim):
    return lax.broadcasted_iota(jnp.int32, shape, dim)


def stacked(rows):
    width = rows.shape[1] // PARTS
    return jnp.concatenate([rows[:, p * width : (p + 1) * width] for p in range(PARTS)], axis=0)


def place_across(route_row, experts, capacity):
    tokens = route_row.shape[1]
    names = iota((max(8, experts), tokens), 0)
    onehot = jnp.where(names == route_row, 1.0, 0.0)
    earlier = jnp.where(iota((tokens, tokens), 0) < iota((tokens, tokens), 1), 1.0, 0.0)
    before = dot(onehot.astype(bf16), earlier.astype(bf16))
    place = onehot * (before + (names * (PARTS * capacity)).astype(f32))
    return jnp.sum(place, axis=0, keepdims=True).astype(jnp.int32)


def place_down(route_column, experts, capacity):
    tokens = route_column.shape[0]
    names = iota((tokens, LANES), 1)
    onehot = jnp.where(names == route_column, 1.0, 0.0)
    earlier = jnp.where(iota((tokens, tokens), 1) < iota((tokens, tokens), 0), 1.0, 0.0)
    before = dot(earlier.astype(bf16), onehot.astype(bf16))
    place = onehot * (before + (names * (PARTS * capacity)).astype(f32))
    return jnp.sum(place, axis=1, keepdims=True).astype(jnp.int32)


def pack_into(rows, place, out_refs, capacity):
    tokens = rows.shape[0]
    height = PARTS * capacity
    total = height * len(out_refs)
    places = jnp.concatenate([place + p * capacity for p in range(PARTS)], axis=1)
    pick = jnp.where(iota((total, PARTS * tokens), 0) == places, 1.0, 0.0).astype(bf16)
    packed = dot(pick, stacked(rows)).astype(bf16)
    for e, ref in enumerate(out_refs):
        ref[...] = packed[e * height : (e + 1) * height]


def back_pack_body(experts, capacity, route_ref, gate_ref, gain_ref, middle_ref, grad_ref, *outs):
    place = place_across(route_ref[...], experts, capacity)
    middle = middle_ref[...].astype(f32)
    normed = (middle * rms_scale(middle) * gain_ref[...]).astype(bf16)
    pack_into(normed, place, outs[:experts], capacity)
    scaled = (gate_ref[...] * grad_ref[...].astype(f32)).astype(bf16)
    pack_into(scaled, place, outs[experts:], capacity)


def join_body(capacity, *refs):
    chunks, out = refs[:-1], refs[-1]
    sources = len(chunks)
    height = PARTS * capacity
    rows = jnp.concatenate([ref[...] for ref in chunks], axis=0)
    slots = sources * capacity
    width = rows.shape[1]
    index = iota((slots, 1), 0)
    source = index * 0
    for s in range(1, sources):
        source = source + jnp.where(index >= s * capacity, 1, 0)
    first = index + source * (height - capacity)
    columns = iota((slots, rows.shape[0]), 1)
    for p in range(PARTS):
        pick = jnp.where(columns == first + p * capacity, 1.0, 0.0).astype(bf16)
        out[:, p * width : (p + 1) * width] = dot(pick, rows).astype(bf16)


def split_body(capacity, count_shares, *refs):
    shares, outs = refs[:count_shares], refs[count_shares:]
    total = shares[0][...].astype(f32)
    for ref in shares[1:]:
        total = total + ref[...].astype(f32)
    rows = stacked(total.astype(bf16))
    height = PARTS * capacity
    slots = shares[0].shape[0]
    count = height * len(outs)
    index = iota((count, 1), 0)
    group = index * 0
    source = index * 0
    for g in range(1, count // capacity):
        group = group + jnp.where(index >= g * capacity, 1, 0)
    for s in range(1, len(outs)):
        source = source + jnp.where(index >= s * height, 1, 0)
    part = group - source * PARTS
    place = part * slots + source * capacity + index - group * capacity
    pick = jnp.where(iota((count, PARTS * slots), 1) == place, 1.0, 0.0).astype(bf16)
    packed = dot(pick, rows).astype(bf16)
    for s, ref in enumerate(outs):
        ref[...] = packed[s * height : (s + 1) * height]


def unpacked(route_column, chunk_refs, experts, capacity):
    tokens = route_column.shape[0]
    place = place_down(route_column, experts, capacity)
    rows = jnp.concatenate([ref[...] for ref in chunk_refs], axis=0)
    columns = iota((tokens, rows.shape[0]), 1)
    parts = []
    for p in range(PARTS):
        pick = jnp.where(columns == place + p * capacity, 1.0, 0.0).astype(bf16)
        parts.append(dot(pick, rows))
    return jnp.concatenate(parts, axis=1)


def front_finish_body(experts, capacity, route_ref, gate_ref, middle_ref, *refs):
    chunks, out = refs[:-1], refs[-1]
    contrib = gate_ref[...] * unpacked(route_ref[...], chunks, experts, capacity)
    out[...] = (middle_ref[...].astype(f32) + contrib).astype(bf16)


def back_finish_body(experts, capacity, route_ref, gain_ref, middle_ref, grad_ref, *refs):
    chunks, out = refs[:-1], refs[-1]
    amount = gain_ref[...] * unpacked(route_ref[...], chunks, experts, capacity)
    middle = middle_ref[...].astype(f32)
    scale = rms_scale(middle)
    cube = scale * scale * scale
    mean = jnp.mean(middle * amount, axis=-1, keepdims=True)
    out[...] = (grad_ref[...].astype(f32) + scale * amount - middle * cube * mean).astype(bf16)


def hidden_body(first_ref, second_ref, gate_ref, up_ref, out_ref):
    rows = jnp.concatenate([first_ref[...], second_ref[...]], axis=0)
    gate_val = dot(rows, gate_ref[...])
    up_val = dot(rows, up_ref[...])
    out_ref[...] = (gate_val / (1.0 + jnp.exp(-gate_val)) * up_val).astype(bf16)


def output_body(own_ref, other_ref, down_ref, top_ref, low_ref, first_out, second_out):
    half = first_out.shape[0]
    hidden = jnp.concatenate([own_ref[...], other_ref[...]], axis=1)
    step = 4 * LANES
    for n in range(0, down_ref.shape[1], step):
        part = slice(n, n + step)
        weight = jnp.concatenate([down_ref[:, part], top_ref[:, part], low_ref[:, part]], axis=0)
        value = dot(hidden, weight).astype(bf16)
        first_out[:, part] = value[:half]
        second_out[:, part] = value[half:]


def down_back_body(first_ref, second_ref, down_ref, top_ref, low_ref, own_out, other_out):
    grads = jnp.concatenate([first_ref[...], second_ref[...]], axis=0)
    own_out[...] = dot_last(grads, down_ref[...]).astype(own_out.dtype)
    far = jnp.concatenate([top_ref[...], low_ref[...]], axis=0)
    other_out[...] = dot_last(grads, far).astype(other_out.dtype)


def backward_body(first_ref, second_ref, back_ref, gate_ref, up_ref, first_out, second_out):
    half = first_ref.shape[0]
    rows = jnp.concatenate([first_ref[...], second_ref[...]], axis=0)
    gate_val = dot(rows, gate_ref[...])
    up_val = dot(rows, up_ref[...])
    down_back = back_ref[...].astype(f32)
    sigmoid_val = 1.0 / (1.0 + jnp.exp(-gate_val))
    slope_val = sigmoid_val * (1.0 + gate_val * (1.0 - sigmoid_val))
    gate_grad = (down_back * up_val * slope_val).astype(bf16)
    up_grad = (down_back * gate_val * sigmoid_val).astype(bf16)
    step = 4 * LANES
    for n in range(0, gate_ref.shape[0], step):
        value = dot_last(gate_grad, gate_ref[n : n + step])
        value = (value + dot_last(up_grad, up_ref[n : n + step])).astype(bf16)
        first_out[:, n : n + step] = value[:half]
        second_out[:, n : n + step] = value[half:]


def attend_body(
    experts,
    capacity,
    chosen_ref,
    index_ref,
    base_ref,
    route_ref,
    gain_ref,
    input_ref,
    query_ref,
    kv0,
    kv1,
    kv2,
    kv3,
    middle_ref,
    *refs,
):
    outs, (kv_all, kv_now, stack, attended) = refs[:experts], refs[experts:]
    tokens, width = query_ref.shape
    lead = 0
    for ref in (kv0, kv1, kv2, kv3):
        kv_all[lead : lead + ref.shape[0], : ref.shape[1]] = ref[...]
        lead += ref.shape[0]
    attended[...] = jnp.zeros_like(attended)
    heads_each = HEADS // KV_HEADS
    period = 8
    window = 2 * LANES
    keys = SEL * BLK
    lane = iota((keys, LANES), 1)
    batch = 4
    scale = HEAD_DIM**-0.5

    def one_block(block, _):
        top = pl.multiple_of(block * BLK, BLK)
        position = (base_ref[0] + block) * BLK + (iota((batch * BLK, keys), 0) & (BLK - 1))
        for head in range(KV_HEADS):
            key_pos = iota((1, keys), 1)
            shift = key_pos * 0
            for s in range(SEL):
                at = (block * KV_HEADS + head) * SEL + s
                start = pl.multiple_of(index_ref[at] * BLK, BLK)
                kv_now[s * BLK : (s + 1) * BLK, :] = kv_all[pl.ds(start, BLK), :].astype(f32)
                inside = (key_pos >= s * BLK) & (key_pos < (s + 1) * BLK)
                shift = jnp.where(inside, (chosen_ref[at] - s) * BLK, shift)
            allowed = key_pos + shift <= position
            sides = []
            for side in range(2):
                lead = (side * KV_HEADS + head) * HEAD_DIM
                tile = min(lead // LANES, 2)
                piece = kv_now[:, tile * LANES : tile * LANES + window]
                offset = lead - tile * LANES
                if offset:
                    piece = pltpu.roll(piece, window - offset, 1)
                sides.append(jnp.where(lane < HEAD_DIM, piece[:, :LANES], 0.0).astype(bf16))
            key_rows, value_rows = sides
            spots = []
            for j in range(heads_each):
                c = j % period
                tile = min(c * HEAD_DIM // LANES, period - 3)
                offset = c * HEAD_DIM - tile * LANES
                tile = tile + (j // period) * (period - 1) + head * heads_each * HEAD_DIM // LANES
                spots.append((tile * LANES, offset))
            for j, (lead, offset) in enumerate(spots):
                piece = query_ref[pl.ds(top, BLK), lead : lead + window].astype(f32)
                if offset:
                    piece = pltpu.roll(piece, window - offset, 1)
                stack[j * BLK : (j + 1) * BLK, :] = piece[:, :LANES].astype(bf16)
            for b in range(0, heads_each, batch):
                scores = dot_last(stack[b * BLK : (b + batch) * BLK, :], key_rows) * scale
                scores = jnp.where(allowed, scores, negative_large)
                exp_scores = jnp.exp(scores - jnp.max(scores, axis=-1, keepdims=True))
                total = jnp.sum(exp_scores, axis=-1, keepdims=True)
                mixed = dot((exp_scores / total).astype(bf16), value_rows)
                for i in range(batch):
                    lead, offset = spots[b + i]
                    piece = mixed[i * BLK : (i + 1) * BLK]
                    piece = jnp.concatenate([piece, jnp.zeros_like(piece)], axis=1)
                    if offset:
                        piece = pltpu.roll(piece, offset, 1)
                    spot = (pl.ds(top, BLK), slice(lead, lead + window))
                    attended[spot] = attended[spot] + piece
        return 0

    lax.fori_loop(0, tokens // BLK, one_block, 0)
    middle = (input_ref[...].astype(f32) + attended[...]).astype(bf16)
    middle_ref[...] = middle
    middle = middle.astype(f32)
    normed = (middle * rms_scale(middle) * gain_ref[...]).astype(bf16)
    pack_into(normed, place_across(route_ref[...], experts, capacity), outs, capacity)


def after(arrays, others):
    count = len(arrays)
    return list(lax.optimization_barrier(tuple(arrays) + tuple(others))[:count])


def shape_of(rows, columns, kind=bf16):
    return jax.ShapeDtypeStruct((rows, columns), kind)


def shards(
    front_input,
    queries,
    keys_values,
    selected_blocks,
    front_route,
    front_gate,
    back_middle,
    back_grad,
    back_route,
    back_gate,
    norm_gain,
    gate_slice,
    up_slice,
    down_slice,
):
    tokens, width = front_input.shape[1:]
    length = lax.axis_size("expert")
    experts = length // GROUP
    average = tokens // experts
    capacity = average + max(1, average // 8)
    slots = experts * capacity
    hidden_width = gate_slice.shape[3]
    w_gate, w_up, w_down = gate_slice[0, 0], up_slice[0, 0], down_slice[0, 0]
    me = lax.axis_index("expert")
    group = me // GROUP
    chunk = shape_of(PARTS * capacity, width // PARTS)
    piece = shape_of(slots, width)
    whole = shape_of(tokens, width)

    column = [keys_values[0]]
    for back in range(1, experts):
        pairs = [(i, i + back * GROUP) for i in range(length - back * GROUP)]
        column.append(lax.ppermute(keys_values[0], "expert", pairs))
    front_from = lax.rem(front_route[0] - group + experts, experts)
    back_from = lax.rem(back_route[0] - group + experts, experts)
    front_row, back_row = front_from.reshape(1, tokens), back_from.reshape(1, tokens)

    pack_flops = 4 * slots * PARTS * tokens * width
    packed = call(
        functools.partial(back_pack_body, experts, capacity),
        [chunk] * (2 * experts),
        (back_row, back_gate[0], norm_gain, back_middle[0], back_grad[0]),
        flops=2 * pack_flops,
    )
    column = after(column, [packed[0]])
    column = jnp.concatenate(column, axis=0)
    other_chip = swapped(column, 2)
    packed = after(packed, [column])

    front_small = jnp.concatenate([front_from.astype(f32), front_gate[0]], axis=0).reshape(1, -1)
    back_small = jnp.concatenate([back_from.astype(f32).reshape(1, -1), norm_gain], axis=1)

    def sent(chunks):
        return [chunks[0]] + [turned(chunks[k], k) for k in range(1, experts)]

    def joined(chunks):
        return call(functools.partial(join_body, capacity), piece, chunks, flops=pack_flops)

    def pieces_of(rows):
        other = swapped(rows, 2)
        return [rows, swapped(rows, 1), other, swapped(other, 1)]

    def split(parts):
        return call(
            functools.partial(split_body, capacity, len(parts)),
            [chunk] * experts,
            parts,
            flops=pack_flops,
        )

    def sent_back(chunks, by):
        return [passed_along(chunks[k], by, k) for k in range(experts)]

    row_chunks, grad_chunks = packed[:experts], packed[experts:]
    first = 1 + 2 * (experts - 1) // 3
    for k in range(1, first):
        row_chunks[k] = turned(row_chunks[k], k)
    arrived = row_chunks[1:first]
    cut = hidden_width * 5 // 8
    (down_top,) = after([w_down[:cut]], arrived[:1])
    down_top = swapped(down_top, 2)
    there_back_middle = passed_along(after([back_middle[0]], arrived)[0], -1)
    far = swapped(after([other_chip], arrived)[0], 1)
    kv = [column, other_chip, swapped(column, 1), far]
    for k in range(first, experts):
        row_chunks[k] = turned(after([row_chunks[k]], arrived)[0], k)
    beside = range(1, 2)
    for k in beside:
        grad_chunks[k] = turned(after([grad_chunks[k]], arrived)[0], k)
    there_back_grad = passed_along(after([back_grad[0]], [there_back_middle])[0], -1)

    per_device = tokens // BLK
    chosen = selected_blocks[0].reshape(-1)
    owner = chosen // per_device
    place = (owner % GROUP) ^ (me % GROUP)
    place = (place % 2) * 2 + place // 2
    index = (place * experts + group - owner // GROUP) * per_device + chosen % per_device
    index = jnp.clip(index, 0, length * per_device - 1)
    base = (me * per_device).astype(jnp.int32).reshape(1)
    result = call(
        functools.partial(attend_body, experts, capacity),
        [whole] + [chunk] * experts,
        (chosen, index, base, front_row, norm_gain, front_input[0], queries[0], *kv),
        scratch=[
            pltpu.VMEM((length * tokens, 4 * LANES), bf16),
            pltpu.VMEM((SEL * BLK, 4 * LANES), f32),
            pltpu.VMEM((HEADS // KV_HEADS * BLK, LANES), bf16),
            pltpu.VMEM((tokens, width), f32),
        ],
        flops=pack_flops + 4 * tokens * HEADS * SEL * BLK * LANES,
        smem=3,
        vmem=VMEM_BYTES + 2 * length * tokens * 4 * LANES * 2,
    )
    middle, front_chunks = result[0], result[1:]
    ready = row_chunks + [grad_chunks[k] for k in beside]
    front_chunks = sent(after(front_chunks, ready))
    back_rows = joined(after(ready, [middle, there_back_middle])[:experts])
    back_pieces = pieces_of(after([back_rows], [down_top])[0])
    down_low = swapped(after([w_down[cut:]], [back_pieces[2]])[0], 2)
    downs = (w_down, down_top, down_low)
    for k in range(1, experts):
        if k not in beside:
            grad_chunks[k] = turned(after([grad_chunks[k]], front_chunks)[0], k)
    front_near = joined(after(front_chunks, [there_back_grad, back_pieces[2]]))
    there_middle = passed_along(after([middle], [front_near])[0], 1)
    front_other = swapped(after([front_near], [down_low])[0], 2)

    front_small, back_small = after([front_small, back_small], [front_near])
    there_small = passed_along(front_small, 1)
    there_back_small = passed_along(back_small, -1)
    there_front_from = there_small[0, :tokens].astype(jnp.int32).reshape(tokens, 1)
    there_front_gate = there_small[0, tokens:].reshape(tokens, 1)
    there_back_from = there_back_small[0, :tokens].astype(jnp.int32).reshape(tokens, 1)
    there_gain = there_back_small[:, tokens:]
    grad_near = joined(after(grad_chunks, [there_small, there_back_small, there_middle]))
    grad_near = [grad_near, swapped(grad_near, 1)]

    work = 2 * 2 * slots * width * hidden_width
    pair = 2 * slots

    def hidden(rows):
        return call(
            hidden_body, shape_of(pair, hidden_width), (*rows, w_gate, w_up), flops=2 * work
        )

    def backward(rows, grads):
        return call(backward_body, [piece, piece], (*rows, grads, w_gate, w_up), flops=4 * work)

    down_back, other_back = call(
        down_back_body,
        [shape_of(pair, hidden_width, f32), shape_of(pair, hidden_width)],
        (*grad_near, *downs),
        flops=2 * work,
    )
    (front_other,) = after([front_other], [other_back])
    front_pieces = [front_near, swapped(front_near, 1), front_other, swapped(front_other, 1)]
    hidden_near = hidden(front_pieces[:2])
    hidden_far = hidden(front_pieces[2:])
    hidden_other = swapped(hidden_far, 2)
    far_back = swapped(other_back, 2)

    back_near = backward(back_pieces[:2], down_back)
    back_far = backward(back_pieces[2:], far_back)
    chip = back_far[0].astype(f32) + swapped(back_far[1], 1).astype(f32)
    back_shares = (back_near[0], swapped(back_near[1], 1), swapped(chip.astype(bf16), 2))

    front_own, front_core = call(
        output_body, [piece, piece], (hidden_near, hidden_other, *downs), flops=2 * work
    )
    front_chunks = split((front_own, swapped(front_core, 1)))
    front_return = sent_back(front_chunks, 1)

    back_chunks = split(after(back_shares, front_chunks))
    back_return = sent_back(back_chunks, -1)

    front_return = after(front_return, back_chunks)
    front_output = call(
        functools.partial(front_finish_body, experts, capacity),
        whole,
        (there_front_from, there_front_gate, there_middle, *front_return),
        flops=pack_flops,
    )
    back_return = after(back_return, [front_output])
    back_output = call(
        functools.partial(back_finish_body, experts, capacity),
        whole,
        (there_back_from, there_gain, there_back_middle, there_back_grad, *back_return),
        flops=pack_flops,
    )
    return (front_output[None], back_output[None])


def solution(mesh):
    placed = (
        P("section", "expert", None),
        P("section", "expert", None),
        P("section", "expert", None),
        P("section", "expert", None, None),
        P("section", "expert", None),
        P("section", "expert", None),
        P("section", "expert", None),
        P("section", "expert", None),
        P("section", "expert", None),
        P("section", "expert", None),
        P("section", None),
        P("section", "expert", None, None),
        P("section", "expert", None, None),
        P("section", "expert", None, None),
    )
    return jax.shard_map(
        shards,
        mesh=mesh,
        in_specs=placed,
        out_specs=(P("section", "expert", None), P("section", "expert", None)),
        check_vma=False,
    )
```

```python
import functools

import jax
import jax.numpy as jnp
from jax import lax
from jax.experimental import pallas as pl
from jax.experimental.pallas import tpu as pltpu
from jax.sharding import PartitionSpec as P

GROUP = 4
HEADS = 32
HEAD_DIM = 112
KV_HEADS = 2
BLK = 64
SEL = 4
PARTS = 4
LANES = 128
VMEM_BYTES = 28 * 1024 * 1024

epsilon = 1e-06
negative_large = -1e30
bf16 = jnp.bfloat16
f32 = jnp.float32


def passed_along(array, by, back=0):
    sections, length = lax.axis_size("section"), lax.axis_size("expert")
    pairs = [
        (s * length + i, (s + by) % sections * length + (i - back * GROUP) % length)
        for s in range(sections)
        for i in range(length)
    ]
    return lax.ppermute(array, ("section", "expert"), pairs)


def swapped(array, bit):
    return lax.ppermute(array, "expert", [(i, i ^ bit) for i in range(lax.axis_size("expert"))])


def turned(array, by):
    length = lax.axis_size("expert")
    return lax.ppermute(
        array, "expert", [(i, (i + by * GROUP) % length) for i in range(length)]
    )


def call(body, outs, args, scratch=(), flops=0, smem=0, vmem=VMEM_BYTES):
    specs = [
        pl.BlockSpec(memory_space=pltpu.SMEM if i < smem else pltpu.VMEM)
        for i in range(len(args))
    ]
    many = isinstance(outs, list)
    shapes = outs if many else [outs]
    result = pl.pallas_call(
        body,
        out_shape=shapes,
        in_specs=specs,
        out_specs=[pl.BlockSpec(memory_space=pltpu.VMEM) for _ in shapes],
        scratch_shapes=list(scratch),
        compiler_params=pltpu.CompilerParams(vmem_limit_bytes=vmem),
        cost_estimate=pl.CostEstimate(flops=1, bytes_accessed=1, transcendentals=0),
    )(*args)
    return list(result) if many else result[0]


def dot(a, b):
    return jnp.dot(a, b, preferred_element_type=f32)


def dot_last(a, b):
    return lax.dot_general(a, b, (((1,), (1,)), ((), ())), preferred_element_type=f32)


def rms_scale(rows):
    return lax.rsqrt(jnp.mean(rows * rows, axis=-1, keepdims=True) + epsilon)


def iota(shape, dim):
    return lax.broadcasted_iota(jnp.int32, shape, dim)


def stacked(rows, parts=PARTS):
    width = rows.shape[1] // parts
    return jnp.concatenate([rows[:, p * width : (p + 1) * width] for p in range(parts)], axis=0)


def place_across(route_row, experts, capacity):
    tokens = route_row.shape[1]
    names = iota((max(8, experts), tokens), 0)
    onehot = jnp.where(names == route_row, 1.0, 0.0)
    earlier = jnp.where(iota((tokens, tokens), 0) < iota((tokens, tokens), 1), 1.0, 0.0)
    before = dot(onehot.astype(bf16), earlier.astype(bf16))
    place = onehot * (before + (names * (PARTS * capacity)).astype(f32))
    return jnp.sum(place, axis=0, keepdims=True).astype(jnp.int32)


def place_down(route_column, height):
    tokens = route_column.shape[0]
    names = iota((tokens, LANES), 1)
    onehot = jnp.where(names == route_column, 1.0, 0.0)
    earlier = jnp.where(iota((tokens, tokens), 1) < iota((tokens, tokens), 0), 1.0, 0.0)
    before = dot(earlier.astype(bf16), onehot.astype(bf16))
    place = onehot * (before + (names * height).astype(f32))
    return jnp.sum(place, axis=1, keepdims=True).astype(jnp.int32)


def pack_into(rows, place, out_refs, capacity):
    tokens = rows.shape[0]
    height = PARTS * capacity
    total = height * len(out_refs)
    places = jnp.concatenate([place + p * capacity for p in range(PARTS)], axis=1)
    pick = jnp.where(iota((total, PARTS * tokens), 0) == places, 1.0, 0.0).astype(bf16)
    packed = dot(pick, stacked(rows)).astype(bf16)
    for e, ref in enumerate(out_refs):
        ref[...] = packed[e * height : (e + 1) * height]


def back_pack_body(experts, capacity, route_ref, gate_ref, gain_ref, middle_ref, grad_ref, *outs):
    place = place_across(route_ref[...], experts, capacity)
    middle = middle_ref[...].astype(f32)
    normed = (middle * rms_scale(middle) * gain_ref[...]).astype(bf16)
    pack_into(normed, place, outs[:experts], capacity)
    scaled = (gate_ref[...] * grad_ref[...].astype(f32)).astype(bf16)
    pack_into(scaled, place, outs[experts:], capacity)


def join_body(capacity, *refs):
    chunks, out = refs[:-1], refs[-1]
    sources = len(chunks)
    height = PARTS * capacity
    rows = jnp.concatenate([ref[...] for ref in chunks], axis=0)
    slots = sources * capacity
    width = rows.shape[1]
    index = iota((slots, 1), 0)
    source = index * 0
    for s in range(1, sources):
        source = source + jnp.where(index >= s * capacity, 1, 0)
    first = index + source * (height - capacity)
    columns = iota((slots, rows.shape[0]), 1)
    for p in range(PARTS):
        pick = jnp.where(columns == first + p * capacity, 1.0, 0.0).astype(bf16)
        out[:, p * width : (p + 1) * width] = dot(pick, rows).astype(bf16)


def split_body(capacity, count_shares, lead, *refs):
    shares, outs = refs[:count_shares], refs[count_shares:]
    height, width = outs[0].shape
    parts = height // capacity
    total = None
    for ref in shares:
        at = lead if ref.shape[1] > parts * width else 0
        share = ref[:, at : at + parts * width].astype(f32)
        total = share if total is None else total + share
    rows = stacked(total.astype(bf16), parts)
    slots = shares[0].shape[0]
    count = height * len(outs)
    index = iota((count, 1), 0)
    group = index * 0
    source = index * 0
    for g in range(1, count // capacity):
        group = group + jnp.where(index >= g * capacity, 1, 0)
    for s in range(1, len(outs)):
        source = source + jnp.where(index >= s * height, 1, 0)
    part = group - source * parts
    place = part * slots + source * capacity + index - group * capacity
    pick = jnp.where(iota((count, parts * slots), 1) == place, 1.0, 0.0).astype(bf16)
    packed = dot(pick, rows).astype(bf16)
    for s, ref in enumerate(outs):
        ref[...] = packed[s * height : (s + 1) * height]


def unpacked(route_column, chunk_refs, experts, capacity):
    tokens = route_column.shape[0]
    groups = len(chunk_refs) // experts
    each = PARTS // groups
    place = place_down(route_column, each * capacity)
    parts = []
    for g in range(groups):
        chunks = chunk_refs[g * experts : (g + 1) * experts]
        rows = jnp.concatenate([ref[...] for ref in chunks], axis=0)
        columns = iota((tokens, rows.shape[0]), 1)
        for p in range(each):
            pick = jnp.where(columns == place + p * capacity, 1.0, 0.0).astype(bf16)
            parts.append(dot(pick, rows))
    return jnp.concatenate(parts, axis=1)


def front_finish_body(experts, capacity, route_ref, gate_ref, middle_ref, *refs):
    chunks, out = refs[:-1], refs[-1]
    contrib = gate_ref[...] * unpacked(route_ref[...], chunks, experts, capacity)
    out[...] = (middle_ref[...].astype(f32) + contrib).astype(bf16)


def back_finish_body(experts, capacity, route_ref, gain_ref, middle_ref, grad_ref, *refs):
    chunks, out = refs[:-1], refs[-1]
    amount = gain_ref[...] * unpacked(route_ref[...], chunks, experts, capacity)
    middle = middle_ref[...].astype(f32)
    scale = rms_scale(middle)
    cube = scale * scale * scale
    mean = jnp.mean(middle * amount, axis=-1, keepdims=True)
    out[...] = (grad_ref[...].astype(f32) + scale * amount - middle * cube * mean).astype(bf16)


def hidden_body(first_ref, second_ref, gate_ref, up_ref, out_ref):
    rows = jnp.concatenate([first_ref[...], second_ref[...]], axis=0)
    gate_val = dot(rows, gate_ref[...])
    up_val = dot(rows, up_ref[...])
    out_ref[...] = (gate_val / (1.0 + jnp.exp(-gate_val)) * up_val).astype(bf16)


def output_body(own_ref, other_ref, down_ref, far_ref, first_out, second_out):
    half = first_out.shape[0]
    hidden = jnp.concatenate([own_ref[...], other_ref[...]], axis=1)
    step = 4 * LANES
    for n in range(0, down_ref.shape[1], step):
        part = slice(n, n + step)
        weight = jnp.concatenate([down_ref[:, part], far_ref[:, part]], axis=0)
        value = dot(hidden, weight).astype(bf16)
        first_out[:, part] = value[:half]
        second_out[:, part] = value[half:]


def down_back_body(first_ref, second_ref, down_ref, far_ref, own_out, other_out):
    grads = jnp.concatenate([first_ref[...], second_ref[...]], axis=0)
    own_out[...] = dot_last(grads, down_ref[...]).astype(own_out.dtype)
    other_out[...] = dot_last(grads, far_ref[...]).astype(other_out.dtype)


def backward_body(first_ref, second_ref, back_ref, gate_ref, up_ref, first_out, second_out):
    half = first_ref.shape[0]
    rows = jnp.concatenate([first_ref[...], second_ref[...]], axis=0)
    gate_val = dot(rows, gate_ref[...])
    up_val = dot(rows, up_ref[...])
    down_back = back_ref[...].astype(f32)
    sigmoid_val = 1.0 / (1.0 + jnp.exp(-gate_val))
    slope_val = sigmoid_val * (1.0 + gate_val * (1.0 - sigmoid_val))
    gate_grad = (down_back * up_val * slope_val).astype(bf16)
    up_grad = (down_back * gate_val * sigmoid_val).astype(bf16)
    step = 4 * LANES
    for n in range(0, gate_ref.shape[0], step):
        value = dot_last(gate_grad, gate_ref[n : n + step])
        value = (value + dot_last(up_grad, up_ref[n : n + step])).astype(bf16)
        first_out[:, n : n + step] = value[:half]
        second_out[:, n : n + step] = value[half:]


def attend_body(
    experts,
    capacity,
    chosen_ref,
    index_ref,
    base_ref,
    route_ref,
    gain_ref,
    input_ref,
    query_ref,
    kv0,
    kv1,
    kv2,
    kv3,
    middle_ref,
    *refs,
):
    outs, (kv_all, kv_now, stack, attended) = refs[:experts], refs[experts:]
    tokens, width = query_ref.shape
    lead = 0
    for ref in (kv0, kv1, kv2, kv3):
        kv_all[lead : lead + ref.shape[0], : ref.shape[1]] = ref[...]
        lead += ref.shape[0]
    attended[...] = jnp.zeros_like(attended)
    heads_each = HEADS // KV_HEADS
    period = 8
    window = 2 * LANES
    keys = SEL * BLK
    lane = iota((keys, LANES), 1)
    batch = 4
    scale = HEAD_DIM**-0.5

    def one_block(block, _):
        top = pl.multiple_of(block * BLK, BLK)
        position = (base_ref[0] + block) * BLK + (iota((batch * BLK, keys), 0) & (BLK - 1))
        for head in range(KV_HEADS):
            key_pos = iota((1, keys), 1)
            shift = key_pos * 0
            for s in range(SEL):
                at = (block * KV_HEADS + head) * SEL + s
                start = pl.multiple_of(index_ref[at] * BLK, BLK)
                kv_now[s * BLK : (s + 1) * BLK, :] = kv_all[pl.ds(start, BLK), :].astype(f32)
                inside = (key_pos >= s * BLK) & (key_pos < (s + 1) * BLK)
                shift = jnp.where(inside, (chosen_ref[at] - s) * BLK, shift)
            allowed = key_pos + shift <= position
            sides = []
            for side in range(2):
                lead = (side * KV_HEADS + head) * HEAD_DIM
                tile = min(lead // LANES, 2)
                piece = kv_now[:, tile * LANES : tile * LANES + window]
                offset = lead - tile * LANES
                if offset:
                    piece = pltpu.roll(piece, window - offset, 1)
                sides.append(jnp.where(lane < HEAD_DIM, piece[:, :LANES], 0.0).astype(bf16))
            key_rows, value_rows = sides
            spots = []
            for j in range(heads_each):
                c = j % period
                tile = min(c * HEAD_DIM // LANES, period - 3)
                offset = c * HEAD_DIM - tile * LANES
                tile = tile + (j // period) * (period - 1) + head * heads_each * HEAD_DIM // LANES
                spots.append((tile * LANES, offset))
            for j, (lead, offset) in enumerate(spots):
                piece = query_ref[pl.ds(top, BLK), lead : lead + window].astype(f32)
                if offset:
                    piece = pltpu.roll(piece, window - offset, 1)
                stack[j * BLK : (j + 1) * BLK, :] = piece[:, :LANES].astype(bf16)
            for b in range(0, heads_each, batch):
                scores = dot_last(stack[b * BLK : (b + batch) * BLK, :], key_rows) * scale
                scores = jnp.where(allowed, scores, negative_large)
                exp_scores = jnp.exp(scores - jnp.max(scores, axis=-1, keepdims=True))
                total = jnp.sum(exp_scores, axis=-1, keepdims=True)
                mixed = dot((exp_scores / total).astype(bf16), value_rows)
                for i in range(batch):
                    lead, offset = spots[b + i]
                    piece = mixed[i * BLK : (i + 1) * BLK]
                    piece = jnp.concatenate([piece, jnp.zeros_like(piece)], axis=1)
                    if offset:
                        piece = pltpu.roll(piece, offset, 1)
                    spot = (pl.ds(top, BLK), slice(lead, lead + window))
                    attended[spot] = attended[spot] + piece
        return 0

    lax.fori_loop(0, tokens // BLK, one_block, 0)
    middle = (input_ref[...].astype(f32) + attended[...]).astype(bf16)
    middle_ref[...] = middle
    middle = middle.astype(f32)
    normed = (middle * rms_scale(middle) * gain_ref[...]).astype(bf16)
    pack_into(normed, place_across(route_ref[...], experts, capacity), outs, capacity)


def after(arrays, others):
    count = len(arrays)
    return list(lax.optimization_barrier(tuple(arrays) + tuple(others))[:count])


def shape_of(rows, columns, kind=bf16):
    return jax.ShapeDtypeStruct((rows, columns), kind)


def shards(
    front_input,
    queries,
    keys_values,
    selected_blocks,
    front_route,
    front_gate,
    back_middle,
    back_grad,
    back_route,
    back_gate,
    norm_gain,
    gate_slice,
    up_slice,
    down_slice,
):
    tokens, width = front_input.shape[1:]
    length = lax.axis_size("expert")
    experts = length // GROUP
    average = tokens // experts
    capacity = average + max(1, average // 8)
    slots = experts * capacity
    hidden_width = gate_slice.shape[3]
    w_gate, w_up, w_down = gate_slice[0, 0], up_slice[0, 0], down_slice[0, 0]
    me = lax.axis_index("expert")
    group = me // GROUP
    chunk = shape_of(PARTS * capacity, width // PARTS)
    piece = shape_of(slots, width)
    whole = shape_of(tokens, width)

    column = [keys_values[0]]
    for back in range(1, experts):
        pairs = [(i, i + back * GROUP) for i in range(length - back * GROUP)]
        column.append(lax.ppermute(keys_values[0], "expert", pairs))
    front_from = lax.rem(front_route[0] - group + experts, experts)
    back_from = lax.rem(back_route[0] - group + experts, experts)
    front_row, back_row = front_from.reshape(1, tokens), back_from.reshape(1, tokens)

    pack_flops = 4 * slots * PARTS * tokens * width
    packed = call(
        functools.partial(back_pack_body, experts, capacity),
        [chunk] * (2 * experts),
        (back_row, back_gate[0], norm_gain, back_middle[0], back_grad[0]),
        flops=2 * pack_flops,
    )
    column = after(column, [packed[0]])
    column = jnp.concatenate(column, axis=0)
    other_chip = swapped(column, 2)
    packed = after(packed, [column])

    front_small = jnp.concatenate([front_from.astype(f32), front_gate[0]], axis=0).reshape(1, -1)
    back_small = jnp.concatenate([back_from.astype(f32).reshape(1, -1), norm_gain], axis=1)

    def sent(chunks):
        return [chunks[0]] + [turned(chunks[k], k) for k in range(1, experts)]

    def joined(chunks):
        return call(functools.partial(join_body, capacity), piece, chunks, flops=pack_flops)

    def pieces_of(rows):
        other = swapped(rows, 2)
        return [rows, swapped(rows, 1), other, swapped(other, 1)]

    def split(shares, groups=1, group=0):
        return call(
            functools.partial(split_body, capacity, len(shares), group * (width // groups)),
            [shape_of(PARTS // groups * capacity, width // PARTS)] * experts,
            shares,
        )

    def sent_back(chunks, by):
        return [passed_along(chunks[k], by, k) for k in range(experts)]

    row_chunks, grad_chunks = packed[:experts], packed[experts:]
    row_chunks[1] = turned(row_chunks[1], 1)
    arrived = [row_chunks[1]]
    down_other = swapped(after([w_down], [other_chip] + arrived)[0], 2)
    downs = (w_down, down_other)
    there_back_middle = passed_along(after([back_middle[0]], [packed[0]])[0], -1)
    there_back_grad = passed_along(after([back_grad[0]], arrived + [there_back_middle])[0], -1)
    there_small = passed_along(after([front_small], arrived)[0], 1)
    there_back_small = passed_along(after([back_small], arrived)[0], -1)
    kv = [column, other_chip, swapped(column, 1), swapped(other_chip, 1)]
    for k in range(2, experts):
        row_chunks[k] = turned(after([row_chunks[k]], arrived)[0], k)
    beside = range(1, 2)
    for k in beside:
        grad_chunks[k] = turned(after([grad_chunks[k]], arrived)[0], k)

    per_device = tokens // BLK
    chosen = selected_blocks[0].reshape(-1)
    owner = chosen // per_device
    place = (owner % GROUP) ^ (me % GROUP)
    place = (place % 2) * 2 + place // 2
    index = (place * experts + group - owner // GROUP) * per_device + chosen % per_device
    index = jnp.clip(index, 0, length * per_device - 1)
    base = (me * per_device).astype(jnp.int32).reshape(1)
    result = call(
        functools.partial(attend_body, experts, capacity),
        [whole] + [chunk] * experts,
        (chosen, index, base, front_row, norm_gain, front_input[0], queries[0], *kv),
        scratch=[
            pltpu.VMEM((length * tokens, 4 * LANES), bf16),
            pltpu.VMEM((SEL * BLK, 4 * LANES), f32),
            pltpu.VMEM((HEADS // KV_HEADS * BLK, LANES), bf16),
            pltpu.VMEM((tokens, width), f32),
        ],
        flops=pack_flops + 4 * tokens * HEADS * SEL * BLK * LANES,
        smem=3,
        vmem=VMEM_BYTES + 2 * length * tokens * 4 * LANES * 2,
    )
    middle, front_chunks = result[0], result[1:]
    ready = row_chunks + [grad_chunks[k] for k in beside]
    front_chunks = sent(after(front_chunks, ready))
    for k in range(1, experts):
        if k not in beside:
            grad_chunks[k] = turned(after([grad_chunks[k]], [middle])[0], k)
    back_rows = joined(after(ready, [middle, there_back_grad, there_small, there_back_small])[:experts])
    grad_near = joined(after(grad_chunks, [back_rows, down_other]))
    grad_near = [grad_near, swapped(grad_near, 1)]
    back_pieces = pieces_of(back_rows)
    there_front_from = there_small[0, :tokens].astype(jnp.int32).reshape(tokens, 1)
    there_front_gate = there_small[0, tokens:].reshape(tokens, 1)
    there_back_from = there_back_small[0, :tokens].astype(jnp.int32).reshape(tokens, 1)
    there_gain = there_back_small[:, tokens:]
    work = 2 * 2 * slots * width * hidden_width
    pair = 2 * slots

    def hidden(rows):
        return call(
            hidden_body, shape_of(pair, hidden_width), (*rows, w_gate, w_up), flops=2 * work
        )

    def backward(rows, grads):
        return call(backward_body, [piece, piece], (*rows, grads, w_gate, w_up), flops=4 * work)

    down_back, other_back = call(
        down_back_body,
        [shape_of(pair, hidden_width, f32), shape_of(pair, hidden_width)],
        (*after(grad_near, front_chunks), *downs),
        flops=2 * work,
    )
    far_back = swapped(other_back, 2)
    back_near = backward(back_pieces[:2], down_back)
    back_core = swapped(back_near[1], 1)
    front_near = joined(after(front_chunks, [back_pieces[2], other_back]))
    front_other = swapped(front_near, 2)
    there_middle = passed_along(after([middle], [front_near])[0], 1)
    front_core = swapped(front_near, 1)
    hidden_near = hidden((front_near, front_core))
    (front_other,) = after([front_other], [back_core, hidden_near, there_middle])
    (far_back,) = after([far_back], [front_other])
    back_far = backward(back_pieces[2:], far_back)
    chip = back_far[0].astype(f32) + swapped(back_far[1], 1).astype(f32)
    chip = chip.astype(bf16)
    hidden_far = hidden((front_other, swapped(front_other, 1)))
    hidden_other = swapped(hidden_far, 2)
    back_shares = [back_near[0], back_core, swapped(after([chip], [hidden_other])[0], 2)]

    front_own, front_core = call(
        output_body, [piece, piece], (hidden_near, hidden_other, *downs), flops=2 * work
    )
    front_core = swapped(front_core, 1)
    front_chunks = split((front_own, front_core))
    front_return = sent_back(front_chunks, 1)

    back_chunks = split(after(back_shares, front_chunks))
    back_return = sent_back(back_chunks, -1)
    front_return = after(front_return, back_chunks)
    front_output = call(
        functools.partial(front_finish_body, experts, capacity),
        whole,
        (there_front_from, there_front_gate, there_middle, *front_return),
        flops=pack_flops,
    )
    back_return = after(back_return, [front_output])
    back_output = call(
        functools.partial(back_finish_body, experts, capacity),
        whole,
        (there_back_from, there_gain, there_back_middle, there_back_grad, *back_return),
        flops=pack_flops,
    )
    return (front_output[None], back_output[None])


def solution(mesh):
    placed = (
        P("section", "expert", None),
        P("section", "expert", None),
        P("section", "expert", None),
        P("section", "expert", None, None),
        P("section", "expert", None),
        P("section", "expert", None),
        P("section", "expert", None),
        P("section", "expert", None),
        P("section", "expert", None),
        P("section", "expert", None),
        P("section", None),
        P("section", "expert", None, None),
        P("section", "expert", None, None),
        P("section", "expert", None, None),
    )
    return jax.shard_map(
        shards,
        mesh=mesh,
        in_specs=placed,
        out_specs=(P("section", "expert", None), P("section", "expert", None)),
        check_vma=False,
    )
```

```python
import functools

import jax
import jax.numpy as jnp
from jax import lax
from jax.experimental import pallas as pl
from jax.experimental.pallas import tpu as pltpu
from jax.sharding import PartitionSpec as P

GROUP = 4
HEADS = 32
HEAD_DIM = 112
KV_HEADS = 2
BLK = 64
SEL = 4
PARTS = 4
LANES = 128
VMEM_BYTES = 28 * 1024 * 1024

epsilon = 1e-06
negative_large = -1e30
bf16 = jnp.bfloat16
f32 = jnp.float32


def passed_along(array, by, back=0):
    sections, length = lax.axis_size("section"), lax.axis_size("expert")
    pairs = [
        (s * length + i, (s + by) % sections * length + (i - back * GROUP) % length)
        for s in range(sections)
        for i in range(length)
    ]
    return lax.ppermute(array, ("section", "expert"), pairs)


def swapped(array, bit):
    return lax.ppermute(array, "expert", [(i, i ^ bit) for i in range(lax.axis_size("expert"))])


def turned(array, by):
    length = lax.axis_size("expert")
    return lax.ppermute(
        array, "expert", [(i, (i + by * GROUP) % length) for i in range(length)]
    )


def call(body, outs, args, scratch=(), flops=0, smem=0, vmem=VMEM_BYTES):
    specs = [
        pl.BlockSpec(memory_space=pltpu.SMEM if i < smem else pltpu.VMEM)
        for i in range(len(args))
    ]
    many = isinstance(outs, list)
    shapes = outs if many else [outs]
    moved_bytes = sum(a.size * a.dtype.itemsize for a in list(args) + shapes)
    result = pl.pallas_call(
        body,
        out_shape=shapes,
        in_specs=specs,
        out_specs=[pl.BlockSpec(memory_space=pltpu.VMEM) for _ in shapes],
        scratch_shapes=list(scratch),
        compiler_params=pltpu.CompilerParams(vmem_limit_bytes=vmem),
        cost_estimate=pl.CostEstimate(
            flops=int(flops), bytes_accessed=int(moved_bytes), transcendentals=0
        ),
    )(*args)
    return list(result) if many else result[0]


def dot(a, b):
    return jnp.dot(a, b, preferred_element_type=f32)


def dot_last(a, b):
    return lax.dot_general(a, b, (((1,), (1,)), ((), ())), preferred_element_type=f32)


def rms_scale(rows):
    return lax.rsqrt(jnp.mean(rows * rows, axis=-1, keepdims=True) + epsilon)


def iota(shape, dim):
    return lax.broadcasted_iota(jnp.int32, shape, dim)


def stacked(rows, parts=PARTS):
    width = rows.shape[1] // parts
    return jnp.concatenate([rows[:, p * width : (p + 1) * width] for p in range(parts)], axis=0)


def place_across(route_row, experts, capacity):
    tokens = route_row.shape[1]
    names = iota((max(8, experts), tokens), 0)
    onehot = jnp.where(names == route_row, 1.0, 0.0)
    earlier = jnp.where(iota((tokens, tokens), 0) < iota((tokens, tokens), 1), 1.0, 0.0)
    before = dot(onehot.astype(bf16), earlier.astype(bf16))
    place = onehot * (before + (names * (PARTS * capacity)).astype(f32))
    return jnp.sum(place, axis=0, keepdims=True).astype(jnp.int32)


def place_down(route_column, height):
    tokens = route_column.shape[0]
    names = iota((tokens, LANES), 1)
    onehot = jnp.where(names == route_column, 1.0, 0.0)
    earlier = jnp.where(iota((tokens, tokens), 1) < iota((tokens, tokens), 0), 1.0, 0.0)
    before = dot(earlier.astype(bf16), onehot.astype(bf16))
    place = onehot * (before + (names * height).astype(f32))
    return jnp.sum(place, axis=1, keepdims=True).astype(jnp.int32)


def pack_into(rows, place, out_refs, capacity):
    tokens = rows.shape[0]
    height = PARTS * capacity
    total = height * len(out_refs)
    places = jnp.concatenate([place + p * capacity for p in range(PARTS)], axis=1)
    pick = jnp.where(iota((total, PARTS * tokens), 0) == places, 1.0, 0.0).astype(bf16)
    packed = dot(pick, stacked(rows)).astype(bf16)
    for e, ref in enumerate(out_refs):
        ref[...] = packed[e * height : (e + 1) * height]


def back_pack_body(experts, capacity, route_ref, gate_ref, gain_ref, middle_ref, grad_ref, *outs):
    place = place_across(route_ref[...], experts, capacity)
    middle = middle_ref[...].astype(f32)
    normed = (middle * rms_scale(middle) * gain_ref[...]).astype(bf16)
    pack_into(normed, place, outs[:experts], capacity)
    scaled = (gate_ref[...] * grad_ref[...].astype(f32)).astype(bf16)
    pack_into(scaled, place, outs[experts:], capacity)


def join_body(capacity, *refs):
    chunks, out = refs[:-1], refs[-1]
    sources = len(chunks)
    height = PARTS * capacity
    rows = jnp.concatenate([ref[...] for ref in chunks], axis=0)
    slots = sources * capacity
    width = rows.shape[1]
    index = iota((slots, 1), 0)
    source = index * 0
    for s in range(1, sources):
        source = source + jnp.where(index >= s * capacity, 1, 0)
    first = index + source * (height - capacity)
    columns = iota((slots, rows.shape[0]), 1)
    for p in range(PARTS):
        pick = jnp.where(columns == first + p * capacity, 1.0, 0.0).astype(bf16)
        out[:, p * width : (p + 1) * width] = dot(pick, rows).astype(bf16)


def split_body(capacity, count_shares, lead, *refs):
    shares, outs = refs[:count_shares], refs[count_shares:]
    height, width = outs[0].shape
    parts = height // capacity
    total = None
    for ref in shares:
        at = lead if ref.shape[1] > parts * width else 0
        share = ref[:, at : at + parts * width].astype(f32)
        total = share if total is None else total + share
    rows = stacked(total.astype(bf16), parts)
    slots = shares[0].shape[0]
    count = height * len(outs)
    index = iota((count, 1), 0)
    group = index * 0
    source = index * 0
    for g in range(1, count // capacity):
        group = group + jnp.where(index >= g * capacity, 1, 0)
    for s in range(1, len(outs)):
        source = source + jnp.where(index >= s * height, 1, 0)
    part = group - source * parts
    place = part * slots + source * capacity + index - group * capacity
    pick = jnp.where(iota((count, parts * slots), 1) == place, 1.0, 0.0).astype(bf16)
    packed = dot(pick, rows).astype(bf16)
    for s, ref in enumerate(outs):
        ref[...] = packed[s * height : (s + 1) * height]


def unpacked(route_column, chunk_refs, experts, capacity):
    tokens = route_column.shape[0]
    groups = len(chunk_refs) // experts
    each = PARTS // groups
    place = place_down(route_column, each * capacity)
    parts = []
    for g in range(groups):
        chunks = chunk_refs[g * experts : (g + 1) * experts]
        rows = jnp.concatenate([ref[...] for ref in chunks], axis=0)
        columns = iota((tokens, rows.shape[0]), 1)
        for p in range(each):
            pick = jnp.where(columns == place + p * capacity, 1.0, 0.0).astype(bf16)
            parts.append(dot(pick, rows))
    return jnp.concatenate(parts, axis=1)


def front_finish_body(experts, capacity, route_ref, gate_ref, middle_ref, *refs):
    chunks, out = refs[:-1], refs[-1]
    contrib = gate_ref[...] * unpacked(route_ref[...], chunks, experts, capacity)
    out[...] = (middle_ref[...].astype(f32) + contrib).astype(bf16)


def back_finish_body(experts, capacity, route_ref, gain_ref, middle_ref, grad_ref, *refs):
    chunks, out = refs[:-1], refs[-1]
    amount = gain_ref[...] * unpacked(route_ref[...], chunks, experts, capacity)
    middle = middle_ref[...].astype(f32)
    scale = rms_scale(middle)
    cube = scale * scale * scale
    mean = jnp.mean(middle * amount, axis=-1, keepdims=True)
    out[...] = (grad_ref[...].astype(f32) + scale * amount - middle * cube * mean).astype(bf16)


def hidden_body(first_ref, second_ref, gate_ref, up_ref, out_ref):
    rows = jnp.concatenate([first_ref[...], second_ref[...]], axis=0)
    gate_val = dot(rows, gate_ref[...])
    up_val = dot(rows, up_ref[...])
    out_ref[...] = (gate_val / (1.0 + jnp.exp(-gate_val)) * up_val).astype(bf16)


def output_body(own_ref, other_ref, down_ref, far_ref, first_out, second_out):
    half = first_out.shape[0]
    hidden = jnp.concatenate([own_ref[...], other_ref[...]], axis=1)
    step = 4 * LANES
    for n in range(0, down_ref.shape[1], step):
        part = slice(n, n + step)
        weight = jnp.concatenate([down_ref[:, part], far_ref[:, part]], axis=0)
        value = dot(hidden, weight).astype(bf16)
        first_out[:, part] = value[:half]
        second_out[:, part] = value[half:]


def down_back_body(first_ref, second_ref, down_ref, far_ref, own_out, other_out):
    grads = jnp.concatenate([first_ref[...], second_ref[...]], axis=0)
    own_out[...] = dot_last(grads, down_ref[...]).astype(own_out.dtype)
    other_out[...] = dot_last(grads, far_ref[...]).astype(other_out.dtype)


def backward_body(first_ref, second_ref, back_ref, gate_ref, up_ref, first_out, second_out):
    half = first_ref.shape[0]
    rows = jnp.concatenate([first_ref[...], second_ref[...]], axis=0)
    gate_val = dot(rows, gate_ref[...])
    up_val = dot(rows, up_ref[...])
    down_back = back_ref[...].astype(f32)
    sigmoid_val = 1.0 / (1.0 + jnp.exp(-gate_val))
    slope_val = sigmoid_val * (1.0 + gate_val * (1.0 - sigmoid_val))
    gate_grad = (down_back * up_val * slope_val).astype(bf16)
    up_grad = (down_back * gate_val * sigmoid_val).astype(bf16)
    step = 4 * LANES
    for n in range(0, gate_ref.shape[0], step):
        value = dot_last(gate_grad, gate_ref[n : n + step])
        value = (value + dot_last(up_grad, up_ref[n : n + step])).astype(bf16)
        first_out[:, n : n + step] = value[:half]
        second_out[:, n : n + step] = value[half:]


def attend_body(
    experts,
    capacity,
    chosen_ref,
    index_ref,
    base_ref,
    route_ref,
    gain_ref,
    input_ref,
    query_ref,
    kv0,
    kv1,
    kv2,
    kv3,
    middle_ref,
    *refs,
):
    outs, (kv_all, kv_now, stack, attended) = refs[:experts], refs[experts:]
    tokens, width = query_ref.shape
    lead = 0
    for ref in (kv0, kv1, kv2, kv3):
        kv_all[lead : lead + ref.shape[0], : ref.shape[1]] = ref[...]
        lead += ref.shape[0]
    attended[...] = jnp.zeros_like(attended)
    heads_each = HEADS // KV_HEADS
    period = 8
    window = 2 * LANES
    keys = SEL * BLK
    lane = iota((keys, LANES), 1)
    batch = 4
    scale = HEAD_DIM**-0.5

    def one_block(block, _):
        top = pl.multiple_of(block * BLK, BLK)
        position = (base_ref[0] + block) * BLK + (iota((batch * BLK, keys), 0) & (BLK - 1))
        for head in range(KV_HEADS):
            key_pos = iota((1, keys), 1)
            shift = key_pos * 0
            for s in range(SEL):
                at = (block * KV_HEADS + head) * SEL + s
                start = pl.multiple_of(index_ref[at] * BLK, BLK)
                kv_now[s * BLK : (s + 1) * BLK, :] = kv_all[pl.ds(start, BLK), :].astype(f32)
                inside = (key_pos >= s * BLK) & (key_pos < (s + 1) * BLK)
                shift = jnp.where(inside, (chosen_ref[at] - s) * BLK, shift)
            allowed = key_pos + shift <= position
            sides = []
            for side in range(2):
                lead = (side * KV_HEADS + head) * HEAD_DIM
                tile = min(lead // LANES, 2)
                piece = kv_now[:, tile * LANES : tile * LANES + window]
                offset = lead - tile * LANES
                if offset:
                    piece = pltpu.roll(piece, window - offset, 1)
                sides.append(jnp.where(lane < HEAD_DIM, piece[:, :LANES], 0.0).astype(bf16))
            key_rows, value_rows = sides
            spots = []
            for j in range(heads_each):
                c = j % period
                tile = min(c * HEAD_DIM // LANES, period - 3)
                offset = c * HEAD_DIM - tile * LANES
                tile = tile + (j // period) * (period - 1) + head * heads_each * HEAD_DIM // LANES
                spots.append((tile * LANES, offset))
            for j, (lead, offset) in enumerate(spots):
                piece = query_ref[pl.ds(top, BLK), lead : lead + window].astype(f32)
                if offset:
                    piece = pltpu.roll(piece, window - offset, 1)
                stack[j * BLK : (j + 1) * BLK, :] = piece[:, :LANES].astype(bf16)
            for b in range(0, heads_each, batch):
                scores = dot_last(stack[b * BLK : (b + batch) * BLK, :], key_rows) * scale
                scores = jnp.where(allowed, scores, negative_large)
                exp_scores = jnp.exp(scores - jnp.max(scores, axis=-1, keepdims=True))
                total = jnp.sum(exp_scores, axis=-1, keepdims=True)
                mixed = dot((exp_scores / total).astype(bf16), value_rows)
                for i in range(batch):
                    lead, offset = spots[b + i]
                    piece = mixed[i * BLK : (i + 1) * BLK]
                    piece = jnp.concatenate([piece, jnp.zeros_like(piece)], axis=1)
                    if offset:
                        piece = pltpu.roll(piece, offset, 1)
                    spot = (pl.ds(top, BLK), slice(lead, lead + window))
                    attended[spot] = attended[spot] + piece
        return 0

    lax.fori_loop(0, tokens // BLK, one_block, 0)
    middle = (input_ref[...].astype(f32) + attended[...]).astype(bf16)
    middle_ref[...] = middle
    middle = middle.astype(f32)
    normed = (middle * rms_scale(middle) * gain_ref[...]).astype(bf16)
    pack_into(normed, place_across(route_ref[...], experts, capacity), outs, capacity)


def after(arrays, others):
    count = len(arrays)
    return list(lax.optimization_barrier(tuple(arrays) + tuple(others))[:count])


def shape_of(rows, columns, kind=bf16):
    return jax.ShapeDtypeStruct((rows, columns), kind)


def shards(
    front_input,
    queries,
    keys_values,
    selected_blocks,
    front_route,
    front_gate,
    back_middle,
    back_grad,
    back_route,
    back_gate,
    norm_gain,
    gate_slice,
    up_slice,
    down_slice,
):
    tokens, width = front_input.shape[1:]
    length = lax.axis_size("expert")
    experts = length // GROUP
    average = tokens // experts
    capacity = average + max(1, average // 8)
    slots = experts * capacity
    hidden_width = gate_slice.shape[3]
    w_gate, w_up, w_down = gate_slice[0, 0], up_slice[0, 0], down_slice[0, 0]
    me = lax.axis_index("expert")
    group = me // GROUP
    chunk = shape_of(PARTS * capacity, width // PARTS)
    piece = shape_of(slots, width)
    whole = shape_of(tokens, width)

    column = [keys_values[0]]
    for back in range(1, experts):
        pairs = [(i, i + back * GROUP) for i in range(length - back * GROUP)]
        column.append(lax.ppermute(keys_values[0], "expert", pairs))
    front_from = lax.rem(front_route[0] - group + experts, experts)
    back_from = lax.rem(back_route[0] - group + experts, experts)
    front_row, back_row = front_from.reshape(1, tokens), back_from.reshape(1, tokens)

    pack_flops = 4 * slots * PARTS * tokens * width
    packed = call(
        functools.partial(back_pack_body, experts, capacity),
        [chunk] * (2 * experts),
        (back_row, back_gate[0], norm_gain, back_middle[0], back_grad[0]),
        flops=2 * pack_flops,
    )
    column = after(column, [packed[0]])
    column = jnp.concatenate(column, axis=0)
    other_chip = swapped(column, 2)
    packed = after(packed, [column])

    front_small = jnp.concatenate([front_from.astype(f32), front_gate[0]], axis=0).reshape(1, -1)
    back_small = jnp.concatenate([back_from.astype(f32).reshape(1, -1), norm_gain], axis=1)

    def sent(chunks):
        return [chunks[0]] + [turned(chunks[k], k) for k in range(1, experts)]

    def joined(chunks):
        return call(functools.partial(join_body, capacity), piece, chunks, flops=pack_flops)

    def pieces_of(rows):
        other = swapped(rows, 2)
        return [rows, swapped(rows, 1), other, swapped(other, 1)]

    def split(shares, groups=1, group=0):
        return call(
            functools.partial(split_body, capacity, len(shares), group * (width // groups)),
            [shape_of(PARTS // groups * capacity, width // PARTS)] * experts,
            shares,
        )

    def sent_back(chunks, by):
        return [passed_along(chunks[k], by, k) for k in range(experts)]

    row_chunks, grad_chunks = packed[:experts], packed[experts:]
    first = 1 + 2 * (experts - 1) // 3
    for k in range(1, first):
        row_chunks[k] = turned(row_chunks[k], k)
    arrived = row_chunks[1:first]
    down_other = swapped(after([w_down], [other_chip, arrived[0]])[0], 2)
    downs = (w_down, down_other)
    far = swapped(after([other_chip], arrived)[0], 1)
    kv = [column, other_chip, swapped(column, 1), far]
    for k in range(first, experts):
        row_chunks[k] = turned(after([row_chunks[k]], arrived)[0], k)
    there_back_middle = passed_along(after([back_middle[0]], arrived)[0], -1)
    beside = range(1, 2)
    for k in beside:
        grad_chunks[k] = turned(after([grad_chunks[k]], arrived)[0], k)

    per_device = tokens // BLK
    chosen = selected_blocks[0].reshape(-1)
    owner = chosen // per_device
    place = (owner % GROUP) ^ (me % GROUP)
    place = (place % 2) * 2 + place // 2
    index = (place * experts + group - owner // GROUP) * per_device + chosen % per_device
    index = jnp.clip(index, 0, length * per_device - 1)
    base = (me * per_device).astype(jnp.int32).reshape(1)
    result = call(
        functools.partial(attend_body, experts, capacity),
        [whole] + [chunk] * experts,
        (chosen, index, base, front_row, norm_gain, front_input[0], queries[0], *kv),
        scratch=[
            pltpu.VMEM((length * tokens, 4 * LANES), bf16),
            pltpu.VMEM((SEL * BLK, 4 * LANES), f32),
            pltpu.VMEM((HEADS // KV_HEADS * BLK, LANES), bf16),
            pltpu.VMEM((tokens, width), f32),
        ],
        flops=pack_flops + 4 * tokens * HEADS * SEL * BLK * LANES,
        smem=3,
        vmem=VMEM_BYTES + 2 * length * tokens * 4 * LANES * 2,
    )
    middle, front_chunks = result[0], result[1:]
    ready = row_chunks + [grad_chunks[k] for k in beside]
    front_chunks = sent(after(front_chunks, ready))
    for k in range(1, experts):
        if k not in beside:
            grad_chunks[k] = turned(after([grad_chunks[k]], [middle])[0], k)
    back_rows = joined(after(ready, [middle])[:experts])
    grad_near = joined(after(grad_chunks, [back_rows, down_other, there_back_middle]))
    grad_near = [grad_near, swapped(grad_near, 1)]
    there_back_grad = passed_along(after([back_grad[0]], [grad_near[0]])[0], -1)
    back_other = swapped(back_rows, 2)

    work = 2 * 2 * slots * width * hidden_width
    pair = 2 * slots

    def hidden(rows):
        return call(
            hidden_body, shape_of(pair, hidden_width), (*rows, w_gate, w_up), flops=2 * work
        )

    def backward(rows, grads):
        return call(backward_body, [piece, piece], (*rows, grads, w_gate, w_up), flops=4 * work)

    down_back, other_back = call(
        down_back_body,
        [shape_of(pair, hidden_width, f32), shape_of(pair, hidden_width)],
        (*after(grad_near, front_chunks), *downs),
        flops=2 * work,
    )
    far_back = swapped(other_back, 2)
    front_near = joined(after(front_chunks, [back_other, other_back, there_back_grad]))
    front_other = swapped(front_near, 2)
    front_small, back_small, late = after([front_small, back_small, middle], [front_near])
    there_middle = passed_along(late, 1)
    there_small = passed_along(front_small, 1)
    there_back_small = passed_along(back_small, -1)
    there_front_from = there_small[0, :tokens].astype(jnp.int32).reshape(tokens, 1)
    there_front_gate = there_small[0, tokens:].reshape(tokens, 1)
    there_back_from = there_back_small[0, :tokens].astype(jnp.int32).reshape(tokens, 1)
    there_gain = there_back_small[:, tokens:]
    back_near = backward((back_rows, swapped(after([back_rows], [front_near])[0], 1)), down_back)
    back_core = swapped(back_near[1], 1)
    front_core = swapped(front_near, 1)
    hidden_near = hidden((front_near, front_core))
    (front_other,) = after([front_other], [back_core, hidden_near, there_middle, there_small, there_back_small])
    (far_back,) = after([far_back], [front_other])
    back_far = backward((back_other, swapped(back_other, 1)), far_back)
    chip = back_far[0].astype(f32) + swapped(back_far[1], 1).astype(f32)
    chip = chip.astype(bf16)
    hidden_far = hidden((front_other, swapped(front_other, 1)))
    hidden_other = swapped(hidden_far, 2)
    back_shares = [back_near[0], back_core, swapped(after([chip], [hidden_other])[0], 2)]

    front_own, front_core = call(
        output_body, [piece, piece], (hidden_near, hidden_other, *downs), flops=2 * work
    )
    front_core = swapped(front_core, 1)
    front_chunks = split((front_own, front_core))
    front_return = sent_back(front_chunks, 1)

    back_chunks = split(after(back_shares, front_chunks))
    back_return = sent_back(back_chunks, -1)
    front_return = after(front_return, back_chunks)
    front_output = call(
        functools.partial(front_finish_body, experts, capacity),
        whole,
        (there_front_from, there_front_gate, there_middle, *front_return),
        flops=pack_flops,
    )
    back_return = after(back_return, [front_output])
    back_output = call(
        functools.partial(back_finish_body, experts, capacity),
        whole,
        (there_back_from, there_gain, there_back_middle, there_back_grad, *back_return),
        flops=pack_flops,
    )
    return (front_output[None], back_output[None])


def solution(mesh):
    placed = (
        P("section", "expert", None),
        P("section", "expert", None),
        P("section", "expert", None),
        P("section", "expert", None, None),
        P("section", "expert", None),
        P("section", "expert", None),
        P("section", "expert", None),
        P("section", "expert", None),
        P("section", "expert", None),
        P("section", "expert", None),
        P("section", None),
        P("section", "expert", None, None),
        P("section", "expert", None, None),
        P("section", "expert", None, None),
    )
    return jax.shard_map(
        shards,
        mesh=mesh,
        in_specs=placed,
        out_specs=(P("section", "expert", None), P("section", "expert", None)),
        check_vma=False,
    )
```

```python
import functools

import jax
import jax.numpy as jnp
from jax import lax
from jax.experimental import pallas as pl
from jax.experimental.pallas import tpu as pltpu
from jax.sharding import PartitionSpec as P

GROUP = 4
HEADS = 32
HEAD_DIM = 112
KV_HEADS = 2
BLK = 64
SEL = 4
PARTS = 4
LANES = 128
VMEM_BYTES = 28 * 1024 * 1024

epsilon = 1e-06
negative_large = -1e30
bf16 = jnp.bfloat16
f32 = jnp.float32


def passed_along(array, by, back=0):
    sections, length = lax.axis_size("section"), lax.axis_size("expert")
    pairs = [
        (s * length + i, (s + by) % sections * length + (i - back * GROUP) % length)
        for s in range(sections)
        for i in range(length)
    ]
    return lax.ppermute(array, ("section", "expert"), pairs)


def swapped(array, bit):
    return lax.ppermute(array, "expert", [(i, i ^ bit) for i in range(lax.axis_size("expert"))])


def turned(array, by):
    length = lax.axis_size("expert")
    return lax.ppermute(
        array, "expert", [(i, (i + by * GROUP) % length) for i in range(length)]
    )


def call(body, outs, args, scratch=(), flops=0, smem=0, vmem=VMEM_BYTES):
    specs = [
        pl.BlockSpec(memory_space=pltpu.SMEM if i < smem else pltpu.VMEM)
        for i in range(len(args))
    ]
    many = isinstance(outs, list)
    shapes = outs if many else [outs]
    moved_bytes = sum(a.size * a.dtype.itemsize for a in list(args) + shapes)
    result = pl.pallas_call(
        body,
        out_shape=shapes,
        in_specs=specs,
        out_specs=[pl.BlockSpec(memory_space=pltpu.VMEM) for _ in shapes],
        scratch_shapes=list(scratch),
        compiler_params=pltpu.CompilerParams(vmem_limit_bytes=vmem),
        cost_estimate=pl.CostEstimate(
            flops=int(flops), bytes_accessed=int(moved_bytes), transcendentals=0
        ),
    )(*args)
    return list(result) if many else result[0]


def dot(a, b):
    return jnp.dot(a, b, preferred_element_type=f32)


def dot_last(a, b):
    return lax.dot_general(a, b, (((1,), (1,)), ((), ())), preferred_element_type=f32)


def rms_scale(rows):
    return lax.rsqrt(jnp.mean(rows * rows, axis=-1, keepdims=True) + epsilon)


def iota(shape, dim):
    return lax.broadcasted_iota(jnp.int32, shape, dim)


def stacked(rows):
    width = rows.shape[1] // PARTS
    return jnp.concatenate([rows[:, p * width : (p + 1) * width] for p in range(PARTS)], axis=0)


def place_across(route_row, experts, capacity):
    tokens = route_row.shape[1]
    names = iota((max(8, experts), tokens), 0)
    onehot = jnp.where(names == route_row, 1.0, 0.0)
    earlier = jnp.where(iota((tokens, tokens), 0) < iota((tokens, tokens), 1), 1.0, 0.0)
    before = dot(onehot.astype(bf16), earlier.astype(bf16))
    place = onehot * (before + (names * (PARTS * capacity)).astype(f32))
    return jnp.sum(place, axis=0, keepdims=True).astype(jnp.int32)


def place_down(route_column, experts, capacity):
    tokens = route_column.shape[0]
    names = iota((tokens, LANES), 1)
    onehot = jnp.where(names == route_column, 1.0, 0.0)
    earlier = jnp.where(iota((tokens, tokens), 1) < iota((tokens, tokens), 0), 1.0, 0.0)
    before = dot(earlier.astype(bf16), onehot.astype(bf16))
    place = onehot * (before + (names * (PARTS * capacity)).astype(f32))
    return jnp.sum(place, axis=1, keepdims=True).astype(jnp.int32)


def pack_into(rows, place, out_refs, capacity):
    tokens = rows.shape[0]
    height = PARTS * capacity
    total = height * len(out_refs)
    places = jnp.concatenate([place + p * capacity for p in range(PARTS)], axis=1)
    pick = jnp.where(iota((total, PARTS * tokens), 0) == places, 1.0, 0.0).astype(bf16)
    packed = dot(pick, stacked(rows)).astype(bf16)
    for e, ref in enumerate(out_refs):
        ref[...] = packed[e * height : (e + 1) * height]


def back_pack_body(experts, capacity, route_ref, gate_ref, gain_ref, middle_ref, grad_ref, *outs):
    place = place_across(route_ref[...], experts, capacity)
    middle = middle_ref[...].astype(f32)
    normed = (middle * rms_scale(middle) * gain_ref[...]).astype(bf16)
    pack_into(normed, place, outs[:experts], capacity)
    scaled = (gate_ref[...] * grad_ref[...].astype(f32)).astype(bf16)
    pack_into(scaled, place, outs[experts:], capacity)


def join_body(capacity, *refs):
    chunks, out = refs[:-1], refs[-1]
    sources = len(chunks)
    height = PARTS * capacity
    rows = jnp.concatenate([ref[...] for ref in chunks], axis=0)
    slots = sources * capacity
    width = rows.shape[1]
    index = iota((slots, 1), 0)
    source = index * 0
    for s in range(1, sources):
        source = source + jnp.where(index >= s * capacity, 1, 0)
    first = index + source * (height - capacity)
    columns = iota((slots, rows.shape[0]), 1)
    for p in range(PARTS):
        pick = jnp.where(columns == first + p * capacity, 1.0, 0.0).astype(bf16)
        out[:, p * width : (p + 1) * width] = dot(pick, rows).astype(bf16)


def split_body(capacity, count_shares, *refs):
    shares, outs = refs[:count_shares], refs[count_shares:]
    total = shares[0][...].astype(f32)
    for ref in shares[1:]:
        total = total + ref[...].astype(f32)
    rows = stacked(total.astype(bf16))
    height = PARTS * capacity
    slots = shares[0].shape[0]
    count = height * len(outs)
    index = iota((count, 1), 0)
    group = index * 0
    source = index * 0
    for g in range(1, count // capacity):
        group = group + jnp.where(index >= g * capacity, 1, 0)
    for s in range(1, len(outs)):
        source = source + jnp.where(index >= s * height, 1, 0)
    part = group - source * PARTS
    place = part * slots + source * capacity + index - group * capacity
    pick = jnp.where(iota((count, PARTS * slots), 1) == place, 1.0, 0.0).astype(bf16)
    packed = dot(pick, rows).astype(bf16)
    for s, ref in enumerate(outs):
        ref[...] = packed[s * height : (s + 1) * height]


def unpacked(route_column, chunk_refs, experts, capacity):
    tokens = route_column.shape[0]
    place = place_down(route_column, experts, capacity)
    rows = jnp.concatenate([ref[...] for ref in chunk_refs], axis=0)
    columns = iota((tokens, rows.shape[0]), 1)
    parts = []
    for p in range(PARTS):
        pick = jnp.where(columns == place + p * capacity, 1.0, 0.0).astype(bf16)
        parts.append(dot(pick, rows))
    return jnp.concatenate(parts, axis=1)


def front_finish_body(experts, capacity, route_ref, gate_ref, middle_ref, *refs):
    chunks, out = refs[:-1], refs[-1]
    contrib = gate_ref[...] * unpacked(route_ref[...], chunks, experts, capacity)
    out[...] = (middle_ref[...].astype(f32) + contrib).astype(bf16)


def back_finish_body(experts, capacity, route_ref, gain_ref, middle_ref, grad_ref, *refs):
    chunks, out = refs[:-1], refs[-1]
    amount = gain_ref[...] * unpacked(route_ref[...], chunks, experts, capacity)
    middle = middle_ref[...].astype(f32)
    scale = rms_scale(middle)
    cube = scale * scale * scale
    mean = jnp.mean(middle * amount, axis=-1, keepdims=True)
    out[...] = (grad_ref[...].astype(f32) + scale * amount - middle * cube * mean).astype(bf16)


def hidden_body(first_ref, second_ref, gate_ref, up_ref, out_ref):
    rows = jnp.concatenate([first_ref[...], second_ref[...]], axis=0)
    gate_val = dot(rows, gate_ref[...])
    up_val = dot(rows, up_ref[...])
    out_ref[...] = (gate_val / (1.0 + jnp.exp(-gate_val)) * up_val).astype(bf16)


def output_body(own_ref, other_ref, down_ref, far_ref, first_out, second_out):
    half = first_out.shape[0]
    hidden = jnp.concatenate([own_ref[...], other_ref[...]], axis=1)
    step = 4 * LANES
    for n in range(0, down_ref.shape[1], step):
        part = slice(n, n + step)
        weight = jnp.concatenate([down_ref[:, part], far_ref[:, part]], axis=0)
        value = dot(hidden, weight).astype(bf16)
        first_out[:, part] = value[:half]
        second_out[:, part] = value[half:]


def down_back_body(first_ref, second_ref, down_ref, far_ref, own_out, other_out):
    grads = jnp.concatenate([first_ref[...], second_ref[...]], axis=0)
    own_out[...] = dot_last(grads, down_ref[...]).astype(own_out.dtype)
    other_out[...] = dot_last(grads, far_ref[...]).astype(other_out.dtype)


def backward_body(first_ref, second_ref, back_ref, gate_ref, up_ref, first_out, second_out):
    half = first_ref.shape[0]
    rows = jnp.concatenate([first_ref[...], second_ref[...]], axis=0)
    gate_val = dot(rows, gate_ref[...])
    up_val = dot(rows, up_ref[...])
    down_back = back_ref[...].astype(f32)
    sigmoid_val = 1.0 / (1.0 + jnp.exp(-gate_val))
    slope_val = sigmoid_val * (1.0 + gate_val * (1.0 - sigmoid_val))
    gate_grad = (down_back * up_val * slope_val).astype(bf16)
    up_grad = (down_back * gate_val * sigmoid_val).astype(bf16)
    step = 4 * LANES
    for n in range(0, gate_ref.shape[0], step):
        value = dot_last(gate_grad, gate_ref[n : n + step])
        value = (value + dot_last(up_grad, up_ref[n : n + step])).astype(bf16)
        first_out[:, n : n + step] = value[:half]
        second_out[:, n : n + step] = value[half:]


def attend_body(
    experts,
    capacity,
    chosen_ref,
    index_ref,
    base_ref,
    route_ref,
    gain_ref,
    input_ref,
    query_ref,
    kv0,
    kv1,
    kv2,
    kv3,
    middle_ref,
    *refs,
):
    outs, (kv_all, kv_now, stack, attended) = refs[:experts], refs[experts:]
    tokens, width = query_ref.shape
    lead = 0
    for ref in (kv0, kv1, kv2, kv3):
        kv_all[lead : lead + ref.shape[0], : ref.shape[1]] = ref[...]
        lead += ref.shape[0]
    attended[...] = jnp.zeros_like(attended)
    heads_each = HEADS // KV_HEADS
    period = 8
    window = 2 * LANES
    keys = SEL * BLK
    lane = iota((keys, LANES), 1)
    batch = 4
    scale = HEAD_DIM**-0.5

    def one_block(block, _):
        top = pl.multiple_of(block * BLK, BLK)
        position = (base_ref[0] + block) * BLK + (iota((batch * BLK, keys), 0) & (BLK - 1))
        for head in range(KV_HEADS):
            key_pos = iota((1, keys), 1)
            shift = key_pos * 0
            for s in range(SEL):
                at = (block * KV_HEADS + head) * SEL + s
                start = pl.multiple_of(index_ref[at] * BLK, BLK)
                kv_now[s * BLK : (s + 1) * BLK, :] = kv_all[pl.ds(start, BLK), :].astype(f32)
                inside = (key_pos >= s * BLK) & (key_pos < (s + 1) * BLK)
                shift = jnp.where(inside, (chosen_ref[at] - s) * BLK, shift)
            allowed = key_pos + shift <= position
            sides = []
            for side in range(2):
                lead = (side * KV_HEADS + head) * HEAD_DIM
                tile = min(lead // LANES, 2)
                piece = kv_now[:, tile * LANES : tile * LANES + window]
                offset = lead - tile * LANES
                if offset:
                    piece = pltpu.roll(piece, window - offset, 1)
                sides.append(jnp.where(lane < HEAD_DIM, piece[:, :LANES], 0.0).astype(bf16))
            key_rows, value_rows = sides
            spots = []
            for j in range(heads_each):
                c = j % period
                tile = min(c * HEAD_DIM // LANES, period - 3)
                offset = c * HEAD_DIM - tile * LANES
                tile = tile + (j // period) * (period - 1) + head * heads_each * HEAD_DIM // LANES
                spots.append((tile * LANES, offset))
            for j, (lead, offset) in enumerate(spots):
                piece = query_ref[pl.ds(top, BLK), lead : lead + window].astype(f32)
                if offset:
                    piece = pltpu.roll(piece, window - offset, 1)
                stack[j * BLK : (j + 1) * BLK, :] = piece[:, :LANES].astype(bf16)
            for b in range(0, heads_each, batch):
                scores = dot_last(stack[b * BLK : (b + batch) * BLK, :], key_rows) * scale
                scores = jnp.where(allowed, scores, negative_large)
                exp_scores = jnp.exp(scores - jnp.max(scores, axis=-1, keepdims=True))
                total = jnp.sum(exp_scores, axis=-1, keepdims=True)
                mixed = dot((exp_scores / total).astype(bf16), value_rows)
                for i in range(batch):
                    lead, offset = spots[b + i]
                    piece = mixed[i * BLK : (i + 1) * BLK]
                    piece = jnp.concatenate([piece, jnp.zeros_like(piece)], axis=1)
                    if offset:
                        piece = pltpu.roll(piece, offset, 1)
                    spot = (pl.ds(top, BLK), slice(lead, lead + window))
                    attended[spot] = attended[spot] + piece
        return 0

    lax.fori_loop(0, tokens // BLK, one_block, 0)
    middle = (input_ref[...].astype(f32) + attended[...]).astype(bf16)
    middle_ref[...] = middle
    middle = middle.astype(f32)
    normed = (middle * rms_scale(middle) * gain_ref[...]).astype(bf16)
    pack_into(normed, place_across(route_ref[...], experts, capacity), outs, capacity)


def after(arrays, others):
    count = len(arrays)
    return list(lax.optimization_barrier(tuple(arrays) + tuple(others))[:count])


def shape_of(rows, columns, kind=bf16):
    return jax.ShapeDtypeStruct((rows, columns), kind)


def shards(
    front_input,
    queries,
    keys_values,
    selected_blocks,
    front_route,
    front_gate,
    back_middle,
    back_grad,
    back_route,
    back_gate,
    norm_gain,
    gate_slice,
    up_slice,
    down_slice,
):
    tokens, width = front_input.shape[1:]
    length = lax.axis_size("expert")
    experts = length // GROUP
    average = tokens // experts
    capacity = average + max(1, average // 8)
    slots = experts * capacity
    hidden_width = gate_slice.shape[3]
    w_gate, w_up, w_down = gate_slice[0, 0], up_slice[0, 0], down_slice[0, 0]
    me = lax.axis_index("expert")
    group = me // GROUP
    chunk = shape_of(PARTS * capacity, width // PARTS)
    piece = shape_of(slots, width)
    whole = shape_of(tokens, width)

    column = [keys_values[0]]
    for back in range(1, experts):
        pairs = [(i, i + back * GROUP) for i in range(length - back * GROUP)]
        column.append(lax.ppermute(keys_values[0], "expert", pairs))
    front_from = lax.rem(front_route[0] - group + experts, experts)
    back_from = lax.rem(back_route[0] - group + experts, experts)
    front_row, back_row = front_from.reshape(1, tokens), back_from.reshape(1, tokens)

    pack_flops = 4 * slots * PARTS * tokens * width
    packed = call(
        functools.partial(back_pack_body, experts, capacity),
        [chunk] * (2 * experts),
        (back_row, back_gate[0], norm_gain, back_middle[0], back_grad[0]),
        flops=2 * pack_flops,
    )
    column = after(column, [packed[0]])
    column = jnp.concatenate(column, axis=0)
    other_chip = swapped(column, 2)
    packed = after(packed, [column])

    front_small = jnp.concatenate([front_from.astype(f32), front_gate[0]], axis=0).reshape(1, -1)
    back_small = jnp.concatenate([back_from.astype(f32).reshape(1, -1), norm_gain], axis=1)

    def sent(chunks):
        return [chunks[0]] + [turned(chunks[k], k) for k in range(1, experts)]

    def joined(chunks):
        return call(functools.partial(join_body, capacity), piece, chunks, flops=pack_flops)

    def pieces_of(rows):
        other = swapped(rows, 2)
        return [rows, swapped(rows, 1), other, swapped(other, 1)]

    def split(parts):
        return call(
            functools.partial(split_body, capacity, len(parts)),
            [chunk] * experts,
            parts,
            flops=pack_flops,
        )

    def sent_back(chunks, by):
        return [passed_along(chunks[k], by, k) for k in range(experts)]

    row_chunks, grad_chunks = packed[:experts], packed[experts:]
    row_chunks[1] = turned(row_chunks[1], 1)
    arrived = [row_chunks[1]]
    down_other = swapped(after([w_down], [other_chip] + arrived)[0], 2)
    downs = (w_down, down_other)
    kv = [column, other_chip, swapped(column, 1), swapped(other_chip, 1)]
    for k in range(2, experts):
        row_chunks[k] = turned(after([row_chunks[k]], arrived)[0], k)
    there_back_middle = passed_along(after([back_middle[0]], [other_chip] + arrived)[0], -1)

    per_device = tokens // BLK
    chosen = selected_blocks[0].reshape(-1)
    owner = chosen // per_device
    place = (owner % GROUP) ^ (me % GROUP)
    place = (place % 2) * 2 + place // 2
    index = (place * experts + group - owner // GROUP) * per_device + chosen % per_device
    index = jnp.clip(index, 0, length * per_device - 1)
    base = (me * per_device).astype(jnp.int32).reshape(1)
    result = call(
        functools.partial(attend_body, experts, capacity),
        [whole] + [chunk] * experts,
        (chosen, index, base, front_row, norm_gain, front_input[0], queries[0], *kv),
        scratch=[
            pltpu.VMEM((length * tokens, 4 * LANES), bf16),
            pltpu.VMEM((SEL * BLK, 4 * LANES), f32),
            pltpu.VMEM((HEADS // KV_HEADS * BLK, LANES), bf16),
            pltpu.VMEM((tokens, width), f32),
        ],
        flops=pack_flops + 4 * tokens * HEADS * SEL * BLK * LANES,
        smem=3,
        vmem=VMEM_BYTES + 2 * length * tokens * 4 * LANES * 2,
    )
    middle, front_chunks = result[0], result[1:]
    front_chunks = sent(after(front_chunks, row_chunks))
    back_rows = joined(after(row_chunks, [middle, there_back_middle]))
    back_pieces = pieces_of(back_rows)
    for k in range(1, experts):
        grad_chunks[k] = turned(after([grad_chunks[k]], front_chunks)[0], k)
    front_near = joined(after(front_chunks, [back_pieces[2], down_other]))
    there_back_grad = passed_along(after([back_grad[0]], [front_near])[0], -1)
    front_other = after([swapped(front_near, 2)], [there_back_grad])[0]

    front_small, back_small = after([front_small, back_small], [front_near])
    there_small = passed_along(front_small, 1)
    there_back_small = passed_along(back_small, -1)
    there_front_from = there_small[0, :tokens].astype(jnp.int32).reshape(tokens, 1)
    there_front_gate = there_small[0, tokens:].reshape(tokens, 1)
    there_back_from = there_back_small[0, :tokens].astype(jnp.int32).reshape(tokens, 1)
    there_gain = there_back_small[:, tokens:]
    grad_near = joined(after(grad_chunks, [front_other]))
    grad_near = [grad_near, swapped(grad_near, 1)]

    work = 2 * 2 * slots * width * hidden_width
    pair = 2 * slots

    def hidden(rows):
        return call(
            hidden_body, shape_of(pair, hidden_width), (*rows, w_gate, w_up), flops=2 * work
        )

    def backward(rows, grads):
        return call(backward_body, [piece, piece], (*rows, grads, w_gate, w_up), flops=4 * work)

    there_middle = passed_along(after([middle], [front_other])[0], 1)
    front_pieces = [front_near, swapped(front_near, 1), front_other, swapped(front_other, 1)]
    hidden_near = hidden(front_pieces[:2])
    hidden_far = hidden(front_pieces[2:])
    hidden_other = swapped(hidden_far, 2)
    down_back, other_back = call(
        down_back_body,
        [shape_of(pair, hidden_width, f32), shape_of(pair, hidden_width)],
        (*after(grad_near, [there_small, there_back_small, hidden_far]), *downs),
        flops=2 * work,
    )
    far_back = swapped(other_back, 2)

    front_own, front_core = call(
        output_body, [piece, piece], (hidden_near, hidden_other, *downs), flops=2 * work
    )
    (far_back,) = after([far_back], [front_own])
    back_near = backward(back_pieces[:2], down_back)
    back_far = backward(back_pieces[2:], far_back)
    chip = back_far[0].astype(f32) + swapped(back_far[1], 1).astype(f32)
    (chip,) = after([chip.astype(bf16)], [hidden_other])
    back_shares = (back_near[0], swapped(back_near[1], 1), swapped(chip, 2))

    front_shares = (front_own, swapped(front_core, 1))
    front_chunks = split(front_shares)
    front_return = sent_back(front_chunks, 1)

    back_chunks = split(after(back_shares, front_chunks + [there_middle]))
    back_return = sent_back(back_chunks, -1)

    front_return = after(front_return, back_chunks)
    front_output = call(
        functools.partial(front_finish_body, experts, capacity),
        whole,
        (there_front_from, there_front_gate, there_middle, *front_return),
        flops=pack_flops,
    )
    back_return = after(back_return, [front_output])
    back_output = call(
        functools.partial(back_finish_body, experts, capacity),
        whole,
        (there_back_from, there_gain, there_back_middle, there_back_grad, *back_return),
        flops=pack_flops,
    )
    return (front_output[None], back_output[None])


def solution(mesh):
    placed = (
        P("section", "expert", None),
        P("section", "expert", None),
        P("section", "expert", None),
        P("section", "expert", None, None),
        P("section", "expert", None),
        P("section", "expert", None),
        P("section", "expert", None),
        P("section", "expert", None),
        P("section", "expert", None),
        P("section", "expert", None),
        P("section", None),
        P("section", "expert", None, None),
        P("section", "expert", None, None),
        P("section", "expert", None, None),
    )
    return jax.shard_map(
        shards,
        mesh=mesh,
        in_specs=placed,
        out_specs=(P("section", "expert", None), P("section", "expert", None)),
        check_vma=False,
    )
```

```python
import functools

import jax
import jax.numpy as jnp
from jax import lax
from jax.experimental import pallas as pl
from jax.experimental.pallas import tpu as pltpu
from jax.sharding import PartitionSpec as P

GROUP = 4
HEADS = 32
HEAD_DIM = 112
KV_HEADS = 2
BLK = 64
SEL = 4
PARTS = 4
LANES = 128
VMEM_BYTES = 28 * 1024 * 1024

epsilon = 1e-06
negative_large = -1e30
bf16 = jnp.bfloat16
f32 = jnp.float32


def passed_along(array, by, back=0):
    sections, length = lax.axis_size("section"), lax.axis_size("expert")
    pairs = [
        (s * length + i, (s + by) % sections * length + (i - back * GROUP) % length)
        for s in range(sections)
        for i in range(length)
    ]
    return lax.ppermute(array, ("section", "expert"), pairs)


def swapped(array, bit):
    return lax.ppermute(array, "expert", [(i, i ^ bit) for i in range(lax.axis_size("expert"))])


def turned(array, by):
    length = lax.axis_size("expert")
    return lax.ppermute(
        array, "expert", [(i, (i + by * GROUP) % length) for i in range(length)]
    )


def call(body, outs, args, scratch=(), flops=0, smem=0, vmem=VMEM_BYTES):
    specs = [
        pl.BlockSpec(memory_space=pltpu.SMEM if i < smem else pltpu.VMEM)
        for i in range(len(args))
    ]
    many = isinstance(outs, list)
    shapes = outs if many else [outs]
    moved_bytes = sum(a.size * a.dtype.itemsize for a in list(args) + shapes)
    result = pl.pallas_call(
        body,
        out_shape=shapes,
        in_specs=specs,
        out_specs=[pl.BlockSpec(memory_space=pltpu.VMEM) for _ in shapes],
        scratch_shapes=list(scratch),
        compiler_params=pltpu.CompilerParams(vmem_limit_bytes=vmem),
        cost_estimate=pl.CostEstimate(
            flops=int(flops), bytes_accessed=int(moved_bytes), transcendentals=0
        ),
    )(*args)
    return list(result) if many else result[0]


def dot(a, b):
    return jnp.dot(a, b, preferred_element_type=f32)


def dot_last(a, b):
    return lax.dot_general(a, b, (((1,), (1,)), ((), ())), preferred_element_type=f32)


def rms_scale(rows):
    return lax.rsqrt(jnp.mean(rows * rows, axis=-1, keepdims=True) + epsilon)


def iota(shape, dim):
    return lax.broadcasted_iota(jnp.int32, shape, dim)


def stacked(rows):
    width = rows.shape[1] // PARTS
    return jnp.concatenate([rows[:, p * width : (p + 1) * width] for p in range(PARTS)], axis=0)


def place_across(route_row, experts, capacity):
    tokens = route_row.shape[1]
    names = iota((max(8, experts), tokens), 0)
    onehot = jnp.where(names == route_row, 1.0, 0.0)
    earlier = jnp.where(iota((tokens, tokens), 0) < iota((tokens, tokens), 1), 1.0, 0.0)
    before = dot(onehot.astype(bf16), earlier.astype(bf16))
    place = onehot * (before + (names * (PARTS * capacity)).astype(f32))
    return jnp.sum(place, axis=0, keepdims=True).astype(jnp.int32)


def place_down(route_column, experts, capacity):
    tokens = route_column.shape[0]
    names = iota((tokens, LANES), 1)
    onehot = jnp.where(names == route_column, 1.0, 0.0)
    earlier = jnp.where(iota((tokens, tokens), 1) < iota((tokens, tokens), 0), 1.0, 0.0)
    before = dot(earlier.astype(bf16), onehot.astype(bf16))
    place = onehot * (before + (names * (PARTS * capacity)).astype(f32))
    return jnp.sum(place, axis=1, keepdims=True).astype(jnp.int32)


def pack_into(rows, place, out_refs, capacity):
    tokens = rows.shape[0]
    height = PARTS * capacity
    total = height * len(out_refs)
    places = jnp.concatenate([place + p * capacity for p in range(PARTS)], axis=1)
    pick = jnp.where(iota((total, PARTS * tokens), 0) == places, 1.0, 0.0).astype(bf16)
    packed = dot(pick, stacked(rows)).astype(bf16)
    for e, ref in enumerate(out_refs):
        ref[...] = packed[e * height : (e + 1) * height]


def back_pack_body(experts, capacity, route_ref, gate_ref, gain_ref, middle_ref, grad_ref, *outs):
    place = place_across(route_ref[...], experts, capacity)
    middle = middle_ref[...].astype(f32)
    normed = (middle * rms_scale(middle) * gain_ref[...]).astype(bf16)
    pack_into(normed, place, outs[:experts], capacity)
    scaled = (gate_ref[...] * grad_ref[...].astype(f32)).astype(bf16)
    pack_into(scaled, place, outs[experts:], capacity)


def join_body(capacity, *refs):
    chunks, out = refs[:-1], refs[-1]
    sources = len(chunks)
    height = PARTS * capacity
    rows = jnp.concatenate([ref[...] for ref in chunks], axis=0)
    slots = sources * capacity
    width = rows.shape[1]
    index = iota((slots, 1), 0)
    source = index * 0
    for s in range(1, sources):
        source = source + jnp.where(index >= s * capacity, 1, 0)
    first = index + source * (height - capacity)
    columns = iota((slots, rows.shape[0]), 1)
    for p in range(PARTS):
        pick = jnp.where(columns == first + p * capacity, 1.0, 0.0).astype(bf16)
        out[:, p * width : (p + 1) * width] = dot(pick, rows).astype(bf16)


def split_body(capacity, count_shares, *refs):
    shares, outs = refs[:count_shares], refs[count_shares:]
    total = shares[0][...].astype(f32)
    for ref in shares[1:]:
        total = total + ref[...].astype(f32)
    rows = stacked(total.astype(bf16))
    height = PARTS * capacity
    slots = shares[0].shape[0]
    count = height * len(outs)
    index = iota((count, 1), 0)
    group = index * 0
    source = index * 0
    for g in range(1, count // capacity):
        group = group + jnp.where(index >= g * capacity, 1, 0)
    for s in range(1, len(outs)):
        source = source + jnp.where(index >= s * height, 1, 0)
    part = group - source * PARTS
    place = part * slots + source * capacity + index - group * capacity
    pick = jnp.where(iota((count, PARTS * slots), 1) == place, 1.0, 0.0).astype(bf16)
    packed = dot(pick, rows).astype(bf16)
    for s, ref in enumerate(outs):
        ref[...] = packed[s * height : (s + 1) * height]


def unpacked(route_column, chunk_refs, experts, capacity):
    tokens = route_column.shape[0]
    place = place_down(route_column, experts, capacity)
    rows = jnp.concatenate([ref[...] for ref in chunk_refs], axis=0)
    columns = iota((tokens, rows.shape[0]), 1)
    parts = []
    for p in range(PARTS):
        pick = jnp.where(columns == place + p * capacity, 1.0, 0.0).astype(bf16)
        parts.append(dot(pick, rows))
    return jnp.concatenate(parts, axis=1)


def front_finish_body(experts, capacity, route_ref, gate_ref, middle_ref, *refs):
    chunks, out = refs[:-1], refs[-1]
    contrib = gate_ref[...] * unpacked(route_ref[...], chunks, experts, capacity)
    out[...] = (middle_ref[...].astype(f32) + contrib).astype(bf16)


def back_finish_body(experts, capacity, route_ref, gain_ref, middle_ref, grad_ref, *refs):
    chunks, out = refs[:-1], refs[-1]
    amount = gain_ref[...] * unpacked(route_ref[...], chunks, experts, capacity)
    middle = middle_ref[...].astype(f32)
    scale = rms_scale(middle)
    cube = scale * scale * scale
    mean = jnp.mean(middle * amount, axis=-1, keepdims=True)
    out[...] = (grad_ref[...].astype(f32) + scale * amount - middle * cube * mean).astype(bf16)


def hidden_body(first_ref, second_ref, gate_ref, up_ref, out_ref):
    rows = jnp.concatenate([first_ref[...], second_ref[...]], axis=0)
    gate_val = dot(rows, gate_ref[...])
    up_val = dot(rows, up_ref[...])
    out_ref[...] = (gate_val / (1.0 + jnp.exp(-gate_val)) * up_val).astype(bf16)


def output_body(own_ref, other_ref, down_ref, far_ref, first_out, second_out):
    half = first_out.shape[0]
    hidden = jnp.concatenate([own_ref[...], other_ref[...]], axis=1)
    step = 4 * LANES
    for n in range(0, down_ref.shape[1], step):
        part = slice(n, n + step)
        weight = jnp.concatenate([down_ref[:, part], far_ref[:, part]], axis=0)
        value = dot(hidden, weight).astype(bf16)
        first_out[:, part] = value[:half]
        second_out[:, part] = value[half:]


def down_back_body(first_ref, second_ref, down_ref, far_ref, own_out, other_out):
    grads = jnp.concatenate([first_ref[...], second_ref[...]], axis=0)
    own_out[...] = dot_last(grads, down_ref[...]).astype(own_out.dtype)
    other_out[...] = dot_last(grads, far_ref[...]).astype(other_out.dtype)


def backward_body(first_ref, second_ref, back_ref, gate_ref, up_ref, first_out, second_out):
    half = first_ref.shape[0]
    rows = jnp.concatenate([first_ref[...], second_ref[...]], axis=0)
    gate_val = dot(rows, gate_ref[...])
    up_val = dot(rows, up_ref[...])
    down_back = back_ref[...].astype(f32)
    sigmoid_val = 1.0 / (1.0 + jnp.exp(-gate_val))
    slope_val = sigmoid_val * (1.0 + gate_val * (1.0 - sigmoid_val))
    gate_grad = (down_back * up_val * slope_val).astype(bf16)
    up_grad = (down_back * gate_val * sigmoid_val).astype(bf16)
    step = 4 * LANES
    for n in range(0, gate_ref.shape[0], step):
        value = dot_last(gate_grad, gate_ref[n : n + step])
        value = (value + dot_last(up_grad, up_ref[n : n + step])).astype(bf16)
        first_out[:, n : n + step] = value[:half]
        second_out[:, n : n + step] = value[half:]


def attend_body(
    experts,
    capacity,
    chosen_ref,
    index_ref,
    base_ref,
    route_ref,
    gain_ref,
    input_ref,
    query_ref,
    kv0,
    kv1,
    kv2,
    kv3,
    middle_ref,
    *refs,
):
    outs, (kv_all, kv_now, stack, attended) = refs[:experts], refs[experts:]
    tokens, width = query_ref.shape
    lead = 0
    for ref in (kv0, kv1, kv2, kv3):
        kv_all[lead : lead + ref.shape[0], : ref.shape[1]] = ref[...]
        lead += ref.shape[0]
    attended[...] = jnp.zeros_like(attended)
    heads_each = HEADS // KV_HEADS
    period = 8
    window = 2 * LANES
    keys = SEL * BLK
    lane = iota((keys, LANES), 1)
    batch = 4
    scale = HEAD_DIM**-0.5

    def one_block(block, _):
        top = pl.multiple_of(block * BLK, BLK)
        position = (base_ref[0] + block) * BLK + (iota((batch * BLK, keys), 0) & (BLK - 1))
        for head in range(KV_HEADS):
            key_pos = iota((1, keys), 1)
            shift = key_pos * 0
            for s in range(SEL):
                at = (block * KV_HEADS + head) * SEL + s
                start = pl.multiple_of(index_ref[at] * BLK, BLK)
                kv_now[s * BLK : (s + 1) * BLK, :] = kv_all[pl.ds(start, BLK), :].astype(f32)
                inside = (key_pos >= s * BLK) & (key_pos < (s + 1) * BLK)
                shift = jnp.where(inside, (chosen_ref[at] - s) * BLK, shift)
            allowed = key_pos + shift <= position
            sides = []
            for side in range(2):
                lead = (side * KV_HEADS + head) * HEAD_DIM
                tile = min(lead // LANES, 2)
                piece = kv_now[:, tile * LANES : tile * LANES + window]
                offset = lead - tile * LANES
                if offset:
                    piece = pltpu.roll(piece, window - offset, 1)
                sides.append(jnp.where(lane < HEAD_DIM, piece[:, :LANES], 0.0).astype(bf16))
            key_rows, value_rows = sides
            spots = []
            for j in range(heads_each):
                c = j % period
                tile = min(c * HEAD_DIM // LANES, period - 3)
                offset = c * HEAD_DIM - tile * LANES
                tile = tile + (j // period) * (period - 1) + head * heads_each * HEAD_DIM // LANES
                spots.append((tile * LANES, offset))
            for j, (lead, offset) in enumerate(spots):
                piece = query_ref[pl.ds(top, BLK), lead : lead + window].astype(f32)
                if offset:
                    piece = pltpu.roll(piece, window - offset, 1)
                stack[j * BLK : (j + 1) * BLK, :] = piece[:, :LANES].astype(bf16)
            for b in range(0, heads_each, batch):
                scores = dot_last(stack[b * BLK : (b + batch) * BLK, :], key_rows) * scale
                scores = jnp.where(allowed, scores, negative_large)
                exp_scores = jnp.exp(scores - jnp.max(scores, axis=-1, keepdims=True))
                total = jnp.sum(exp_scores, axis=-1, keepdims=True)
                mixed = dot((exp_scores / total).astype(bf16), value_rows)
                for i in range(batch):
                    lead, offset = spots[b + i]
                    piece = mixed[i * BLK : (i + 1) * BLK]
                    piece = jnp.concatenate([piece, jnp.zeros_like(piece)], axis=1)
                    if offset:
                        piece = pltpu.roll(piece, offset, 1)
                    spot = (pl.ds(top, BLK), slice(lead, lead + window))
                    attended[spot] = attended[spot] + piece
        return 0

    lax.fori_loop(0, tokens // BLK, one_block, 0)
    middle = (input_ref[...].astype(f32) + attended[...]).astype(bf16)
    middle_ref[...] = middle
    middle = middle.astype(f32)
    normed = (middle * rms_scale(middle) * gain_ref[...]).astype(bf16)
    pack_into(normed, place_across(route_ref[...], experts, capacity), outs, capacity)


def after(arrays, others):
    count = len(arrays)
    return list(lax.optimization_barrier(tuple(arrays) + tuple(others))[:count])


def shape_of(rows, columns, kind=bf16):
    return jax.ShapeDtypeStruct((rows, columns), kind)


def shards(
    front_input,
    queries,
    keys_values,
    selected_blocks,
    front_route,
    front_gate,
    back_middle,
    back_grad,
    back_route,
    back_gate,
    norm_gain,
    gate_slice,
    up_slice,
    down_slice,
):
    tokens, width = front_input.shape[1:]
    length = lax.axis_size("expert")
    experts = length // GROUP
    average = tokens // experts
    capacity = average + max(1, average // 8)
    slots = experts * capacity
    hidden_width = gate_slice.shape[3]
    w_gate, w_up, w_down = gate_slice[0, 0], up_slice[0, 0], down_slice[0, 0]
    me = lax.axis_index("expert")
    group = me // GROUP
    chunk = shape_of(PARTS * capacity, width // PARTS)
    piece = shape_of(slots, width)
    whole = shape_of(tokens, width)

    column = [keys_values[0]]
    for back in range(1, experts):
        pairs = [(i, i + back * GROUP) for i in range(length - back * GROUP)]
        column.append(lax.ppermute(keys_values[0], "expert", pairs))
    front_from = lax.rem(front_route[0] - group + experts, experts)
    back_from = lax.rem(back_route[0] - group + experts, experts)
    front_row, back_row = front_from.reshape(1, tokens), back_from.reshape(1, tokens)

    pack_flops = 4 * slots * PARTS * tokens * width
    packed = call(
        functools.partial(back_pack_body, experts, capacity),
        [chunk] * (2 * experts),
        (back_row, back_gate[0], norm_gain, back_middle[0], back_grad[0]),
        flops=2 * pack_flops,
    )
    column = after(column, [packed[0]])
    column = jnp.concatenate(column, axis=0)
    other_chip = swapped(column, 2)
    packed = after(packed, [column])

    front_small = jnp.concatenate([front_from.astype(f32), front_gate[0]], axis=0).reshape(1, -1)
    back_small = jnp.concatenate([back_from.astype(f32).reshape(1, -1), norm_gain], axis=1)

    def sent(chunks):
        return [chunks[0]] + [turned(chunks[k], k) for k in range(1, experts)]

    def joined(chunks):
        return call(functools.partial(join_body, capacity), piece, chunks, flops=pack_flops)

    def pieces_of(rows):
        other = swapped(rows, 2)
        return [rows, swapped(rows, 1), other, swapped(other, 1)]

    def split(parts):
        return call(
            functools.partial(split_body, capacity, len(parts)),
            [chunk] * experts,
            parts,
            flops=pack_flops,
        )

    def sent_back(chunks, by):
        return [passed_along(chunks[k], by, k) for k in range(experts)]

    row_chunks, grad_chunks = packed[:experts], packed[experts:]
    row_chunks[1] = turned(row_chunks[1], 1)
    arrived = [row_chunks[1]]
    down_other = swapped(after([w_down], [other_chip] + arrived)[0], 2)
    downs = (w_down, down_other)
    kv = [column, other_chip, swapped(column, 1), swapped(other_chip, 1)]
    for k in range(2, experts):
        row_chunks[k] = turned(after([row_chunks[k]], arrived)[0], k)
    there_back_middle = passed_along(after([back_middle[0]], [other_chip] + arrived)[0], -1)

    per_device = tokens // BLK
    chosen = selected_blocks[0].reshape(-1)
    owner = chosen // per_device
    place = (owner % GROUP) ^ (me % GROUP)
    place = (place % 2) * 2 + place // 2
    index = (place * experts + group - owner // GROUP) * per_device + chosen % per_device
    index = jnp.clip(index, 0, length * per_device - 1)
    base = (me * per_device).astype(jnp.int32).reshape(1)
    result = call(
        functools.partial(attend_body, experts, capacity),
        [whole] + [chunk] * experts,
        (chosen, index, base, front_row, norm_gain, front_input[0], queries[0], *kv),
        scratch=[
            pltpu.VMEM((length * tokens, 4 * LANES), bf16),
            pltpu.VMEM((SEL * BLK, 4 * LANES), f32),
            pltpu.VMEM((HEADS // KV_HEADS * BLK, LANES), bf16),
            pltpu.VMEM((tokens, width), f32),
        ],
        flops=pack_flops + 4 * tokens * HEADS * SEL * BLK * LANES,
        smem=3,
        vmem=VMEM_BYTES + 2 * length * tokens * 4 * LANES * 2,
    )
    middle, front_chunks = result[0], result[1:]
    work = 2 * 2 * slots * width * hidden_width
    pair = 2 * slots

    def hidden(rows):
        return call(
            hidden_body, shape_of(pair, hidden_width), (*rows, w_gate, w_up), flops=2 * work
        )

    def backward(rows, grads):
        return call(backward_body, [piece, piece], (*rows, grads, w_gate, w_up), flops=4 * work)

    for k in range(1, experts):
        grad_chunks[k] = turned(after([grad_chunks[k]], [middle])[0], k)
    front_chunks = sent(after(front_chunks, row_chunks + grad_chunks[1:2]))
    back_rows = joined(after(row_chunks, [middle, there_back_middle]))
    back_pieces = pieces_of(back_rows)
    grad_near = joined(after(grad_chunks, [back_rows, down_other]))
    there_back_grad = passed_along(after([back_grad[0]], [grad_near])[0], -1)
    grad_near = [grad_near, swapped(grad_near, 1)]
    down_back, other_back = call(
        down_back_body,
        [shape_of(pair, hidden_width, f32), shape_of(pair, hidden_width)],
        (*grad_near, *downs),
        flops=2 * work,
    )
    far_back = swapped(other_back, 2)
    back_near = backward(back_pieces[:2], down_back)
    back_core = swapped(back_near[1], 1)
    front_near = joined(after(front_chunks, [back_pieces[2], there_back_grad, far_back, back_near[0]]))
    there_middle = passed_along(after([middle], [front_near])[0], 1)
    front_other = after([swapped(front_near, 2)], [there_middle])[0]

    front_small, back_small = after([front_small, back_small], [front_near])
    there_small = passed_along(front_small, 1)
    there_back_small = passed_along(back_small, -1)
    there_front_from = there_small[0, :tokens].astype(jnp.int32).reshape(tokens, 1)
    there_front_gate = there_small[0, tokens:].reshape(tokens, 1)
    there_back_from = there_back_small[0, :tokens].astype(jnp.int32).reshape(tokens, 1)
    there_gain = there_back_small[:, tokens:]
    front_pieces = [front_near, swapped(front_near, 1), front_other, swapped(front_other, 1)]
    hidden_near = hidden(front_pieces[:2])
    hidden_far = hidden(front_pieces[2:])
    hidden_other = swapped(hidden_far, 2)
    (hidden_other,) = after([hidden_other], [there_small, there_back_small])
    front_own, front_core = call(
        output_body, [piece, piece], (hidden_near, hidden_other, *downs), flops=2 * work
    )
    (far_back,) = after([far_back], [front_other])
    back_far = backward(back_pieces[2:], far_back)
    chip = back_far[0].astype(f32) + swapped(back_far[1], 1).astype(f32)
    (chip,) = after([chip.astype(bf16)], [hidden_other])
    back_shares = (back_near[0], back_core, swapped(chip, 2))

    front_shares = (front_own, swapped(front_core, 1))
    front_chunks = split(front_shares)
    front_return = sent_back(front_chunks, 1)

    back_chunks = split(after(back_shares, front_chunks))
    back_return = sent_back(back_chunks, -1)

    front_return = after(front_return, back_chunks)
    front_output = call(
        functools.partial(front_finish_body, experts, capacity),
        whole,
        (there_front_from, there_front_gate, there_middle, *front_return),
        flops=pack_flops,
    )
    back_return = after(back_return, [front_output])
    back_output = call(
        functools.partial(back_finish_body, experts, capacity),
        whole,
        (there_back_from, there_gain, there_back_middle, there_back_grad, *back_return),
        flops=pack_flops,
    )
    return (front_output[None], back_output[None])


def solution(mesh):
    placed = (
        P("section", "expert", None),
        P("section", "expert", None),
        P("section", "expert", None),
        P("section", "expert", None, None),
        P("section", "expert", None),
        P("section", "expert", None),
        P("section", "expert", None),
        P("section", "expert", None),
        P("section", "expert", None),
        P("section", "expert", None),
        P("section", None),
        P("section", "expert", None, None),
        P("section", "expert", None, None),
        P("section", "expert", None, None),
    )
    return jax.shard_map(
        shards,
        mesh=mesh,
        in_specs=placed,
        out_specs=(P("section", "expert", None), P("section", "expert", None)),
        check_vma=False,
    )
```

```python
import functools

import jax
import jax.numpy as jnp
from jax import lax
from jax.experimental import pallas as pl
from jax.experimental.pallas import tpu as pltpu
from jax.sharding import PartitionSpec as P

GROUP = 4
HEADS = 32
HEAD_DIM = 112
KV_HEADS = 2
BLK = 64
SEL = 4
PARTS = 4
LANES = 128
VMEM_BYTES = 28 * 1024 * 1024

epsilon = 1e-06
negative_large = -1e30
bf16 = jnp.bfloat16
f32 = jnp.float32


def passed_along(array, by, back=0):
    sections, length = lax.axis_size("section"), lax.axis_size("expert")
    pairs = [
        (s * length + i, (s + by) % sections * length + (i - back * GROUP) % length)
        for s in range(sections)
        for i in range(length)
    ]
    return lax.ppermute(array, ("section", "expert"), pairs)


def swapped(array, bit):
    return lax.ppermute(array, "expert", [(i, i ^ bit) for i in range(lax.axis_size("expert"))])


def turned(array, by):
    length = lax.axis_size("expert")
    return lax.ppermute(
        array, "expert", [(i, (i + by * GROUP) % length) for i in range(length)]
    )


def call(body, outs, args, scratch=(), flops=0, smem=0, vmem=VMEM_BYTES, cheap=False):
    specs = [
        pl.BlockSpec(memory_space=pltpu.SMEM if i < smem else pltpu.VMEM)
        for i in range(len(args))
    ]
    many = isinstance(outs, list)
    shapes = outs if many else [outs]
    moved_bytes = sum(a.size * a.dtype.itemsize for a in list(args) + shapes)
    result = pl.pallas_call(
        body,
        out_shape=shapes,
        in_specs=specs,
        out_specs=[pl.BlockSpec(memory_space=pltpu.VMEM) for _ in shapes],
        scratch_shapes=list(scratch),
        compiler_params=pltpu.CompilerParams(vmem_limit_bytes=vmem),
        cost_estimate=pl.CostEstimate(
            flops=1 if cheap else int(flops),
            bytes_accessed=1 if cheap else int(moved_bytes),
            transcendentals=0,
        ),
    )(*args)
    return list(result) if many else result[0]


def dot(a, b):
    return jnp.dot(a, b, preferred_element_type=f32)


def dot_last(a, b):
    return lax.dot_general(a, b, (((1,), (1,)), ((), ())), preferred_element_type=f32)


def rms_scale(rows):
    return lax.rsqrt(jnp.mean(rows * rows, axis=-1, keepdims=True) + epsilon)


def iota(shape, dim):
    return lax.broadcasted_iota(jnp.int32, shape, dim)


def stacked(rows):
    width = rows.shape[1] // PARTS
    return jnp.concatenate([rows[:, p * width : (p + 1) * width] for p in range(PARTS)], axis=0)


def place_across(route_row, experts, capacity):
    tokens = route_row.shape[1]
    names = iota((max(8, experts), tokens), 0)
    onehot = jnp.where(names == route_row, 1.0, 0.0)
    earlier = jnp.where(iota((tokens, tokens), 0) < iota((tokens, tokens), 1), 1.0, 0.0)
    before = dot(onehot.astype(bf16), earlier.astype(bf16))
    place = onehot * (before + (names * (PARTS * capacity)).astype(f32))
    return jnp.sum(place, axis=0, keepdims=True).astype(jnp.int32)


def place_down(route_column, experts, capacity):
    tokens = route_column.shape[0]
    names = iota((tokens, LANES), 1)
    onehot = jnp.where(names == route_column, 1.0, 0.0)
    earlier = jnp.where(iota((tokens, tokens), 1) < iota((tokens, tokens), 0), 1.0, 0.0)
    before = dot(earlier.astype(bf16), onehot.astype(bf16))
    place = onehot * (before + (names * (PARTS * capacity)).astype(f32))
    return jnp.sum(place, axis=1, keepdims=True).astype(jnp.int32)


def pack_into(rows, place, out_refs, capacity):
    tokens = rows.shape[0]
    height = PARTS * capacity
    total = height * len(out_refs)
    places = jnp.concatenate([place + p * capacity for p in range(PARTS)], axis=1)
    pick = jnp.where(iota((total, PARTS * tokens), 0) == places, 1.0, 0.0).astype(bf16)
    packed = dot(pick, stacked(rows)).astype(bf16)
    for e, ref in enumerate(out_refs):
        ref[...] = packed[e * height : (e + 1) * height]


def back_pack_body(experts, capacity, route_ref, gate_ref, gain_ref, middle_ref, grad_ref, *outs):
    place = place_across(route_ref[...], experts, capacity)
    middle = middle_ref[...].astype(f32)
    normed = (middle * rms_scale(middle) * gain_ref[...]).astype(bf16)
    pack_into(normed, place, outs[:experts], capacity)
    scaled = (gate_ref[...] * grad_ref[...].astype(f32)).astype(bf16)
    pack_into(scaled, place, outs[experts:], capacity)


def join_body(capacity, *refs):
    chunks, out = refs[:-1], refs[-1]
    sources = len(chunks)
    height = PARTS * capacity
    rows = jnp.concatenate([ref[...] for ref in chunks], axis=0)
    slots = sources * capacity
    width = rows.shape[1]
    index = iota((slots, 1), 0)
    source = index * 0
    for s in range(1, sources):
        source = source + jnp.where(index >= s * capacity, 1, 0)
    first = index + source * (height - capacity)
    columns = iota((slots, rows.shape[0]), 1)
    for p in range(PARTS):
        pick = jnp.where(columns == first + p * capacity, 1.0, 0.0).astype(bf16)
        out[:, p * width : (p + 1) * width] = dot(pick, rows).astype(bf16)


def split_body(capacity, count_shares, *refs):
    shares, outs = refs[:count_shares], refs[count_shares:]
    total = shares[0][...].astype(f32)
    for ref in shares[1:]:
        total = total + ref[...].astype(f32)
    rows = stacked(total.astype(bf16))
    height = PARTS * capacity
    slots = shares[0].shape[0]
    count = height * len(outs)
    index = iota((count, 1), 0)
    group = index * 0
    source = index * 0
    for g in range(1, count // capacity):
        group = group + jnp.where(index >= g * capacity, 1, 0)
    for s in range(1, len(outs)):
        source = source + jnp.where(index >= s * height, 1, 0)
    part = group - source * PARTS
    place = part * slots + source * capacity + index - group * capacity
    pick = jnp.where(iota((count, PARTS * slots), 1) == place, 1.0, 0.0).astype(bf16)
    packed = dot(pick, rows).astype(bf16)
    for s, ref in enumerate(outs):
        ref[...] = packed[s * height : (s + 1) * height]


def unpacked(route_column, chunk_refs, experts, capacity):
    tokens = route_column.shape[0]
    place = place_down(route_column, experts, capacity)
    rows = jnp.concatenate([ref[...] for ref in chunk_refs], axis=0)
    columns = iota((tokens, rows.shape[0]), 1)
    parts = []
    for p in range(PARTS):
        pick = jnp.where(columns == place + p * capacity, 1.0, 0.0).astype(bf16)
        parts.append(dot(pick, rows))
    return jnp.concatenate(parts, axis=1)


def front_finish_body(experts, capacity, route_ref, gate_ref, middle_ref, *refs):
    chunks, out = refs[:-1], refs[-1]
    contrib = gate_ref[...] * unpacked(route_ref[...], chunks, experts, capacity)
    out[...] = (middle_ref[...].astype(f32) + contrib).astype(bf16)


def back_finish_body(experts, capacity, route_ref, gain_ref, middle_ref, grad_ref, *refs):
    chunks, out = refs[:-1], refs[-1]
    amount = gain_ref[...] * unpacked(route_ref[...], chunks, experts, capacity)
    middle = middle_ref[...].astype(f32)
    scale = rms_scale(middle)
    cube = scale * scale * scale
    mean = jnp.mean(middle * amount, axis=-1, keepdims=True)
    out[...] = (grad_ref[...].astype(f32) + scale * amount - middle * cube * mean).astype(bf16)


def hidden_body(first_ref, second_ref, gate_ref, up_ref, out_ref):
    rows = jnp.concatenate([first_ref[...], second_ref[...]], axis=0)
    gate_val = dot(rows, gate_ref[...])
    up_val = dot(rows, up_ref[...])
    out_ref[...] = (gate_val / (1.0 + jnp.exp(-gate_val)) * up_val).astype(bf16)


def output_body(own_ref, other_ref, down_ref, far_ref, first_out, second_out):
    half = first_out.shape[0]
    hidden = jnp.concatenate([own_ref[...], other_ref[...]], axis=1)
    step = 4 * LANES
    for n in range(0, down_ref.shape[1], step):
        part = slice(n, n + step)
        weight = jnp.concatenate([down_ref[:, part], far_ref[:, part]], axis=0)
        value = dot(hidden, weight).astype(bf16)
        first_out[:, part] = value[:half]
        second_out[:, part] = value[half:]


def down_back_body(first_ref, second_ref, down_ref, far_ref, own_out, other_out):
    grads = jnp.concatenate([first_ref[...], second_ref[...]], axis=0)
    own_out[...] = dot_last(grads, down_ref[...]).astype(own_out.dtype)
    other_out[...] = dot_last(grads, far_ref[...]).astype(other_out.dtype)


def backward_body(first_ref, second_ref, back_ref, gate_ref, up_ref, first_out, second_out):
    half = first_ref.shape[0]
    rows = jnp.concatenate([first_ref[...], second_ref[...]], axis=0)
    gate_val = dot(rows, gate_ref[...])
    up_val = dot(rows, up_ref[...])
    down_back = back_ref[...].astype(f32)
    sigmoid_val = 1.0 / (1.0 + jnp.exp(-gate_val))
    slope_val = sigmoid_val * (1.0 + gate_val * (1.0 - sigmoid_val))
    gate_grad = (down_back * up_val * slope_val).astype(bf16)
    up_grad = (down_back * gate_val * sigmoid_val).astype(bf16)
    step = 4 * LANES
    for n in range(0, gate_ref.shape[0], step):
        value = dot_last(gate_grad, gate_ref[n : n + step])
        value = (value + dot_last(up_grad, up_ref[n : n + step])).astype(bf16)
        first_out[:, n : n + step] = value[:half]
        second_out[:, n : n + step] = value[half:]


def attend_body(
    experts,
    capacity,
    chosen_ref,
    index_ref,
    base_ref,
    route_ref,
    gain_ref,
    input_ref,
    query_ref,
    kv0,
    kv1,
    kv2,
    kv3,
    middle_ref,
    *refs,
):
    outs, (kv_all, kv_now, stack, attended) = refs[:experts], refs[experts:]
    tokens, width = query_ref.shape
    lead = 0
    for ref in (kv0, kv1, kv2, kv3):
        kv_all[lead : lead + ref.shape[0], : ref.shape[1]] = ref[...]
        lead += ref.shape[0]
    attended[...] = jnp.zeros_like(attended)
    heads_each = HEADS // KV_HEADS
    period = 8
    window = 2 * LANES
    keys = SEL * BLK
    lane = iota((keys, LANES), 1)
    batch = 4
    scale = HEAD_DIM**-0.5

    def one_block(block, _):
        top = pl.multiple_of(block * BLK, BLK)
        position = (base_ref[0] + block) * BLK + (iota((batch * BLK, keys), 0) & (BLK - 1))
        for head in range(KV_HEADS):
            key_pos = iota((1, keys), 1)
            shift = key_pos * 0
            for s in range(SEL):
                at = (block * KV_HEADS + head) * SEL + s
                start = pl.multiple_of(index_ref[at] * BLK, BLK)
                kv_now[s * BLK : (s + 1) * BLK, :] = kv_all[pl.ds(start, BLK), :].astype(f32)
                inside = (key_pos >= s * BLK) & (key_pos < (s + 1) * BLK)
                shift = jnp.where(inside, (chosen_ref[at] - s) * BLK, shift)
            allowed = key_pos + shift <= position
            sides = []
            for side in range(2):
                lead = (side * KV_HEADS + head) * HEAD_DIM
                tile = min(lead // LANES, 2)
                piece = kv_now[:, tile * LANES : tile * LANES + window]
                offset = lead - tile * LANES
                if offset:
                    piece = pltpu.roll(piece, window - offset, 1)
                sides.append(jnp.where(lane < HEAD_DIM, piece[:, :LANES], 0.0).astype(bf16))
            key_rows, value_rows = sides
            spots = []
            for j in range(heads_each):
                c = j % period
                tile = min(c * HEAD_DIM // LANES, period - 3)
                offset = c * HEAD_DIM - tile * LANES
                tile = tile + (j // period) * (period - 1) + head * heads_each * HEAD_DIM // LANES
                spots.append((tile * LANES, offset))
            for j, (lead, offset) in enumerate(spots):
                piece = query_ref[pl.ds(top, BLK), lead : lead + window].astype(f32)
                if offset:
                    piece = pltpu.roll(piece, window - offset, 1)
                stack[j * BLK : (j + 1) * BLK, :] = piece[:, :LANES].astype(bf16)
            for b in range(0, heads_each, batch):
                scores = dot_last(stack[b * BLK : (b + batch) * BLK, :], key_rows) * scale
                scores = jnp.where(allowed, scores, negative_large)
                exp_scores = jnp.exp(scores - jnp.max(scores, axis=-1, keepdims=True))
                total = jnp.sum(exp_scores, axis=-1, keepdims=True)
                mixed = dot((exp_scores / total).astype(bf16), value_rows)
                for i in range(batch):
                    lead, offset = spots[b + i]
                    piece = mixed[i * BLK : (i + 1) * BLK]
                    piece = jnp.concatenate([piece, jnp.zeros_like(piece)], axis=1)
                    if offset:
                        piece = pltpu.roll(piece, offset, 1)
                    spot = (pl.ds(top, BLK), slice(lead, lead + window))
                    attended[spot] = attended[spot] + piece
        return 0

    lax.fori_loop(0, tokens // BLK, one_block, 0)
    middle = (input_ref[...].astype(f32) + attended[...]).astype(bf16)
    middle_ref[...] = middle
    middle = middle.astype(f32)
    normed = (middle * rms_scale(middle) * gain_ref[...]).astype(bf16)
    pack_into(normed, place_across(route_ref[...], experts, capacity), outs, capacity)


def after(arrays, others):
    count = len(arrays)
    return list(lax.optimization_barrier(tuple(arrays) + tuple(others))[:count])


def shape_of(rows, columns, kind=bf16):
    return jax.ShapeDtypeStruct((rows, columns), kind)


def shards(
    front_input,
    queries,
    keys_values,
    selected_blocks,
    front_route,
    front_gate,
    back_middle,
    back_grad,
    back_route,
    back_gate,
    norm_gain,
    gate_slice,
    up_slice,
    down_slice,
):
    tokens, width = front_input.shape[1:]
    length = lax.axis_size("expert")
    experts = length // GROUP
    average = tokens // experts
    capacity = average + max(1, average // 8)
    slots = experts * capacity
    hidden_width = gate_slice.shape[3]
    w_gate, w_up, w_down = gate_slice[0, 0], up_slice[0, 0], down_slice[0, 0]
    me = lax.axis_index("expert")
    group = me // GROUP
    chunk = shape_of(PARTS * capacity, width // PARTS)
    piece = shape_of(slots, width)
    whole = shape_of(tokens, width)

    column = [keys_values[0]]
    for back in range(1, experts):
        pairs = [(i, i + back * GROUP) for i in range(length - back * GROUP)]
        column.append(lax.ppermute(keys_values[0], "expert", pairs))
    front_from = lax.rem(front_route[0] - group + experts, experts)
    back_from = lax.rem(back_route[0] - group + experts, experts)
    front_row, back_row = front_from.reshape(1, tokens), back_from.reshape(1, tokens)

    pack_flops = 4 * slots * PARTS * tokens * width
    packed = call(
        functools.partial(back_pack_body, experts, capacity),
        [chunk] * (2 * experts),
        (back_row, back_gate[0], norm_gain, back_middle[0], back_grad[0]),
        flops=2 * pack_flops,
    )
    column = after(column, [packed[0]])
    column = jnp.concatenate(column, axis=0)
    other_chip = swapped(column, 2)
    packed = after(packed, [column])

    front_small = jnp.concatenate([front_from.astype(f32), front_gate[0]], axis=0).reshape(1, -1)
    back_small = jnp.concatenate([back_from.astype(f32).reshape(1, -1), norm_gain], axis=1)

    def sent(chunks):
        return [chunks[0]] + [turned(chunks[k], k) for k in range(1, experts)]

    def joined(chunks):
        return call(functools.partial(join_body, capacity), piece, chunks, flops=pack_flops)

    def pieces_of(rows):
        other = swapped(rows, 2)
        return [rows, swapped(rows, 1), other, swapped(other, 1)]

    def split(parts):
        return call(
            functools.partial(split_body, capacity, len(parts)),
            [chunk] * experts,
            parts,
            cheap=True,
        )

    def sent_back(chunks, by):
        return [passed_along(chunks[k], by, k) for k in range(experts)]

    row_chunks, grad_chunks = packed[:experts], packed[experts:]
    row_chunks[1] = turned(row_chunks[1], 1)
    arrived = [row_chunks[1]]
    down_other = swapped(after([w_down], [other_chip] + arrived)[0], 2)
    downs = (w_down, down_other)
    kv = [column, other_chip, swapped(column, 1), swapped(other_chip, 1)]
    for k in range(2, experts):
        row_chunks[k] = turned(after([row_chunks[k]], arrived)[0], k)
    there_back_middle = passed_along(after([back_middle[0]], [other_chip] + arrived)[0], -1)

    per_device = tokens // BLK
    chosen = selected_blocks[0].reshape(-1)
    owner = chosen // per_device
    place = (owner % GROUP) ^ (me % GROUP)
    place = (place % 2) * 2 + place // 2
    index = (place * experts + group - owner // GROUP) * per_device + chosen % per_device
    index = jnp.clip(index, 0, length * per_device - 1)
    base = (me * per_device).astype(jnp.int32).reshape(1)
    result = call(
        functools.partial(attend_body, experts, capacity),
        [whole] + [chunk] * experts,
        (chosen, index, base, front_row, norm_gain, front_input[0], queries[0], *kv),
        scratch=[
            pltpu.VMEM((length * tokens, 4 * LANES), bf16),
            pltpu.VMEM((SEL * BLK, 4 * LANES), f32),
            pltpu.VMEM((HEADS // KV_HEADS * BLK, LANES), bf16),
            pltpu.VMEM((tokens, width), f32),
        ],
        flops=pack_flops + 4 * tokens * HEADS * SEL * BLK * LANES,
        smem=3,
        vmem=VMEM_BYTES + 2 * length * tokens * 4 * LANES * 2,
    )
    middle, front_chunks = result[0], result[1:]
    work = 2 * 2 * slots * width * hidden_width
    pair = 2 * slots

    def hidden(rows):
        return call(
            hidden_body, shape_of(pair, hidden_width), (*rows, w_gate, w_up), flops=2 * work
        )

    def backward(rows, grads):
        return call(backward_body, [piece, piece], (*rows, grads, w_gate, w_up), flops=4 * work)

    for k in range(1, experts):
        grad_chunks[k] = turned(after([grad_chunks[k]], [middle])[0], k)
    front_chunks = sent(after(front_chunks, row_chunks + grad_chunks[1:2]))
    back_rows = joined(after(row_chunks, [middle, there_back_middle]))
    back_other = swapped(back_rows, 2)
    grad_near = joined(after(grad_chunks, [back_rows, down_other]))
    there_back_grad = passed_along(after([back_grad[0]], [grad_near])[0], -1)
    grad_near = [grad_near, swapped(grad_near, 1)]
    down_back, other_back = call(
        down_back_body,
        [shape_of(pair, hidden_width, f32), shape_of(pair, hidden_width)],
        (*grad_near, *downs),
        flops=2 * work,
    )
    far_back = swapped(other_back, 2)
    back_near = backward((back_rows, swapped(back_rows, 1)), down_back)
    back_core = swapped(back_near[1], 1)
    ready = [back_other, there_back_grad, far_back, back_near[0]]
    front_near = joined(after(front_chunks, ready))
    there_middle = passed_along(after([middle], [front_near])[0], 1)
    (far_back,) = after([far_back], [there_middle])
    back_far = backward((back_other, swapped(after([back_other], [front_near])[0], 1)), far_back)
    chip = (back_far[0].astype(f32) + swapped(back_far[1], 1).astype(f32)).astype(bf16)
    front_other = after([swapped(front_near, 2)], back_far[:1])[0]

    front_small, back_small = after([front_small, back_small], [front_near])
    there_small = passed_along(front_small, 1)
    there_back_small = passed_along(back_small, -1)
    there_front_from = there_small[0, :tokens].astype(jnp.int32).reshape(tokens, 1)
    there_front_gate = there_small[0, tokens:].reshape(tokens, 1)
    there_back_from = there_back_small[0, :tokens].astype(jnp.int32).reshape(tokens, 1)
    there_gain = there_back_small[:, tokens:]
    front_pieces = [front_near, swapped(front_near, 1), front_other, swapped(front_other, 1)]
    hidden_near = hidden(front_pieces[:2])
    hidden_far = hidden(front_pieces[2:])
    hidden_other = swapped(hidden_far, 2)
    (hidden_other,) = after([hidden_other], [there_small, there_back_small, chip])
    front_own, front_core = call(
        output_body, [piece, piece], (hidden_near, hidden_other, *downs), cheap=True
    )
    (chip,) = after([chip], [hidden_far])
    back_shares = (back_near[0], back_core, swapped(chip, 2))

    front_shares = (front_own, swapped(front_core, 1))
    front_chunks = split(front_shares)
    front_return = sent_back(front_chunks, 1)

    back_chunks = split(after(back_shares, front_chunks))
    back_return = sent_back(back_chunks, -1)

    front_return = after(front_return, back_chunks)
    front_output = call(
        functools.partial(front_finish_body, experts, capacity),
        whole,
        (there_front_from, there_front_gate, there_middle, *front_return),
        flops=pack_flops,
    )
    back_return = after(back_return, [front_output])
    back_output = call(
        functools.partial(back_finish_body, experts, capacity),
        whole,
        (there_back_from, there_gain, there_back_middle, there_back_grad, *back_return),
        flops=pack_flops,
    )
    return (front_output[None], back_output[None])


def solution(mesh):
    placed = (
        P("section", "expert", None),
        P("section", "expert", None),
        P("section", "expert", None),
        P("section", "expert", None, None),
        P("section", "expert", None),
        P("section", "expert", None),
        P("section", "expert", None),
        P("section", "expert", None),
        P("section", "expert", None),
        P("section", "expert", None),
        P("section", None),
        P("section", "expert", None, None),
        P("section", "expert", None, None),
        P("section", "expert", None, None),
    )
    return jax.shard_map(
        shards,
        mesh=mesh,
        in_specs=placed,
        out_specs=(P("section", "expert", None), P("section", "expert", None)),
        check_vma=False,
    )
```

```python
import functools

import jax
import jax.numpy as jnp
from jax import lax
from jax.experimental import pallas as pl
from jax.experimental.pallas import tpu as pltpu
from jax.sharding import PartitionSpec as P

GROUP = 4
HEADS = 32
HEAD_DIM = 112
KV_HEADS = 2
BLK = 64
SEL = 4
PARTS = 4
LANES = 128
VMEM_BYTES = 28 * 1024 * 1024

epsilon = 1e-06
negative_large = -1e30
bf16 = jnp.bfloat16
f32 = jnp.float32


def passed_along(array, by, back=0):
    sections, length = lax.axis_size("section"), lax.axis_size("expert")
    pairs = [
        (s * length + i, (s + by) % sections * length + (i - back * GROUP) % length)
        for s in range(sections)
        for i in range(length)
    ]
    return lax.ppermute(array, ("section", "expert"), pairs)


def swapped(array, bit):
    return lax.ppermute(array, "expert", [(i, i ^ bit) for i in range(lax.axis_size("expert"))])


def turned(array, by):
    length = lax.axis_size("expert")
    return lax.ppermute(
        array, "expert", [(i, (i + by * GROUP) % length) for i in range(length)]
    )


def call(body, outs, args, scratch=(), flops=0, smem=0, vmem=VMEM_BYTES, cheap=False):
    specs = [
        pl.BlockSpec(memory_space=pltpu.SMEM if i < smem else pltpu.VMEM)
        for i in range(len(args))
    ]
    many = isinstance(outs, list)
    shapes = outs if many else [outs]
    moved_bytes = sum(a.size * a.dtype.itemsize for a in list(args) + shapes)
    result = pl.pallas_call(
        body,
        out_shape=shapes,
        in_specs=specs,
        out_specs=[pl.BlockSpec(memory_space=pltpu.VMEM) for _ in shapes],
        scratch_shapes=list(scratch),
        compiler_params=pltpu.CompilerParams(vmem_limit_bytes=vmem),
        cost_estimate=pl.CostEstimate(
            flops=1 if cheap else int(flops),
            bytes_accessed=1 if cheap else int(moved_bytes),
            transcendentals=0,
        ),
    )(*args)
    return list(result) if many else result[0]


def dot(a, b):
    return jnp.dot(a, b, preferred_element_type=f32)


def dot_last(a, b):
    return lax.dot_general(a, b, (((1,), (1,)), ((), ())), preferred_element_type=f32)


def rms_scale(rows):
    return lax.rsqrt(jnp.mean(rows * rows, axis=-1, keepdims=True) + epsilon)


def iota(shape, dim):
    return lax.broadcasted_iota(jnp.int32, shape, dim)


def stacked(rows):
    width = rows.shape[1] // PARTS
    return jnp.concatenate([rows[:, p * width : (p + 1) * width] for p in range(PARTS)], axis=0)


def place_across(route_row, experts, capacity):
    tokens = route_row.shape[1]
    names = iota((max(8, experts), tokens), 0)
    onehot = jnp.where(names == route_row, 1.0, 0.0)
    earlier = jnp.where(iota((tokens, tokens), 0) < iota((tokens, tokens), 1), 1.0, 0.0)
    before = dot(onehot.astype(bf16), earlier.astype(bf16))
    place = onehot * (before + (names * (PARTS * capacity)).astype(f32))
    return jnp.sum(place, axis=0, keepdims=True).astype(jnp.int32)


def place_down(route_column, experts, capacity):
    tokens = route_column.shape[0]
    names = iota((tokens, LANES), 1)
    onehot = jnp.where(names == route_column, 1.0, 0.0)
    earlier = jnp.where(iota((tokens, tokens), 1) < iota((tokens, tokens), 0), 1.0, 0.0)
    before = dot(earlier.astype(bf16), onehot.astype(bf16))
    place = onehot * (before + (names * (PARTS * capacity)).astype(f32))
    return jnp.sum(place, axis=1, keepdims=True).astype(jnp.int32)


def pack_into(rows, place, out_refs, capacity):
    tokens = rows.shape[0]
    height = PARTS * capacity
    total = height * len(out_refs)
    places = jnp.concatenate([place + p * capacity for p in range(PARTS)], axis=1)
    pick = jnp.where(iota((total, PARTS * tokens), 0) == places, 1.0, 0.0).astype(bf16)
    packed = dot(pick, stacked(rows)).astype(bf16)
    for e, ref in enumerate(out_refs):
        ref[...] = packed[e * height : (e + 1) * height]


def back_pack_body(experts, capacity, route_ref, gate_ref, gain_ref, middle_ref, grad_ref, *outs):
    place = place_across(route_ref[...], experts, capacity)
    middle = middle_ref[...].astype(f32)
    normed = (middle * rms_scale(middle) * gain_ref[...]).astype(bf16)
    pack_into(normed, place, outs[:experts], capacity)
    scaled = (gate_ref[...] * grad_ref[...].astype(f32)).astype(bf16)
    pack_into(scaled, place, outs[experts:], capacity)


def join_body(capacity, *refs):
    chunks, out = refs[:-1], refs[-1]
    sources = len(chunks)
    height = PARTS * capacity
    rows = jnp.concatenate([ref[...] for ref in chunks], axis=0)
    slots = sources * capacity
    width = rows.shape[1]
    index = iota((slots, 1), 0)
    source = index * 0
    for s in range(1, sources):
        source = source + jnp.where(index >= s * capacity, 1, 0)
    first = index + source * (height - capacity)
    columns = iota((slots, rows.shape[0]), 1)
    for p in range(PARTS):
        pick = jnp.where(columns == first + p * capacity, 1.0, 0.0).astype(bf16)
        out[:, p * width : (p + 1) * width] = dot(pick, rows).astype(bf16)


def split_body(capacity, count_shares, *refs):
    shares, outs = refs[:count_shares], refs[count_shares:]
    total = shares[0][...].astype(f32)
    for ref in shares[1:]:
        total = total + ref[...].astype(f32)
    rows = stacked(total.astype(bf16))
    height = PARTS * capacity
    slots = shares[0].shape[0]
    count = height * len(outs)
    index = iota((count, 1), 0)
    group = index * 0
    source = index * 0
    for g in range(1, count // capacity):
        group = group + jnp.where(index >= g * capacity, 1, 0)
    for s in range(1, len(outs)):
        source = source + jnp.where(index >= s * height, 1, 0)
    part = group - source * PARTS
    place = part * slots + source * capacity + index - group * capacity
    pick = jnp.where(iota((count, PARTS * slots), 1) == place, 1.0, 0.0).astype(bf16)
    packed = dot(pick, rows).astype(bf16)
    for s, ref in enumerate(outs):
        ref[...] = packed[s * height : (s + 1) * height]


def unpacked(route_column, chunk_refs, experts, capacity):
    tokens = route_column.shape[0]
    place = place_down(route_column, experts, capacity)
    rows = jnp.concatenate([ref[...] for ref in chunk_refs], axis=0)
    columns = iota((tokens, rows.shape[0]), 1)
    parts = []
    for p in range(PARTS):
        pick = jnp.where(columns == place + p * capacity, 1.0, 0.0).astype(bf16)
        parts.append(dot(pick, rows))
    return jnp.concatenate(parts, axis=1)


def front_finish_body(experts, capacity, route_ref, gate_ref, middle_ref, *refs):
    chunks, out = refs[:-1], refs[-1]
    contrib = gate_ref[...] * unpacked(route_ref[...], chunks, experts, capacity)
    out[...] = (middle_ref[...].astype(f32) + contrib).astype(bf16)


def back_finish_body(experts, capacity, route_ref, gain_ref, middle_ref, grad_ref, *refs):
    chunks, out = refs[:-1], refs[-1]
    amount = gain_ref[...] * unpacked(route_ref[...], chunks, experts, capacity)
    middle = middle_ref[...].astype(f32)
    scale = rms_scale(middle)
    cube = scale * scale * scale
    mean = jnp.mean(middle * amount, axis=-1, keepdims=True)
    out[...] = (grad_ref[...].astype(f32) + scale * amount - middle * cube * mean).astype(bf16)


def hidden_body(first_ref, second_ref, gate_ref, up_ref, out_ref):
    rows = jnp.concatenate([first_ref[...], second_ref[...]], axis=0)
    gate_val = dot(rows, gate_ref[...])
    up_val = dot(rows, up_ref[...])
    out_ref[...] = (gate_val / (1.0 + jnp.exp(-gate_val)) * up_val).astype(bf16)


def output_body(own_ref, other_ref, down_ref, top_ref, low_ref, first_out, second_out):
    half = first_out.shape[0]
    hidden = jnp.concatenate([own_ref[...], other_ref[...]], axis=1)
    step = 4 * LANES
    for n in range(0, down_ref.shape[1], step):
        part = slice(n, n + step)
        weight = jnp.concatenate([down_ref[:, part], top_ref[:, part], low_ref[:, part]], axis=0)
        value = dot(hidden, weight).astype(bf16)
        first_out[:, part] = value[:half]
        second_out[:, part] = value[half:]


def down_back_body(first_ref, second_ref, down_ref, top_ref, low_ref, own_out, other_out):
    grads = jnp.concatenate([first_ref[...], second_ref[...]], axis=0)
    own_out[...] = dot_last(grads, down_ref[...]).astype(own_out.dtype)
    far = jnp.concatenate([top_ref[...], low_ref[...]], axis=0)
    other_out[...] = dot_last(grads, far).astype(other_out.dtype)


def backward_body(first_ref, second_ref, back_ref, gate_ref, up_ref, first_out, second_out):
    half = first_ref.shape[0]
    rows = jnp.concatenate([first_ref[...], second_ref[...]], axis=0)
    gate_val = dot(rows, gate_ref[...])
    up_val = dot(rows, up_ref[...])
    down_back = back_ref[...].astype(f32)
    sigmoid_val = 1.0 / (1.0 + jnp.exp(-gate_val))
    slope_val = sigmoid_val * (1.0 + gate_val * (1.0 - sigmoid_val))
    gate_grad = (down_back * up_val * slope_val).astype(bf16)
    up_grad = (down_back * gate_val * sigmoid_val).astype(bf16)
    step = 4 * LANES
    for n in range(0, gate_ref.shape[0], step):
        value = dot_last(gate_grad, gate_ref[n : n + step])
        value = (value + dot_last(up_grad, up_ref[n : n + step])).astype(bf16)
        first_out[:, n : n + step] = value[:half]
        second_out[:, n : n + step] = value[half:]


def attend_body(
    experts,
    capacity,
    chosen_ref,
    index_ref,
    base_ref,
    route_ref,
    gain_ref,
    input_ref,
    query_ref,
    kv0,
    kv1,
    kv2,
    kv3,
    middle_ref,
    *refs,
):
    outs, (kv_all, kv_now, stack, attended) = refs[:experts], refs[experts:]
    tokens, width = query_ref.shape
    lead = 0
    for ref in (kv0, kv1, kv2, kv3):
        kv_all[lead : lead + ref.shape[0], : ref.shape[1]] = ref[...]
        lead += ref.shape[0]
    attended[...] = jnp.zeros_like(attended)
    heads_each = HEADS // KV_HEADS
    period = 8
    window = 2 * LANES
    keys = SEL * BLK
    lane = iota((keys, LANES), 1)
    batch = 4
    scale = HEAD_DIM**-0.5

    def one_block(block, _):
        top = pl.multiple_of(block * BLK, BLK)
        position = (base_ref[0] + block) * BLK + (iota((batch * BLK, keys), 0) & (BLK - 1))
        for head in range(KV_HEADS):
            key_pos = iota((1, keys), 1)
            shift = key_pos * 0
            for s in range(SEL):
                at = (block * KV_HEADS + head) * SEL + s
                start = pl.multiple_of(index_ref[at] * BLK, BLK)
                kv_now[s * BLK : (s + 1) * BLK, :] = kv_all[pl.ds(start, BLK), :].astype(f32)
                inside = (key_pos >= s * BLK) & (key_pos < (s + 1) * BLK)
                shift = jnp.where(inside, (chosen_ref[at] - s) * BLK, shift)
            allowed = key_pos + shift <= position
            sides = []
            for side in range(2):
                lead = (side * KV_HEADS + head) * HEAD_DIM
                tile = min(lead // LANES, 2)
                piece = kv_now[:, tile * LANES : tile * LANES + window]
                offset = lead - tile * LANES
                if offset:
                    piece = pltpu.roll(piece, window - offset, 1)
                sides.append(jnp.where(lane < HEAD_DIM, piece[:, :LANES], 0.0).astype(bf16))
            key_rows, value_rows = sides
            spots = []
            for j in range(heads_each):
                c = j % period
                tile = min(c * HEAD_DIM // LANES, period - 3)
                offset = c * HEAD_DIM - tile * LANES
                tile = tile + (j // period) * (period - 1) + head * heads_each * HEAD_DIM // LANES
                spots.append((tile * LANES, offset))
            for j, (lead, offset) in enumerate(spots):
                piece = query_ref[pl.ds(top, BLK), lead : lead + window].astype(f32)
                if offset:
                    piece = pltpu.roll(piece, window - offset, 1)
                stack[j * BLK : (j + 1) * BLK, :] = piece[:, :LANES].astype(bf16)
            for b in range(0, heads_each, batch):
                scores = dot_last(stack[b * BLK : (b + batch) * BLK, :], key_rows) * scale
                scores = jnp.where(allowed, scores, negative_large)
                exp_scores = jnp.exp(scores - jnp.max(scores, axis=-1, keepdims=True))
                total = jnp.sum(exp_scores, axis=-1, keepdims=True)
                mixed = dot((exp_scores / total).astype(bf16), value_rows)
                for i in range(batch):
                    lead, offset = spots[b + i]
                    piece = mixed[i * BLK : (i + 1) * BLK]
                    piece = jnp.concatenate([piece, jnp.zeros_like(piece)], axis=1)
                    if offset:
                        piece = pltpu.roll(piece, offset, 1)
                    spot = (pl.ds(top, BLK), slice(lead, lead + window))
                    attended[spot] = attended[spot] + piece
        return 0

    lax.fori_loop(0, tokens // BLK, one_block, 0)
    middle = (input_ref[...].astype(f32) + attended[...]).astype(bf16)
    middle_ref[...] = middle
    middle = middle.astype(f32)
    normed = (middle * rms_scale(middle) * gain_ref[...]).astype(bf16)
    pack_into(normed, place_across(route_ref[...], experts, capacity), outs, capacity)


def after(arrays, others):
    count = len(arrays)
    return list(lax.optimization_barrier(tuple(arrays) + tuple(others))[:count])


def shape_of(rows, columns, kind=bf16):
    return jax.ShapeDtypeStruct((rows, columns), kind)


def shards(
    front_input,
    queries,
    keys_values,
    selected_blocks,
    front_route,
    front_gate,
    back_middle,
    back_grad,
    back_route,
    back_gate,
    norm_gain,
    gate_slice,
    up_slice,
    down_slice,
):
    tokens, width = front_input.shape[1:]
    length = lax.axis_size("expert")
    experts = length // GROUP
    average = tokens // experts
    capacity = average + max(1, average // 8)
    slots = experts * capacity
    hidden_width = gate_slice.shape[3]
    w_gate, w_up, w_down = gate_slice[0, 0], up_slice[0, 0], down_slice[0, 0]
    me = lax.axis_index("expert")
    group = me // GROUP
    chunk = shape_of(PARTS * capacity, width // PARTS)
    piece = shape_of(slots, width)
    whole = shape_of(tokens, width)

    column = [keys_values[0]]
    for back in range(1, experts):
        pairs = [(i, i + back * GROUP) for i in range(length - back * GROUP)]
        column.append(lax.ppermute(keys_values[0], "expert", pairs))
    front_from = lax.rem(front_route[0] - group + experts, experts)
    back_from = lax.rem(back_route[0] - group + experts, experts)
    front_row, back_row = front_from.reshape(1, tokens), back_from.reshape(1, tokens)

    pack_flops = 4 * slots * PARTS * tokens * width
    packed = call(
        functools.partial(back_pack_body, experts, capacity),
        [chunk] * (2 * experts),
        (back_row, back_gate[0], norm_gain, back_middle[0], back_grad[0]),
        flops=2 * pack_flops,
    )
    column = after(column, [packed[0]])
    column = jnp.concatenate(column, axis=0)
    other_chip = swapped(column, 2)
    packed = after(packed, [column])

    front_small = jnp.concatenate([front_from.astype(f32), front_gate[0]], axis=0).reshape(1, -1)
    back_small = jnp.concatenate([back_from.astype(f32).reshape(1, -1), norm_gain], axis=1)

    def sent(chunks):
        return [chunks[0]] + [turned(chunks[k], k) for k in range(1, experts)]

    def joined(chunks):
        return call(functools.partial(join_body, capacity), piece, chunks, flops=pack_flops)

    def pieces_of(rows):
        other = swapped(rows, 2)
        return [rows, swapped(rows, 1), other, swapped(other, 1)]

    def split(parts):
        return call(
            functools.partial(split_body, capacity, len(parts)),
            [chunk] * experts,
            parts,
            cheap=True,
        )

    def sent_back(chunks, by):
        return [passed_along(chunks[k], by, k) for k in range(experts)]

    row_chunks, grad_chunks = packed[:experts], packed[experts:]
    first = 1 + 2 * (experts - 1) // 3
    for k in range(1, first):
        row_chunks[k] = turned(row_chunks[k], k)
    arrived = row_chunks[1:first]
    cut = hidden_width * 5 // 8
    (down_top,) = after([w_down[:cut]], arrived[:1])
    down_top = swapped(down_top, 2)
    there_back_middle = passed_along(after([back_middle[0]], arrived)[0], -1)
    far = swapped(after([other_chip], arrived)[0], 1)
    kv = [column, other_chip, swapped(column, 1), far]
    for k in range(first, experts):
        row_chunks[k] = turned(after([row_chunks[k]], arrived)[0], k)

    per_device = tokens // BLK
    chosen = selected_blocks[0].reshape(-1)
    owner = chosen // per_device
    place = (owner % GROUP) ^ (me % GROUP)
    place = (place % 2) * 2 + place // 2
    index = (place * experts + group - owner // GROUP) * per_device + chosen % per_device
    index = jnp.clip(index, 0, length * per_device - 1)
    base = (me * per_device).astype(jnp.int32).reshape(1)
    result = call(
        functools.partial(attend_body, experts, capacity),
        [whole] + [chunk] * experts,
        (chosen, index, base, front_row, norm_gain, front_input[0], queries[0], *kv),
        scratch=[
            pltpu.VMEM((length * tokens, 4 * LANES), bf16),
            pltpu.VMEM((SEL * BLK, 4 * LANES), f32),
            pltpu.VMEM((HEADS // KV_HEADS * BLK, LANES), bf16),
            pltpu.VMEM((tokens, width), f32),
        ],
        flops=pack_flops + 4 * tokens * HEADS * SEL * BLK * LANES,
        smem=3,
        vmem=VMEM_BYTES + 2 * length * tokens * 4 * LANES * 2,
    )
    middle, front_chunks = result[0], result[1:]
    work = 2 * 2 * slots * width * hidden_width
    pair = 2 * slots

    def hidden(rows):
        return call(
            hidden_body, shape_of(pair, hidden_width), (*rows, w_gate, w_up), flops=2 * work
        )

    def backward(rows, grads):
        return call(backward_body, [piece, piece], (*rows, grads, w_gate, w_up), flops=4 * work)

    for k in range(1, experts):
        grad_chunks[k] = turned(after([grad_chunks[k]], [middle])[0], k)
    front_chunks = sent(after(front_chunks, row_chunks + grad_chunks[1:2]))
    back_rows = joined(after(row_chunks, [middle]))
    back_other = swapped(back_rows, 2)
    down_low = swapped(after([w_down[cut:]], [back_rows])[0], 2)
    downs = (w_down, down_top, down_low)
    grad_near = joined(after(grad_chunks, [back_rows, down_top, there_back_middle]))
    there_back_grad = passed_along(after([back_grad[0]], [grad_near])[0], -1)
    ready = [back_other, there_back_grad, down_low]
    front_near = joined(after(front_chunks, ready))
    there_middle = passed_along(after([middle], [front_near])[0], 1)
    grad_near = [grad_near, swapped(after([grad_near], [front_near])[0], 1)]
    down_back, other_back = call(
        down_back_body,
        [shape_of(pair, hidden_width, f32), shape_of(pair, hidden_width)],
        (*grad_near, *downs),
        flops=2 * work,
    )
    far_back = swapped(other_back, 2)
    late = after([back_rows], [front_near])[0]
    back_near = backward((back_rows, swapped(late, 1)), down_back)
    back_core = swapped(back_near[1], 1)
    (far_back,) = after([far_back], [there_middle])
    back_far = backward((back_other, swapped(after([back_other], [front_near])[0], 1)), far_back)
    chip = (back_far[0].astype(f32) + swapped(back_far[1], 1).astype(f32)).astype(bf16)
    front_other = after([swapped(front_near, 2)], [back_near[0], there_middle])[0]

    front_small, back_small = after([front_small, back_small], [front_near])
    there_small = passed_along(front_small, 1)
    there_back_small = passed_along(back_small, -1)
    there_front_from = there_small[0, :tokens].astype(jnp.int32).reshape(tokens, 1)
    there_front_gate = there_small[0, tokens:].reshape(tokens, 1)
    there_back_from = there_back_small[0, :tokens].astype(jnp.int32).reshape(tokens, 1)
    there_gain = there_back_small[:, tokens:]
    front_pieces = [front_near, swapped(front_near, 1), front_other, swapped(front_other, 1)]
    hidden_near = hidden(front_pieces[:2])
    hidden_far = hidden(front_pieces[2:])
    hidden_other = swapped(hidden_far, 2)
    (hidden_other,) = after([hidden_other], [there_small, there_back_small, chip])
    front_own, front_core = call(
        output_body, [piece, piece], (hidden_near, hidden_other, *downs), cheap=True
    )
    (chip,) = after([chip], [hidden_far])
    back_shares = (back_near[0], back_core, swapped(chip, 2))

    front_shares = (front_own, swapped(front_core, 1))
    front_chunks = split(front_shares)
    front_return = sent_back(front_chunks, 1)

    back_chunks = split(after(back_shares, front_chunks))
    back_return = sent_back(back_chunks, -1)

    front_return = after(front_return, back_chunks)
    front_output = call(
        functools.partial(front_finish_body, experts, capacity),
        whole,
        (there_front_from, there_front_gate, there_middle, *front_return),
        flops=pack_flops,
    )
    back_return = after(back_return, [front_output])
    back_output = call(
        functools.partial(back_finish_body, experts, capacity),
        whole,
        (there_back_from, there_gain, there_back_middle, there_back_grad, *back_return),
        flops=pack_flops,
    )
    return (front_output[None], back_output[None])


def solution(mesh):
    placed = (
        P("section", "expert", None),
        P("section", "expert", None),
        P("section", "expert", None),
        P("section", "expert", None, None),
        P("section", "expert", None),
        P("section", "expert", None),
        P("section", "expert", None),
        P("section", "expert", None),
        P("section", "expert", None),
        P("section", "expert", None),
        P("section", None),
        P("section", "expert", None, None),
        P("section", "expert", None, None),
        P("section", "expert", None, None),
    )
    return jax.shard_map(
        shards,
        mesh=mesh,
        in_specs=placed,
        out_specs=(P("section", "expert", None), P("section", "expert", None)),
        check_vma=False,
    )
```

```python
import functools

import jax
import jax.numpy as jnp
from jax import lax
from jax.experimental import pallas as pl
from jax.experimental.pallas import tpu as pltpu
from jax.sharding import PartitionSpec as P

GROUP = 4
HEADS = 32
HEAD_DIM = 112
KV_HEADS = 2
BLK = 64
SEL = 4
PARTS = 4
LANES = 128
VMEM_BYTES = 28 * 1024 * 1024

epsilon = 1e-06
negative_large = -1e30
bf16 = jnp.bfloat16
f32 = jnp.float32


def passed_along(array, by, back=0):
    sections, length = lax.axis_size("section"), lax.axis_size("expert")
    pairs = [
        (s * length + i, (s + by) % sections * length + (i - back * GROUP) % length)
        for s in range(sections)
        for i in range(length)
    ]
    return lax.ppermute(array, ("section", "expert"), pairs)


def swapped(array, bit):
    return lax.ppermute(array, "expert", [(i, i ^ bit) for i in range(lax.axis_size("expert"))])


def turned(array, by):
    length = lax.axis_size("expert")
    return lax.ppermute(
        array, "expert", [(i, (i + by * GROUP) % length) for i in range(length)]
    )


def call(body, outs, args, scratch=(), flops=0, smem=0, vmem=VMEM_BYTES, cheap=False):
    specs = [
        pl.BlockSpec(memory_space=pltpu.SMEM if i < smem else pltpu.VMEM)
        for i in range(len(args))
    ]
    many = isinstance(outs, list)
    shapes = outs if many else [outs]
    moved_bytes = sum(a.size * a.dtype.itemsize for a in list(args) + shapes)
    result = pl.pallas_call(
        body,
        out_shape=shapes,
        in_specs=specs,
        out_specs=[pl.BlockSpec(memory_space=pltpu.VMEM) for _ in shapes],
        scratch_shapes=list(scratch),
        compiler_params=pltpu.CompilerParams(vmem_limit_bytes=vmem),
        cost_estimate=pl.CostEstimate(
            flops=1 if cheap else int(flops),
            bytes_accessed=1 if cheap else int(moved_bytes),
            transcendentals=0,
        ),
    )(*args)
    return list(result) if many else result[0]


def dot(a, b):
    return jnp.dot(a, b, preferred_element_type=f32)


def dot_last(a, b):
    return lax.dot_general(a, b, (((1,), (1,)), ((), ())), preferred_element_type=f32)


def rms_scale(rows):
    return lax.rsqrt(jnp.mean(rows * rows, axis=-1, keepdims=True) + epsilon)


def iota(shape, dim):
    return lax.broadcasted_iota(jnp.int32, shape, dim)


def stacked(rows):
    width = rows.shape[1] // PARTS
    return jnp.concatenate([rows[:, p * width : (p + 1) * width] for p in range(PARTS)], axis=0)


def place_across(route_row, experts, capacity):
    tokens = route_row.shape[1]
    names = iota((max(8, experts), tokens), 0)
    onehot = jnp.where(names == route_row, 1.0, 0.0)
    earlier = jnp.where(iota((tokens, tokens), 0) < iota((tokens, tokens), 1), 1.0, 0.0)
    before = dot(onehot.astype(bf16), earlier.astype(bf16))
    place = onehot * (before + (names * (PARTS * capacity)).astype(f32))
    return jnp.sum(place, axis=0, keepdims=True).astype(jnp.int32)


def place_down(route_column, experts, capacity):
    tokens = route_column.shape[0]
    names = iota((tokens, LANES), 1)
    onehot = jnp.where(names == route_column, 1.0, 0.0)
    earlier = jnp.where(iota((tokens, tokens), 1) < iota((tokens, tokens), 0), 1.0, 0.0)
    before = dot(earlier.astype(bf16), onehot.astype(bf16))
    place = onehot * (before + (names * (PARTS * capacity)).astype(f32))
    return jnp.sum(place, axis=1, keepdims=True).astype(jnp.int32)


def pack_into(rows, place, out_refs, capacity):
    tokens = rows.shape[0]
    height = PARTS * capacity
    total = height * len(out_refs)
    places = jnp.concatenate([place + p * capacity for p in range(PARTS)], axis=1)
    pick = jnp.where(iota((total, PARTS * tokens), 0) == places, 1.0, 0.0).astype(bf16)
    packed = dot(pick, stacked(rows)).astype(bf16)
    for e, ref in enumerate(out_refs):
        ref[...] = packed[e * height : (e + 1) * height]


def back_pack_body(experts, capacity, route_ref, gate_ref, gain_ref, middle_ref, grad_ref, *outs):
    place = place_across(route_ref[...], experts, capacity)
    middle = middle_ref[...].astype(f32)
    normed = (middle * rms_scale(middle) * gain_ref[...]).astype(bf16)
    pack_into(normed, place, outs[:experts], capacity)
    scaled = (gate_ref[...] * grad_ref[...].astype(f32)).astype(bf16)
    pack_into(scaled, place, outs[experts:], capacity)


def join_body(capacity, *refs):
    chunks, out = refs[:-1], refs[-1]
    sources = len(chunks)
    height = PARTS * capacity
    rows = jnp.concatenate([ref[...] for ref in chunks], axis=0)
    slots = sources * capacity
    width = rows.shape[1]
    index = iota((slots, 1), 0)
    source = index * 0
    for s in range(1, sources):
        source = source + jnp.where(index >= s * capacity, 1, 0)
    first = index + source * (height - capacity)
    columns = iota((slots, rows.shape[0]), 1)
    for p in range(PARTS):
        pick = jnp.where(columns == first + p * capacity, 1.0, 0.0).astype(bf16)
        out[:, p * width : (p + 1) * width] = dot(pick, rows).astype(bf16)


def split_body(capacity, count_shares, *refs):
    shares, outs = refs[:count_shares], refs[count_shares:]
    total = shares[0][...].astype(f32)
    for ref in shares[1:]:
        total = total + ref[...].astype(f32)
    rows = stacked(total.astype(bf16))
    height = PARTS * capacity
    slots = shares[0].shape[0]
    count = height * len(outs)
    index = iota((count, 1), 0)
    group = index * 0
    source = index * 0
    for g in range(1, count // capacity):
        group = group + jnp.where(index >= g * capacity, 1, 0)
    for s in range(1, len(outs)):
        source = source + jnp.where(index >= s * height, 1, 0)
    part = group - source * PARTS
    place = part * slots + source * capacity + index - group * capacity
    pick = jnp.where(iota((count, PARTS * slots), 1) == place, 1.0, 0.0).astype(bf16)
    packed = dot(pick, rows).astype(bf16)
    for s, ref in enumerate(outs):
        ref[...] = packed[s * height : (s + 1) * height]


def unpacked(route_column, chunk_refs, experts, capacity):
    tokens = route_column.shape[0]
    place = place_down(route_column, experts, capacity)
    rows = jnp.concatenate([ref[...] for ref in chunk_refs], axis=0)
    columns = iota((tokens, rows.shape[0]), 1)
    parts = []
    for p in range(PARTS):
        pick = jnp.where(columns == place + p * capacity, 1.0, 0.0).astype(bf16)
        parts.append(dot(pick, rows))
    return jnp.concatenate(parts, axis=1)


def front_finish_body(experts, capacity, route_ref, gate_ref, middle_ref, *refs):
    chunks, out = refs[:-1], refs[-1]
    contrib = gate_ref[...] * unpacked(route_ref[...], chunks, experts, capacity)
    out[...] = (middle_ref[...].astype(f32) + contrib).astype(bf16)


def back_finish_body(experts, capacity, route_ref, gain_ref, middle_ref, grad_ref, *refs):
    chunks, out = refs[:-1], refs[-1]
    amount = gain_ref[...] * unpacked(route_ref[...], chunks, experts, capacity)
    middle = middle_ref[...].astype(f32)
    scale = rms_scale(middle)
    cube = scale * scale * scale
    mean = jnp.mean(middle * amount, axis=-1, keepdims=True)
    out[...] = (grad_ref[...].astype(f32) + scale * amount - middle * cube * mean).astype(bf16)


def hidden_body(first_ref, second_ref, gate_ref, up_ref, out_ref):
    rows = jnp.concatenate([first_ref[...], second_ref[...]], axis=0)
    gate_val = dot(rows, gate_ref[...])
    up_val = dot(rows, up_ref[...])
    out_ref[...] = (gate_val / (1.0 + jnp.exp(-gate_val)) * up_val).astype(bf16)


def output_body(own_ref, other_ref, down_ref, top_ref, low_ref, first_out, second_out):
    half = first_out.shape[0]
    hidden = jnp.concatenate([own_ref[...], other_ref[...]], axis=1)
    step = 4 * LANES
    for n in range(0, down_ref.shape[1], step):
        part = slice(n, n + step)
        weight = jnp.concatenate([down_ref[:, part], top_ref[:, part], low_ref[:, part]], axis=0)
        value = dot(hidden, weight).astype(bf16)
        first_out[:, part] = value[:half]
        second_out[:, part] = value[half:]


def down_back_body(first_ref, second_ref, down_ref, top_ref, low_ref, own_out, other_out):
    grads = jnp.concatenate([first_ref[...], second_ref[...]], axis=0)
    own_out[...] = dot_last(grads, down_ref[...]).astype(own_out.dtype)
    far = jnp.concatenate([top_ref[...], low_ref[...]], axis=0)
    other_out[...] = dot_last(grads, far).astype(other_out.dtype)


def backward_body(first_ref, second_ref, back_ref, gate_ref, up_ref, first_out, second_out):
    half = first_ref.shape[0]
    rows = jnp.concatenate([first_ref[...], second_ref[...]], axis=0)
    gate_val = dot(rows, gate_ref[...])
    up_val = dot(rows, up_ref[...])
    down_back = back_ref[...].astype(f32)
    sigmoid_val = 1.0 / (1.0 + jnp.exp(-gate_val))
    slope_val = sigmoid_val * (1.0 + gate_val * (1.0 - sigmoid_val))
    gate_grad = (down_back * up_val * slope_val).astype(bf16)
    up_grad = (down_back * gate_val * sigmoid_val).astype(bf16)
    step = 4 * LANES
    for n in range(0, gate_ref.shape[0], step):
        value = dot_last(gate_grad, gate_ref[n : n + step])
        value = (value + dot_last(up_grad, up_ref[n : n + step])).astype(bf16)
        first_out[:, n : n + step] = value[:half]
        second_out[:, n : n + step] = value[half:]


def attend_body(
    experts,
    capacity,
    chosen_ref,
    index_ref,
    base_ref,
    route_ref,
    gain_ref,
    input_ref,
    query_ref,
    kv0,
    kv1,
    kv2,
    kv3,
    middle_ref,
    *refs,
):
    outs, (kv_all, kv_now, stack, attended) = refs[:experts], refs[experts:]
    tokens, width = query_ref.shape
    lead = 0
    for ref in (kv0, kv1, kv2, kv3):
        kv_all[lead : lead + ref.shape[0], : ref.shape[1]] = ref[...]
        lead += ref.shape[0]
    attended[...] = jnp.zeros_like(attended)
    heads_each = HEADS // KV_HEADS
    period = 8
    window = 2 * LANES
    keys = SEL * BLK
    lane = iota((keys, LANES), 1)
    batch = 4
    scale = HEAD_DIM**-0.5

    def one_block(block, _):
        top = pl.multiple_of(block * BLK, BLK)
        position = (base_ref[0] + block) * BLK + (iota((batch * BLK, keys), 0) & (BLK - 1))
        for head in range(KV_HEADS):
            key_pos = iota((1, keys), 1)
            shift = key_pos * 0
            for s in range(SEL):
                at = (block * KV_HEADS + head) * SEL + s
                start = pl.multiple_of(index_ref[at] * BLK, BLK)
                kv_now[s * BLK : (s + 1) * BLK, :] = kv_all[pl.ds(start, BLK), :].astype(f32)
                inside = (key_pos >= s * BLK) & (key_pos < (s + 1) * BLK)
                shift = jnp.where(inside, (chosen_ref[at] - s) * BLK, shift)
            allowed = key_pos + shift <= position
            sides = []
            for side in range(2):
                lead = (side * KV_HEADS + head) * HEAD_DIM
                tile = min(lead // LANES, 2)
                piece = kv_now[:, tile * LANES : tile * LANES + window]
                offset = lead - tile * LANES
                if offset:
                    piece = pltpu.roll(piece, window - offset, 1)
                sides.append(jnp.where(lane < HEAD_DIM, piece[:, :LANES], 0.0).astype(bf16))
            key_rows, value_rows = sides
            spots = []
            for j in range(heads_each):
                c = j % period
                tile = min(c * HEAD_DIM // LANES, period - 3)
                offset = c * HEAD_DIM - tile * LANES
                tile = tile + (j // period) * (period - 1) + head * heads_each * HEAD_DIM // LANES
                spots.append((tile * LANES, offset))
            for j, (lead, offset) in enumerate(spots):
                piece = query_ref[pl.ds(top, BLK), lead : lead + window].astype(f32)
                if offset:
                    piece = pltpu.roll(piece, window - offset, 1)
                stack[j * BLK : (j + 1) * BLK, :] = piece[:, :LANES].astype(bf16)
            for b in range(0, heads_each, batch):
                scores = dot_last(stack[b * BLK : (b + batch) * BLK, :], key_rows) * scale
                scores = jnp.where(allowed, scores, negative_large)
                exp_scores = jnp.exp(scores - jnp.max(scores, axis=-1, keepdims=True))
                total = jnp.sum(exp_scores, axis=-1, keepdims=True)
                mixed = dot((exp_scores / total).astype(bf16), value_rows)
                for i in range(batch):
                    lead, offset = spots[b + i]
                    piece = mixed[i * BLK : (i + 1) * BLK]
                    piece = jnp.concatenate([piece, jnp.zeros_like(piece)], axis=1)
                    if offset:
                        piece = pltpu.roll(piece, offset, 1)
                    spot = (pl.ds(top, BLK), slice(lead, lead + window))
                    attended[spot] = attended[spot] + piece
        return 0

    lax.fori_loop(0, tokens // BLK, one_block, 0)
    middle = (input_ref[...].astype(f32) + attended[...]).astype(bf16)
    middle_ref[...] = middle
    middle = middle.astype(f32)
    normed = (middle * rms_scale(middle) * gain_ref[...]).astype(bf16)
    pack_into(normed, place_across(route_ref[...], experts, capacity), outs, capacity)


def after(arrays, others):
    count = len(arrays)
    return list(lax.optimization_barrier(tuple(arrays) + tuple(others))[:count])


def shape_of(rows, columns, kind=bf16):
    return jax.ShapeDtypeStruct((rows, columns), kind)


def shards(
    front_input,
    queries,
    keys_values,
    selected_blocks,
    front_route,
    front_gate,
    back_middle,
    back_grad,
    back_route,
    back_gate,
    norm_gain,
    gate_slice,
    up_slice,
    down_slice,
):
    tokens, width = front_input.shape[1:]
    length = lax.axis_size("expert")
    experts = length // GROUP
    average = tokens // experts
    capacity = average + max(1, average // 8)
    slots = experts * capacity
    hidden_width = gate_slice.shape[3]
    w_gate, w_up, w_down = gate_slice[0, 0], up_slice[0, 0], down_slice[0, 0]
    me = lax.axis_index("expert")
    group = me // GROUP
    chunk = shape_of(PARTS * capacity, width // PARTS)
    piece = shape_of(slots, width)
    whole = shape_of(tokens, width)

    column = [keys_values[0]]
    for back in range(1, experts):
        pairs = [(i, i + back * GROUP) for i in range(length - back * GROUP)]
        column.append(lax.ppermute(keys_values[0], "expert", pairs))
    front_from = lax.rem(front_route[0] - group + experts, experts)
    back_from = lax.rem(back_route[0] - group + experts, experts)
    front_row, back_row = front_from.reshape(1, tokens), back_from.reshape(1, tokens)

    pack_flops = 4 * slots * PARTS * tokens * width
    packed = call(
        functools.partial(back_pack_body, experts, capacity),
        [chunk] * (2 * experts),
        (back_row, back_gate[0], norm_gain, back_middle[0], back_grad[0]),
        flops=2 * pack_flops,
    )
    column = after(column, [packed[0]])
    column = jnp.concatenate(column, axis=0)
    other_chip = swapped(column, 2)
    packed = after(packed, [column])

    front_small = jnp.concatenate([front_from.astype(f32), front_gate[0]], axis=0).reshape(1, -1)
    back_small = jnp.concatenate([back_from.astype(f32).reshape(1, -1), norm_gain], axis=1)

    def sent(chunks):
        return [chunks[0]] + [turned(chunks[k], k) for k in range(1, experts)]

    def joined(chunks):
        return call(functools.partial(join_body, capacity), piece, chunks, flops=pack_flops)

    def pieces_of(rows):
        other = swapped(rows, 2)
        return [rows, swapped(rows, 1), other, swapped(other, 1)]

    def split(parts):
        return call(
            functools.partial(split_body, capacity, len(parts)),
            [chunk] * experts,
            parts,
            cheap=True,
        )

    def sent_back(chunks, by):
        return [passed_along(chunks[k], by, k) for k in range(experts)]

    row_chunks, grad_chunks = packed[:experts], packed[experts:]
    first = 1 + 2 * (experts - 1) // 3
    for k in range(1, first):
        row_chunks[k] = turned(row_chunks[k], k)
    arrived = row_chunks[1:first]
    cut = hidden_width * 5 // 8
    (down_top,) = after([w_down[:cut]], arrived[:1])
    down_top = swapped(down_top, 2)
    there_back_middle = passed_along(after([back_middle[0]], arrived)[0], -1)
    far = swapped(after([other_chip], arrived)[0], 1)
    kv = [column, other_chip, swapped(column, 1), far]
    for k in range(first, experts):
        row_chunks[k] = turned(after([row_chunks[k]], arrived)[0], k)
    grad_chunks[1] = turned(after([grad_chunks[1]], arrived)[0], 1)

    per_device = tokens // BLK
    chosen = selected_blocks[0].reshape(-1)
    owner = chosen // per_device
    place = (owner % GROUP) ^ (me % GROUP)
    place = (place % 2) * 2 + place // 2
    index = (place * experts + group - owner // GROUP) * per_device + chosen % per_device
    index = jnp.clip(index, 0, length * per_device - 1)
    base = (me * per_device).astype(jnp.int32).reshape(1)
    result = call(
        functools.partial(attend_body, experts, capacity),
        [whole] + [chunk] * experts,
        (chosen, index, base, front_row, norm_gain, front_input[0], queries[0], *kv),
        scratch=[
            pltpu.VMEM((length * tokens, 4 * LANES), bf16),
            pltpu.VMEM((SEL * BLK, 4 * LANES), f32),
            pltpu.VMEM((HEADS // KV_HEADS * BLK, LANES), bf16),
            pltpu.VMEM((tokens, width), f32),
        ],
        flops=pack_flops + 4 * tokens * HEADS * SEL * BLK * LANES,
        smem=3,
        vmem=VMEM_BYTES + 2 * length * tokens * 4 * LANES * 2,
    )
    middle, front_chunks = result[0], result[1:]
    work = 2 * 2 * slots * width * hidden_width
    pair = 2 * slots

    def hidden(rows):
        return call(
            hidden_body, shape_of(pair, hidden_width), (*rows, w_gate, w_up), flops=2 * work
        )

    def backward(rows, grads):
        return call(backward_body, [piece, piece], (*rows, grads, w_gate, w_up), flops=4 * work)

    for k in range(2, experts):
        grad_chunks[k] = turned(after([grad_chunks[k]], [middle])[0], k)
    front_chunks = sent(after(front_chunks, row_chunks + grad_chunks[1:2]))
    back_rows = joined(after(row_chunks, [middle, grad_chunks[1]]))
    back_other = swapped(back_rows, 2)
    down_low = swapped(after([w_down[cut:]], [back_rows])[0], 2)
    downs = (w_down, down_top, down_low)
    grad_near = joined(after(grad_chunks, [back_rows, down_top, there_back_middle]))
    there_back_grad = passed_along(after([back_grad[0]], [grad_near])[0], -1)
    ready = [back_other, there_back_grad, down_low]
    front_near = joined(after(front_chunks, ready))
    there_middle = passed_along(after([middle], [front_near])[0], 1)
    grad_near = [grad_near, swapped(after([grad_near], [front_near])[0], 1)]
    down_back, other_back = call(
        down_back_body,
        [shape_of(pair, hidden_width, f32), shape_of(pair, hidden_width)],
        (*grad_near, *downs),
        flops=2 * work,
    )
    far_back = swapped(other_back, 2)
    late = after([back_rows], [front_near])[0]
    back_near = backward((back_rows, swapped(late, 1)), down_back)
    back_core = swapped(back_near[1], 1)
    (far_back,) = after([far_back], [there_middle])
    back_far = backward((back_other, swapped(after([back_other], [front_near])[0], 1)), far_back)
    chip = (back_far[0].astype(f32) + swapped(back_far[1], 1).astype(f32)).astype(bf16)
    front_other = after([swapped(front_near, 2)], [back_near[0], there_middle])[0]

    front_small, back_small = after([front_small, back_small], [front_near])
    there_small = passed_along(front_small, 1)
    there_back_small = passed_along(back_small, -1)
    there_front_from = there_small[0, :tokens].astype(jnp.int32).reshape(tokens, 1)
    there_front_gate = there_small[0, tokens:].reshape(tokens, 1)
    there_back_from = there_back_small[0, :tokens].astype(jnp.int32).reshape(tokens, 1)
    there_gain = there_back_small[:, tokens:]
    front_pieces = [front_near, swapped(front_near, 1), front_other, swapped(front_other, 1)]
    hidden_near = hidden(front_pieces[:2])
    hidden_far = hidden(front_pieces[2:])
    hidden_other = swapped(hidden_far, 2)
    (hidden_other,) = after([hidden_other], [there_small, there_back_small, chip])
    front_own, front_core = call(
        output_body, [piece, piece], (hidden_near, hidden_other, *downs), cheap=True
    )
    (chip,) = after([chip], [hidden_far])
    back_shares = (back_near[0], back_core, swapped(chip, 2))

    front_shares = (front_own, swapped(front_core, 1))
    front_chunks = split(front_shares)
    front_return = sent_back(front_chunks, 1)

    back_chunks = split(after(back_shares, front_chunks))
    back_return = sent_back(back_chunks, -1)

    front_return = after(front_return, back_chunks)
    front_output = call(
        functools.partial(front_finish_body, experts, capacity),
        whole,
        (there_front_from, there_front_gate, there_middle, *front_return),
        flops=pack_flops,
    )
    back_return = after(back_return, [front_output])
    back_output = call(
        functools.partial(back_finish_body, experts, capacity),
        whole,
        (there_back_from, there_gain, there_back_middle, there_back_grad, *back_return),
        flops=pack_flops,
    )
    return (front_output[None], back_output[None])


def solution(mesh):
    placed = (
        P("section", "expert", None),
        P("section", "expert", None),
        P("section", "expert", None),
        P("section", "expert", None, None),
        P("section", "expert", None),
        P("section", "expert", None),
        P("section", "expert", None),
        P("section", "expert", None),
        P("section", "expert", None),
        P("section", "expert", None),
        P("section", None),
        P("section", "expert", None, None),
        P("section", "expert", None, None),
        P("section", "expert", None, None),
    )
    return jax.shard_map(
        shards,
        mesh=mesh,
        in_specs=placed,
        out_specs=(P("section", "expert", None), P("section", "expert", None)),
        check_vma=False,
    )
```

```python
import functools

import jax
import jax.numpy as jnp
from jax import lax
from jax.experimental import pallas as pl
from jax.experimental.pallas import tpu as pltpu
from jax.sharding import PartitionSpec as P

GROUP = 4
HEADS = 32
HEAD_DIM = 112
KV_HEADS = 2
BLK = 64
SEL = 4
PARTS = 4
LANES = 128
VMEM_BYTES = 28 * 1024 * 1024

epsilon = 1e-06
negative_large = -1e30
bf16 = jnp.bfloat16
f32 = jnp.float32


def passed_along(array, by, back=0):
    sections, length = lax.axis_size("section"), lax.axis_size("expert")
    pairs = [
        (s * length + i, (s + by) % sections * length + (i - back * GROUP) % length)
        for s in range(sections)
        for i in range(length)
    ]
    return lax.ppermute(array, ("section", "expert"), pairs)


def swapped(array, bit):
    return lax.ppermute(array, "expert", [(i, i ^ bit) for i in range(lax.axis_size("expert"))])


def turned(array, by):
    length = lax.axis_size("expert")
    return lax.ppermute(
        array, "expert", [(i, (i + by * GROUP) % length) for i in range(length)]
    )


def call(body, outs, args, scratch=(), flops=0, smem=0, vmem=VMEM_BYTES, cheap=False):
    specs = [
        pl.BlockSpec(memory_space=pltpu.SMEM if i < smem else pltpu.VMEM)
        for i in range(len(args))
    ]
    many = isinstance(outs, list)
    shapes = outs if many else [outs]
    moved_bytes = sum(a.size * a.dtype.itemsize for a in list(args) + shapes)
    result = pl.pallas_call(
        body,
        out_shape=shapes,
        in_specs=specs,
        out_specs=[pl.BlockSpec(memory_space=pltpu.VMEM) for _ in shapes],
        scratch_shapes=list(scratch),
        compiler_params=pltpu.CompilerParams(vmem_limit_bytes=vmem),
        cost_estimate=pl.CostEstimate(
            flops=1 if cheap else int(flops),
            bytes_accessed=1 if cheap else int(moved_bytes),
            transcendentals=0,
        ),
    )(*args)
    return list(result) if many else result[0]


def dot(a, b):
    return jnp.dot(a, b, preferred_element_type=f32)


def dot_last(a, b):
    return lax.dot_general(a, b, (((1,), (1,)), ((), ())), preferred_element_type=f32)


def rms_scale(rows):
    return lax.rsqrt(jnp.mean(rows * rows, axis=-1, keepdims=True) + epsilon)


def iota(shape, dim):
    return lax.broadcasted_iota(jnp.int32, shape, dim)


def stacked(rows):
    width = rows.shape[1] // PARTS
    return jnp.concatenate([rows[:, p * width : (p + 1) * width] for p in range(PARTS)], axis=0)


def place_across(route_row, experts, capacity):
    tokens = route_row.shape[1]
    names = iota((max(8, experts), tokens), 0)
    onehot = jnp.where(names == route_row, 1.0, 0.0)
    earlier = jnp.where(iota((tokens, tokens), 0) < iota((tokens, tokens), 1), 1.0, 0.0)
    before = dot(onehot.astype(bf16), earlier.astype(bf16))
    place = onehot * (before + (names * (PARTS * capacity)).astype(f32))
    return jnp.sum(place, axis=0, keepdims=True).astype(jnp.int32)


def place_down(route_column, experts, capacity):
    tokens = route_column.shape[0]
    names = iota((tokens, LANES), 1)
    onehot = jnp.where(names == route_column, 1.0, 0.0)
    earlier = jnp.where(iota((tokens, tokens), 1) < iota((tokens, tokens), 0), 1.0, 0.0)
    before = dot(earlier.astype(bf16), onehot.astype(bf16))
    place = onehot * (before + (names * (PARTS * capacity)).astype(f32))
    return jnp.sum(place, axis=1, keepdims=True).astype(jnp.int32)


def pack_into(rows, place, out_refs, capacity):
    tokens = rows.shape[0]
    height = PARTS * capacity
    total = height * len(out_refs)
    places = jnp.concatenate([place + p * capacity for p in range(PARTS)], axis=1)
    pick = jnp.where(iota((total, PARTS * tokens), 0) == places, 1.0, 0.0).astype(bf16)
    packed = dot(pick, stacked(rows)).astype(bf16)
    for e, ref in enumerate(out_refs):
        ref[...] = packed[e * height : (e + 1) * height]


def back_pack_body(experts, capacity, route_ref, gate_ref, gain_ref, middle_ref, grad_ref, *outs):
    place = place_across(route_ref[...], experts, capacity)
    middle = middle_ref[...].astype(f32)
    normed = (middle * rms_scale(middle) * gain_ref[...]).astype(bf16)
    pack_into(normed, place, outs[:experts], capacity)
    scaled = (gate_ref[...] * grad_ref[...].astype(f32)).astype(bf16)
    pack_into(scaled, place, outs[experts:], capacity)


def join_body(capacity, *refs):
    chunks, out = refs[:-1], refs[-1]
    sources = len(chunks)
    height = PARTS * capacity
    rows = jnp.concatenate([ref[...] for ref in chunks], axis=0)
    slots = sources * capacity
    width = rows.shape[1]
    index = iota((slots, 1), 0)
    source = index * 0
    for s in range(1, sources):
        source = source + jnp.where(index >= s * capacity, 1, 0)
    first = index + source * (height - capacity)
    columns = iota((slots, rows.shape[0]), 1)
    for p in range(PARTS):
        pick = jnp.where(columns == first + p * capacity, 1.0, 0.0).astype(bf16)
        out[:, p * width : (p + 1) * width] = dot(pick, rows).astype(bf16)


def split_body(capacity, count_shares, *refs):
    shares, outs = refs[:count_shares], refs[count_shares:]
    total = shares[0][...].astype(f32)
    for ref in shares[1:]:
        total = total + ref[...].astype(f32)
    rows = stacked(total.astype(bf16))
    height = PARTS * capacity
    slots = shares[0].shape[0]
    count = height * len(outs)
    index = iota((count, 1), 0)
    group = index * 0
    source = index * 0
    for g in range(1, count // capacity):
        group = group + jnp.where(index >= g * capacity, 1, 0)
    for s in range(1, len(outs)):
        source = source + jnp.where(index >= s * height, 1, 0)
    part = group - source * PARTS
    place = part * slots + source * capacity + index - group * capacity
    pick = jnp.where(iota((count, PARTS * slots), 1) == place, 1.0, 0.0).astype(bf16)
    packed = dot(pick, rows).astype(bf16)
    for s, ref in enumerate(outs):
        ref[...] = packed[s * height : (s + 1) * height]


def unpacked(route_column, chunk_refs, experts, capacity):
    tokens = route_column.shape[0]
    place = place_down(route_column, experts, capacity)
    rows = jnp.concatenate([ref[...] for ref in chunk_refs], axis=0)
    columns = iota((tokens, rows.shape[0]), 1)
    parts = []
    for p in range(PARTS):
        pick = jnp.where(columns == place + p * capacity, 1.0, 0.0).astype(bf16)
        parts.append(dot(pick, rows))
    return jnp.concatenate(parts, axis=1)


def front_finish_body(experts, capacity, route_ref, gate_ref, middle_ref, *refs):
    chunks, out = refs[:-1], refs[-1]
    contrib = gate_ref[...] * unpacked(route_ref[...], chunks, experts, capacity)
    out[...] = (middle_ref[...].astype(f32) + contrib).astype(bf16)


def back_finish_body(experts, capacity, route_ref, gain_ref, middle_ref, grad_ref, *refs):
    chunks, out = refs[:-1], refs[-1]
    amount = gain_ref[...] * unpacked(route_ref[...], chunks, experts, capacity)
    middle = middle_ref[...].astype(f32)
    scale = rms_scale(middle)
    cube = scale * scale * scale
    mean = jnp.mean(middle * amount, axis=-1, keepdims=True)
    out[...] = (grad_ref[...].astype(f32) + scale * amount - middle * cube * mean).astype(bf16)


def hidden_body(first_ref, second_ref, gate_ref, up_ref, out_ref):
    rows = jnp.concatenate([first_ref[...], second_ref[...]], axis=0)
    gate_val = dot(rows, gate_ref[...])
    up_val = dot(rows, up_ref[...])
    out_ref[...] = (gate_val / (1.0 + jnp.exp(-gate_val)) * up_val).astype(bf16)


def output_body(own_ref, other_ref, down_ref, top_ref, low_ref, first_out, second_out):
    half = first_out.shape[0]
    hidden = jnp.concatenate([own_ref[...], other_ref[...]], axis=1)
    step = 4 * LANES
    for n in range(0, down_ref.shape[1], step):
        part = slice(n, n + step)
        weight = jnp.concatenate([down_ref[:, part], top_ref[:, part], low_ref[:, part]], axis=0)
        value = dot(hidden, weight).astype(bf16)
        first_out[:, part] = value[:half]
        second_out[:, part] = value[half:]


def down_back_body(first_ref, second_ref, down_ref, top_ref, low_ref, own_out, other_out):
    grads = jnp.concatenate([first_ref[...], second_ref[...]], axis=0)
    own_out[...] = dot_last(grads, down_ref[...]).astype(own_out.dtype)
    far = jnp.concatenate([top_ref[...], low_ref[...]], axis=0)
    other_out[...] = dot_last(grads, far).astype(other_out.dtype)


def backward_body(first_ref, second_ref, back_ref, gate_ref, up_ref, first_out, second_out):
    half = first_ref.shape[0]
    rows = jnp.concatenate([first_ref[...], second_ref[...]], axis=0)
    gate_val = dot(rows, gate_ref[...])
    up_val = dot(rows, up_ref[...])
    down_back = back_ref[...].astype(f32)
    sigmoid_val = 1.0 / (1.0 + jnp.exp(-gate_val))
    slope_val = sigmoid_val * (1.0 + gate_val * (1.0 - sigmoid_val))
    gate_grad = (down_back * up_val * slope_val).astype(bf16)
    up_grad = (down_back * gate_val * sigmoid_val).astype(bf16)
    step = 4 * LANES
    for n in range(0, gate_ref.shape[0], step):
        value = dot_last(gate_grad, gate_ref[n : n + step])
        value = (value + dot_last(up_grad, up_ref[n : n + step])).astype(bf16)
        first_out[:, n : n + step] = value[:half]
        second_out[:, n : n + step] = value[half:]


def attend_body(
    experts,
    capacity,
    chosen_ref,
    index_ref,
    base_ref,
    route_ref,
    gain_ref,
    input_ref,
    query_ref,
    kv0,
    kv1,
    kv2,
    kv3,
    middle_ref,
    *refs,
):
    outs, (kv_all, kv_now, stack, attended) = refs[:experts], refs[experts:]
    tokens, width = query_ref.shape
    lead = 0
    for ref in (kv0, kv1, kv2, kv3):
        kv_all[lead : lead + ref.shape[0], : ref.shape[1]] = ref[...]
        lead += ref.shape[0]
    attended[...] = jnp.zeros_like(attended)
    heads_each = HEADS // KV_HEADS
    period = 8
    window = 2 * LANES
    keys = SEL * BLK
    lane = iota((keys, LANES), 1)
    batch = 4
    scale = HEAD_DIM**-0.5

    def one_block(block, _):
        top = pl.multiple_of(block * BLK, BLK)
        position = (base_ref[0] + block) * BLK + (iota((batch * BLK, keys), 0) & (BLK - 1))
        for head in range(KV_HEADS):
            key_pos = iota((1, keys), 1)
            shift = key_pos * 0
            for s in range(SEL):
                at = (block * KV_HEADS + head) * SEL + s
                start = pl.multiple_of(index_ref[at] * BLK, BLK)
                kv_now[s * BLK : (s + 1) * BLK, :] = kv_all[pl.ds(start, BLK), :].astype(f32)
                inside = (key_pos >= s * BLK) & (key_pos < (s + 1) * BLK)
                shift = jnp.where(inside, (chosen_ref[at] - s) * BLK, shift)
            allowed = key_pos + shift <= position
            sides = []
            for side in range(2):
                lead = (side * KV_HEADS + head) * HEAD_DIM
                tile = min(lead // LANES, 2)
                piece = kv_now[:, tile * LANES : tile * LANES + window]
                offset = lead - tile * LANES
                if offset:
                    piece = pltpu.roll(piece, window - offset, 1)
                sides.append(jnp.where(lane < HEAD_DIM, piece[:, :LANES], 0.0).astype(bf16))
            key_rows, value_rows = sides
            spots = []
            for j in range(heads_each):
                c = j % period
                tile = min(c * HEAD_DIM // LANES, period - 3)
                offset = c * HEAD_DIM - tile * LANES
                tile = tile + (j // period) * (period - 1) + head * heads_each * HEAD_DIM // LANES
                spots.append((tile * LANES, offset))
            for j, (lead, offset) in enumerate(spots):
                piece = query_ref[pl.ds(top, BLK), lead : lead + window].astype(f32)
                if offset:
                    piece = pltpu.roll(piece, window - offset, 1)
                stack[j * BLK : (j + 1) * BLK, :] = piece[:, :LANES].astype(bf16)
            for b in range(0, heads_each, batch):
                scores = dot_last(stack[b * BLK : (b + batch) * BLK, :], key_rows) * scale
                scores = jnp.where(allowed, scores, negative_large)
                exp_scores = jnp.exp(scores - jnp.max(scores, axis=-1, keepdims=True))
                total = jnp.sum(exp_scores, axis=-1, keepdims=True)
                mixed = dot((exp_scores / total).astype(bf16), value_rows)
                for i in range(batch):
                    lead, offset = spots[b + i]
                    piece = mixed[i * BLK : (i + 1) * BLK]
                    piece = jnp.concatenate([piece, jnp.zeros_like(piece)], axis=1)
                    if offset:
                        piece = pltpu.roll(piece, offset, 1)
                    spot = (pl.ds(top, BLK), slice(lead, lead + window))
                    attended[spot] = attended[spot] + piece
        return 0

    lax.fori_loop(0, tokens // BLK, one_block, 0)
    middle = (input_ref[...].astype(f32) + attended[...]).astype(bf16)
    middle_ref[...] = middle
    middle = middle.astype(f32)
    normed = (middle * rms_scale(middle) * gain_ref[...]).astype(bf16)
    pack_into(normed, place_across(route_ref[...], experts, capacity), outs, capacity)


def after(arrays, others):
    count = len(arrays)
    return list(lax.optimization_barrier(tuple(arrays) + tuple(others))[:count])


def shape_of(rows, columns, kind=bf16):
    return jax.ShapeDtypeStruct((rows, columns), kind)


def shards(
    front_input,
    queries,
    keys_values,
    selected_blocks,
    front_route,
    front_gate,
    back_middle,
    back_grad,
    back_route,
    back_gate,
    norm_gain,
    gate_slice,
    up_slice,
    down_slice,
):
    tokens, width = front_input.shape[1:]
    length = lax.axis_size("expert")
    experts = length // GROUP
    average = tokens // experts
    capacity = average + max(1, average // 8)
    slots = experts * capacity
    hidden_width = gate_slice.shape[3]
    w_gate, w_up, w_down = gate_slice[0, 0], up_slice[0, 0], down_slice[0, 0]
    me = lax.axis_index("expert")
    group = me // GROUP
    chunk = shape_of(PARTS * capacity, width // PARTS)
    piece = shape_of(slots, width)
    whole = shape_of(tokens, width)

    column = [keys_values[0]]
    for back in range(1, experts):
        pairs = [(i, i + back * GROUP) for i in range(length - back * GROUP)]
        column.append(lax.ppermute(keys_values[0], "expert", pairs))
    front_from = lax.rem(front_route[0] - group + experts, experts)
    back_from = lax.rem(back_route[0] - group + experts, experts)
    front_row, back_row = front_from.reshape(1, tokens), back_from.reshape(1, tokens)

    pack_flops = 4 * slots * PARTS * tokens * width
    packed = call(
        functools.partial(back_pack_body, experts, capacity),
        [chunk] * (2 * experts),
        (back_row, back_gate[0], norm_gain, back_middle[0], back_grad[0]),
        flops=2 * pack_flops,
    )
    column = after(column, [packed[0]])
    column = jnp.concatenate(column, axis=0)
    other_chip = swapped(column, 2)
    packed = after(packed, [column])

    front_small = jnp.concatenate([front_from.astype(f32), front_gate[0]], axis=0).reshape(1, -1)
    back_small = jnp.concatenate([back_from.astype(f32).reshape(1, -1), norm_gain], axis=1)

    def sent(chunks):
        return [chunks[0]] + [turned(chunks[k], k) for k in range(1, experts)]

    def joined(chunks):
        return call(functools.partial(join_body, capacity), piece, chunks, flops=pack_flops)

    def pieces_of(rows):
        other = swapped(rows, 2)
        return [rows, swapped(rows, 1), other, swapped(other, 1)]

    def split(parts):
        return call(
            functools.partial(split_body, capacity, len(parts)),
            [chunk] * experts,
            parts,
            cheap=True,
        )

    def sent_back(chunks, by):
        return [passed_along(chunks[k], by, k) for k in range(experts)]

    row_chunks, grad_chunks = packed[:experts], packed[experts:]
    first = 1 + 2 * (experts - 1) // 3
    for k in range(1, first):
        row_chunks[k] = turned(row_chunks[k], k)
    arrived = row_chunks[1:first]
    cut = hidden_width * 5 // 8
    (down_top,) = after([w_down[:cut]], arrived[:1])
    down_top = swapped(down_top, 2)
    there_back_middle = passed_along(after([back_middle[0]], arrived)[0], -1)
    far = swapped(after([other_chip], arrived)[0], 1)
    kv = [column, other_chip, swapped(column, 1), far]
    for k in range(first, experts):
        row_chunks[k] = turned(after([row_chunks[k]], arrived)[0], k)
    grad_chunks[1] = turned(after([grad_chunks[1]], arrived)[0], 1)

    per_device = tokens // BLK
    chosen = selected_blocks[0].reshape(-1)
    owner = chosen // per_device
    place = (owner % GROUP) ^ (me % GROUP)
    place = (place % 2) * 2 + place // 2
    index = (place * experts + group - owner // GROUP) * per_device + chosen % per_device
    index = jnp.clip(index, 0, length * per_device - 1)
    base = (me * per_device).astype(jnp.int32).reshape(1)
    result = call(
        functools.partial(attend_body, experts, capacity),
        [whole] + [chunk] * experts,
        (chosen, index, base, front_row, norm_gain, front_input[0], queries[0], *kv),
        scratch=[
            pltpu.VMEM((length * tokens, 4 * LANES), bf16),
            pltpu.VMEM((SEL * BLK, 4 * LANES), f32),
            pltpu.VMEM((HEADS // KV_HEADS * BLK, LANES), bf16),
            pltpu.VMEM((tokens, width), f32),
        ],
        flops=pack_flops + 4 * tokens * HEADS * SEL * BLK * LANES,
        smem=3,
        vmem=VMEM_BYTES + 2 * length * tokens * 4 * LANES * 2,
    )
    middle, front_chunks = result[0], result[1:]
    work = 2 * 2 * slots * width * hidden_width
    pair = 2 * slots

    def hidden(rows):
        return call(
            hidden_body, shape_of(pair, hidden_width), (*rows, w_gate, w_up), flops=2 * work
        )

    def backward(rows, grads):
        return call(backward_body, [piece, piece], (*rows, grads, w_gate, w_up), flops=4 * work)

    for k in range(2, experts):
        grad_chunks[k] = turned(after([grad_chunks[k]], [middle])[0], k)
    front_chunks = sent(after(front_chunks, row_chunks + grad_chunks[1:2]))
    back_rows = joined(after(row_chunks, [middle, grad_chunks[1]]))
    back_other = swapped(back_rows, 2)
    grad_near = joined(after(grad_chunks, [back_rows, down_top, there_back_middle]))
    there_back_grad = passed_along(after([back_grad[0]], [grad_near])[0], -1)
    ready = [back_other, there_back_grad]
    front_near = joined(after(front_chunks, ready))
    there_middle = passed_along(after([middle], [front_near])[0], 1)
    down_low = swapped(after([w_down[cut:]], [front_near])[0], 2)
    downs = (w_down, down_top, down_low)
    grad_near = [grad_near, swapped(after([grad_near], [front_near])[0], 1)]
    front_other = after([swapped(front_near, 2)], [there_middle])[0]

    front_small, back_small = after([front_small, back_small], [front_near])
    there_small = passed_along(front_small, 1)
    there_back_small = passed_along(back_small, -1)
    there_front_from = there_small[0, :tokens].astype(jnp.int32).reshape(tokens, 1)
    there_front_gate = there_small[0, tokens:].reshape(tokens, 1)
    there_back_from = there_back_small[0, :tokens].astype(jnp.int32).reshape(tokens, 1)
    there_gain = there_back_small[:, tokens:]
    front_pieces = [front_near, swapped(front_near, 1), front_other, swapped(front_other, 1)]
    hidden_near = hidden(front_pieces[:2])
    hidden_far = hidden(front_pieces[2:])
    hidden_other = swapped(hidden_far, 2)
    down_back, other_back = call(
        down_back_body,
        [shape_of(pair, hidden_width, f32), shape_of(pair, hidden_width)],
        (*after(grad_near, [hidden_other, hidden_near]), *downs),
        flops=2 * work,
    )
    far_back = swapped(other_back, 2)
    late = after([back_rows], [front_near])[0]
    back_near = backward((back_rows, swapped(late, 1)), down_back)
    back_core = swapped(back_near[1], 1)
    (far_back,) = after([far_back], [there_middle])
    back_far = backward((back_other, swapped(after([back_other], [front_near])[0], 1)), far_back)
    chip = (back_far[0].astype(f32) + swapped(back_far[1], 1).astype(f32)).astype(bf16)
    (hidden_other,) = after([hidden_other], [there_small, there_back_small])
    front_own, front_core = call(
        output_body, [piece, piece], (hidden_near, hidden_other, *downs), cheap=True
    )
    (chip,) = after([chip], [hidden_far])
    back_shares = (back_near[0], back_core, swapped(chip, 2))

    front_shares = (front_own, swapped(front_core, 1))
    front_chunks = split(front_shares)
    front_return = sent_back(front_chunks, 1)

    back_chunks = split(after(back_shares, front_chunks))
    back_return = sent_back(back_chunks, -1)

    front_return = after(front_return, back_chunks)
    front_output = call(
        functools.partial(front_finish_body, experts, capacity),
        whole,
        (there_front_from, there_front_gate, there_middle, *front_return),
        flops=pack_flops,
    )
    back_return = after(back_return, [front_output])
    back_output = call(
        functools.partial(back_finish_body, experts, capacity),
        whole,
        (there_back_from, there_gain, there_back_middle, there_back_grad, *back_return),
        flops=pack_flops,
    )
    return (front_output[None], back_output[None])


def solution(mesh):
    placed = (
        P("section", "expert", None),
        P("section", "expert", None),
        P("section", "expert", None),
        P("section", "expert", None, None),
        P("section", "expert", None),
        P("section", "expert", None),
        P("section", "expert", None),
        P("section", "expert", None),
        P("section", "expert", None),
        P("section", "expert", None),
        P("section", None),
        P("section", "expert", None, None),
        P("section", "expert", None, None),
        P("section", "expert", None, None),
    )
    return jax.shard_map(
        shards,
        mesh=mesh,
        in_specs=placed,
        out_specs=(P("section", "expert", None), P("section", "expert", None)),
        check_vma=False,
    )
```
